256 devices in a mesh: section: 2 (over core), tensor: 4 (over z_lo), dp: 32 (over z_hi, y, x).
Axes of the slice: x: 4, y: 4, z: 8 (z_hi: 2, z_lo: 4; z = z_hi * 4 + z_lo), core: 2. Of those that a mesh axis runs over, the one named last changes fastest.
Arguments:
- weights: bfloat16 [2, 4096, 4096], P('section', 'tensor'), may hold values from -0.09375 to 0.09375
- stash_in: bfloat16 [2, 4, 4096, 4096], P('section', None, 'dp', 'tensor'), may hold values from -0.079589844 to 0.079589844
- stash_grad: bfloat16 [2, 3, 4096, 4096], P('section', None, 'dp'), may hold values from -6 to 6
- head_grad: bfloat16 [4096, 4096], P('dp'), may hold values from -6 to 6
- pending: int32 [2], replicated, may hold values from 1 to 4, as said below
Outputs:
- input_grad: float32 [2, 4096, 4096], P('section', 'dp', 'tensor')
- weight_grad: float32 [2, 4096, 4096], P('section', 'tensor', 'dp')
The draws below stay inside these ranges and needn't reach their ends.
Inputs may be any that keep to these rules, and one draw needn't show every extreme that they name: pending[s] counts the deferred tasks of segment s, which are its last pending[s] micro-batches; some segment has 4 of them.
All inputs are finite; a program needn't handle non-finite values.
Results may differ from the reference program's by a relative error of at most 0.0021.
Values may be sent and summed in bfloat16 or wider, within the bound.
No kernel may reach another device: no remote copies, remote signals or barrier semaphores. Data moves between devices by JAX's collectives and lax.ppermute only.
A program may use at most 128 MiB of HBM per device.

```python
import jax
import jax.numpy as jnp
from jax import lax

D = 4096
MICRO = 4
SEGMENTS = 2
ROWS = 4096


def draw_pending(key, part):
    key = jax.random.fold_in(key, 7)
    first, second = jax.random.split(key, 2)
    counts = jax.random.randint(first, (SEGMENTS,), 1, MICRO)
    fullest = jax.random.randint(second, (), 0, SEGMENTS)
    segment_ids = jnp.arange(SEGMENTS, dtype=jnp.int32)
    counts = jnp.where(segment_ids == fullest, MICRO, counts)
    return counts.astype(jnp.int32)


def strengthened(result, rng, source, target, shards_of, factor):
    owner, partner = [(jnp.arange(result.shape[axis_at]) // (result.shape[axis_at] // shards_of)).reshape([-1 if axis == axis_at else 1 for axis in range(result.ndim)]) for axis_at in (source, target)]
    chosen = jax.random.permutation(rng, shards_of)[partner]
    strong = (owner == chosen) | (owner == (partner + shards_of // 2) % shards_of)
    return jnp.where(strong, factor * result, result)


def block_levels(key, dims, cuts, least, top_value):
    def one(dim, shards_of):
        draws = jax.random.uniform(jax.random.fold_in(jax.random.fold_in(key, 6), dim), (shards_of,), jnp.float32, least / len(cuts), top_value / len(cuts))
        return jnp.repeat(jnp.exp(draws), dims[dim] // shards_of).reshape((-1,) + (1,) * (len(dims) - dim - 1))

    loudness = one(*cuts[0])
    for cut in cuts[1:]:
        loudness = loudness * one(*cut)
    return loudness


def gaussian(own_key, extent, deviation, bound, shards=(), held_as=jnp.bfloat16):
    drawn = jax.random.normal(own_key, extent, jnp.float32) * deviation
    if len(shards) > 0:
        drawn = block_levels(own_key, extent, shards, -0.22, 0.18) * drawn
    return jnp.clip(drawn, min=-bound, max=bound).astype(held_as)


def bell_draw_with(rng, dims, spread, most, pieces, heavy, held_as=jnp.bfloat16):
    array = spread * jax.random.normal(rng, dims, jnp.float32)
    if pieces:
        array = array * block_levels(rng, dims, pieces, -0.22, 0.18)
    return jnp.clip(strengthened(array, jax.random.fold_in(rng, 3), *heavy), -most, most).astype(held_as)


def setup_inputs(seed: int = 0) -> dict:
    key_of = jax.random.split(jax.random.key(seed), 6)
    weights = gaussian(key_of[0], (SEGMENTS, D, D), D ** -0.5, 0.09375, ((0, 2), (1, 4)))
    stash_in = gaussian(key_of[1], (SEGMENTS, MICRO, ROWS, D), 0.01, 0.079589844, ((0, 2), (2, 32), (3, 4)))
    stash_grad = bell_draw_with(key_of[2], (SEGMENTS, MICRO - 1, ROWS, D), 1.0, 6.0, ((0, 2), (2, 32)), (2, 3, 32, 2.75))
    head_grad = gaussian(key_of[3], (ROWS, D), 1.0, 6.0, ((0, 32),))
    pending = draw_pending(jax.random.fold_in(key_of[5], 71), 0)
    return {"weights": weights, "stash_in": stash_in, "stash_grad": stash_grad, "head_grad": head_grad, "pending": pending}


def segment_grad(items):
    inputs, grads, last, count = items
    grads_all = jnp.concatenate([grads, last[None]], 0)
    micro = jnp.arange(MICRO, dtype=jnp.int32)
    keep = micro >= MICRO - count
    masked = jnp.where(keep[:, None, None], inputs, jnp.zeros_like(inputs))
    return jnp.dot(masked.reshape(-1, D).T, grads_all.reshape(-1, D), preferred_element_type=jnp.float32)

def reference(weights, stash_in, stash_grad, head_grad, pending):
    grad = head_grad
    lasts = []
    inputs_out = []
    for segment in range(SEGMENTS - 1, -1, -1):
        lasts.append(grad)
        exact = jnp.dot(grad, weights[segment].T, preferred_element_type=jnp.float32)
        inputs_out.append(exact)
        grad = exact.astype(jnp.bfloat16)
    last_grad = jnp.stack(lasts[::-1], 0)
    input_grad = jnp.stack(inputs_out[::-1], 0)
    weight_grad = lax.map(segment_grad, (stash_in, stash_grad, last_grad, pending))
    return (input_grad, weight_grad)
```

```python
import functools

import jax
import jax.numpy as jnp
from jax import lax
from jax.experimental import pallas as pl
from jax.experimental.pallas import tpu as pltpu
from jax.sharding import Mesh
from jax.sharding import PartitionSpec as P

F32 = jnp.float32
BF16 = jnp.bfloat16
RING = 4
LANES = 128


def block_index(pos, zr, yr, xr):
    z = lax.rem(pos[0] + zr, 2)
    y = lax.rem(pos[1] + yr, RING)
    x = lax.rem(pos[2] + xr, RING)
    return z * (RING * RING) + y * RING + x


SEND_RIGHT = [(0, 2, j) for j in range(RING)] + [(1, 1, j) for j in range(RING)]
SEND_LEFT = [(1, 2, j) for j in range(RING)] + [(0, 3, j) for j in range(RING)]
PASS_ON = [(0, 1, j) for j in range(RING)] + [(1, 3, j) for j in range(RING)]
KEEP = [(0, 0, j) for j in range(RING)] + [(1, 0, j) for j in range(RING)]


def products_kernel(plans, pos_ref, x_ref, stash_ref, head_ref, rel_ref, *rest):
    outs, xt_ref = rest[:-1], rest[-1]
    micro, rows, width = x_ref.shape
    half = width // 2
    pos = (pos_ref[0], pos_ref[1], pos_ref[2])
    tensor, is_last, count = pos_ref[3], pos_ref[4], pos_ref[5]
    for m in range(micro):
        keep = (m >= micro - count).astype(F32)
        masked = jnp.where(keep > 0, x_ref[m].astype(F32), 0.0)
        xt_ref[:, m * rows:(m + 1) * rows] = masked.T.astype(BF16)
    shard_blocks = rel_ref.shape[2] // LANES

    def columns(block):
        at = pl.multiple_of(block * LANES, LANES)
        parts = [stash_ref[m, :, pl.ds(at, LANES)] for m in range(micro - 1)]
        owner = lax.div(block, shard_blocks)
        turn = lax.rem(tensor - owner + RING, RING)
        inner = pl.multiple_of(lax.rem(block, shard_blocks) * LANES, LANES)
        chained = rel_ref[turn, :, pl.ds(inner, LANES)]
        given = head_ref[:, pl.ds(at, LANES)]
        parts.append(jnp.where(is_last > 0, given, chained))
        return jnp.concatenate(parts, axis=0)

    for out, (part, slots) in zip(outs, plans):
        xt = xt_ref[part * half:(part + 1) * half, :]
        for j in range(0, len(slots), 2):
            pair = []
            for zr, along, across in slots[j:j + 2]:
                yr, xr = (across, along) if part == 0 else (along, across)
                pair.append(columns(block_index(pos, zr, yr, xr)))
            both = jnp.dot(xt, jnp.concatenate(pair, axis=1), preferred_element_type=F32)
            out[j * half:(j + 1) * half, :] = both[:, :LANES].astype(out.dtype)
            out[(j + 1) * half:(j + 2) * half, :] = both[:, LANES:].astype(out.dtype)


def products(plans, dtypes, pos, inputs, stash_grad, head_grad, rel):
    micro, rows, width = inputs.shape
    half = width // 2
    whole = pl.BlockSpec(memory_space=pltpu.VMEM)
    shapes = [jax.ShapeDtypeStruct((len(slots) * half, LANES), dtype) for (_, slots), dtype in zip(plans, dtypes)]
    n_slots = sum(len(slots) for _, slots in plans)
    return pl.pallas_call(
        functools.partial(products_kernel, plans),
        out_shape=shapes,
        in_specs=[pl.BlockSpec(memory_space=pltpu.SMEM)] + [whole] * 4,
        out_specs=[whole] * len(shapes),
        scratch_shapes=[pltpu.VMEM((width, micro * rows), BF16)],
        compiler_params=pltpu.CompilerParams(vmem_limit_bytes=40 * 2**20),
        cost_estimate=pl.CostEstimate(
            flops=2 * n_slots * half * LANES * micro * rows,
            bytes_accessed=6 * 2**20 + n_slots * half * LANES * 4,
            transcendentals=0,
        ),
    )(pos, inputs, stash_grad, head_grad, rel)


def shifted(value, axis, by):
    return lax.ppermute(value, axis, [(i, (i + by) % RING) for i in range(RING)])


def local(weights, stash_in, stash_grad, head_grad, pending):
    segment = lax.axis_index("section")
    is_last = segment == lax.axis_size("section") - 1
    tensor = lax.axis_index("z_lo")
    weight = weights[0]
    inputs, grads = stash_in[0], stash_grad[0]
    rows = head_grad.shape[0]

    def backward_step(grad):
        return lax.dot_general(grad, weight, (((1,), (1,)), ((), ())), preferred_element_type=F32)

    first = backward_step(head_grad)
    shard = lax.ppermute(first.astype(BF16), "section", [(1, 0)])
    rel = [shard]
    for by in range(1, RING):
        pairs = [(i, (i + by) % RING) for i in range(RING)]
        rel.append(lax.ppermute(shard, ("section", "z_lo"), pairs))
    rel_stack = jnp.stack(rel, 0)

    count = lax.dynamic_index_in_dim(pending, segment, 0, keepdims=False)
    place = [lax.axis_index("z_hi"), lax.axis_index("y"), lax.axis_index("x"), tensor, is_last, count]
    pos = jnp.stack([v.astype(jnp.int32) for v in place])
    args = (pos, inputs, grads, head_grad, rel_stack)
    axes = ("x", "y")
    sends = products([(part, s) for part in (0, 1) for s in (SEND_RIGHT, SEND_LEFT)], [BF16] * 4, *args)
    got = []
    for part in (0, 1):
        got.append((shifted(sends[2 * part], axes[part], 1), shifted(sends[2 * part + 1], axes[part], -1)))
    own = products([(part, s) for part in (0, 1) for s in (PASS_ON, KEEP)], [F32] * 4, *args)
    mid = own[0].shape[0] // 2
    passed = []
    for part in (0, 1):
        from_left, from_right = got[part]
        going = own[2 * part]
        right = (going[:mid] + from_left[:mid].astype(F32)).astype(BF16)
        left = (going[mid:] + from_right[:mid].astype(F32)).astype(BF16)
        passed.append((shifted(right, axes[part], 1), shifted(left, axes[part], -1)))
    totals = []
    for part in (0, 1):
        from_left, from_right = got[part]
        late_left, late_right = passed[part]
        kept = own[2 * part + 1]
        near = kept[:mid] + from_right[mid:].astype(F32) + late_left.astype(F32)
        far = kept[mid:] + from_left[mid:].astype(F32) + late_right.astype(F32)
        both = jnp.stack([near, far], 0).reshape(2, RING, -1, LANES)
        axis = axes[1 - part]
        total = both[:, 0]
        for by in range(1, RING):
            total = total + shifted(both[:, by], axis, by)
        totals.append(total)
    block = jnp.concatenate(totals, 1)
    block = block[0] + lax.ppermute(block[1], "z_hi", [(0, 1), (1, 0)])
    weight_grad = block[None]

    order = jnp.stack(rel[::-1] + rel[::-1], 0)
    whole = lax.dynamic_slice_in_dim(order, RING - 1 - tensor, RING, 0)
    whole = jnp.moveaxis(whole, 0, 1).reshape(rows, -1)
    second = backward_step(whole)
    input_grad = jnp.where(is_last, first, second)[None]
    return (input_grad, weight_grad)


def solution(mesh):
    fine = Mesh(mesh.devices.reshape(2, 4, 2, 4, 4), ("section", "z_lo", "z_hi", "y", "x"))
    dp = ("z_hi", "y", "x")
    return jax.shard_map(
        local,
        mesh=fine,
        in_specs=(
            P("section", "z_lo", None),
            P("section", None, dp, "z_lo"),
            P("section", None, dp, None),
            P(dp, None),
            P(),
        ),
        out_specs=(P("section", dp, "z_lo"), P("section", "z_lo", dp)),
        check_vma=False,
    )
```

```python
import functools
import math

import jax
import jax.numpy as jnp
from jax import lax
from jax.experimental import pallas as pl
from jax.experimental.pallas import tpu as pltpu
from jax.sharding import Mesh
from jax.sharding import PartitionSpec as P

F32 = jnp.float32
F16 = jnp.float16
BF16 = jnp.bfloat16
RING = 4
LANES = 128
TAIL = 16
TOP = 15
TINY = 1e-30

SEND_RIGHT = [(0, 2, j) for j in range(RING)] + [(1, 1, j) for j in range(RING)]
SEND_LEFT = [(1, 2, j) for j in range(RING)] + [(0, 3, j) for j in range(RING)]
PASS_RIGHT = [(0, 1, j) for j in range(RING)]
PASS_LEFT = [(1, 3, j) for j in range(RING)]
KEEP_NEAR = [(0, 0, j) for j in range(RING)]
KEEP_FAR = [(1, 0, j) for j in range(RING)]
FIRST = [(part, s) for part in (0, 1) for s in (SEND_RIGHT, SEND_LEFT)]
OWN = [(part, s) for part in (0, 1) for s in (PASS_RIGHT, PASS_LEFT, KEEP_NEAR, KEEP_FAR)]


def on_last():
    return lax.axis_index("section") == lax.axis_size("section") - 1


def block_index(zr, yr, xr):
    z = lax.rem(lax.axis_index("z_hi") + zr, 2)
    y = lax.rem(lax.axis_index("y") + yr, RING)
    x = lax.rem(lax.axis_index("x") + xr, RING)
    return z * (RING * RING) + y * RING + x


def largest(value):
    return jnp.max(jnp.max(jnp.abs(value.astype(F32)), axis=0, keepdims=True), axis=1, keepdims=True)


def products_kernel(plans, scaled, pending_ref, x_ref, stash_ref, head_ref, rel_ref, *rest):
    outs, xt_ref = rest[:-1], rest[-1]
    micro, rows, width = x_ref.shape
    half = width // 2
    tensor, is_last = lax.axis_index("z_lo"), on_last()
    count = pending_ref[lax.axis_index("section")]
    bound = jnp.full((1, 1), TINY, F32)
    for m in range(micro):
        masked = jnp.where(m >= micro - count, x_ref[m].astype(F32), 0.0)
        xt_ref[:, m * rows:(m + 1) * rows] = masked.T.astype(BF16)
        if scaled:
            if m < micro - 1:
                top = largest(stash_ref[m])
            else:
                chained = functools.reduce(jnp.maximum, [largest(rel_ref[k]) for k in range(RING)])
                top = jnp.where(is_last, largest(head_ref[...]), chained)
            bound = bound + rows * largest(masked) * top
    if scaled:
        power = jnp.broadcast_to(jnp.ceil(jnp.log2(bound)) - TOP, (1, LANES))
        factor = jnp.exp2(-power)
    shard_blocks = rel_ref.shape[2] // LANES

    def columns(block):
        at = pl.multiple_of(block * LANES, LANES)
        parts = [stash_ref[m, :, pl.ds(at, LANES)] for m in range(micro - 1)]
        owner = lax.div(block, shard_blocks)
        turn = lax.rem(tensor - owner + RING, RING)
        inner = pl.multiple_of(lax.rem(block, shard_blocks) * LANES, LANES)
        chained = rel_ref[turn, :, pl.ds(inner, LANES)]
        given = head_ref[:, pl.ds(at, LANES)]
        parts.append(jnp.where(is_last, given, chained))
        return jnp.concatenate(parts, axis=0)

    for out, (part, slots) in zip(outs, plans):
        xt = xt_ref[part * half:(part + 1) * half, :]
        for j in range(0, len(slots), 2):
            pair = []
            for zr, along, across in slots[j:j + 2]:
                yr, xr = (across, along) if part == 0 else (along, across)
                pair.append(columns(block_index(zr, yr, xr)))
            both = jnp.dot(xt, jnp.concatenate(pair, axis=1), preferred_element_type=F32)
            for k in range(2):
                tile = both[:, k * LANES:(k + 1) * LANES]
                if scaled:
                    tile = tile * factor
                out[(j + k) * half:(j + k + 1) * half, :] = tile
        if scaled:
            out[len(slots) * half:, :] = jnp.broadcast_to(power, (TAIL, LANES))


def products(plans, scaled, pending, inputs, stash_grad, head_grad, rel):
    micro, rows, width = inputs.shape
    half = width // 2
    whole = pl.BlockSpec(memory_space=pltpu.VMEM)
    extra = TAIL if scaled else 0
    shapes = [jax.ShapeDtypeStruct((len(slots) * half + extra, LANES), F32) for _, slots in plans]
    n_slots = sum(len(slots) for _, slots in plans)
    return pl.pallas_call(
        functools.partial(products_kernel, plans, scaled),
        out_shape=shapes,
        in_specs=[pl.BlockSpec(memory_space=pltpu.SMEM)] + [whole] * 4,
        out_specs=[whole] * len(shapes),
        scratch_shapes=[pltpu.VMEM((width, micro * rows), BF16)],
        compiler_params=pltpu.CompilerParams(vmem_limit_bytes=40 * 2**20),
        cost_estimate=pl.CostEstimate(
            flops=2 * n_slots * half * LANES * micro * rows,
            bytes_accessed=6 * 2**20 + n_slots * half * LANES * 4,
            transcendentals=0,
        ),
    )(pending, inputs, stash_grad, head_grad, rel)


CONTRACT_LAST = (((1,), (1,)), ((), ()))


def first_kernel(grad_ref, weight_ref, out_ref, small_ref):
    out = lax.dot_general(grad_ref[...], weight_ref[...], CONTRACT_LAST, preferred_element_type=F32)
    out_ref[...] = out
    small_ref[...] = out.astype(BF16)


def second_kernel(rel_ref, weight_ref, first_ref, out_ref):
    tensor = lax.axis_index("z_lo")
    share = rel_ref.shape[2]
    total = jnp.zeros(out_ref.shape, F32)
    for k in range(RING):
        owner = lax.rem(tensor - k + RING, RING)
        cols = weight_ref[:, pl.ds(pl.multiple_of(owner * share, share), share)]
        total = total + lax.dot_general(rel_ref[k], cols, CONTRACT_LAST, preferred_element_type=F32)
    out_ref[...] = jnp.where(on_last(), first_ref[...], total)


def chain_call(kernel, out_types, grad, weight, *more, step=256):
    rows = grad.shape[-2]
    width, depth = weight.shape
    tile = pl.BlockSpec((rows, step), lambda i: (0, i))
    outs = [jax.ShapeDtypeStruct((rows, width), t) for t in out_types]
    return pl.pallas_call(
        kernel,
        grid=(width // step,),
        out_shape=outs,
        in_specs=[pl.BlockSpec(memory_space=pltpu.VMEM), pl.BlockSpec((step, depth), lambda i: (i, 0))] + [tile] * len(more),
        out_specs=[tile] * len(outs),
        compiler_params=pltpu.CompilerParams(vmem_limit_bytes=24 * 2**20),
        cost_estimate=pl.CostEstimate(flops=2 * rows * width * depth, bytes_accessed=2 * width * depth + 2**21, transcendentals=0),
    )(grad, weight, *more)


def shifted(value, axis, by):
    return lax.ppermute(value, axis, [(i, (i + by) % RING) for i in range(RING)])


def packed(parts, powers):
    power = functools.reduce(jnp.maximum, powers) + math.ceil(math.log2(len(powers)))
    factor = jnp.exp2(-power)
    rows = [(p * factor).astype(F16) for p in parts]
    return jnp.concatenate(rows + [jnp.broadcast_to(power, (TAIL, LANES)).astype(F16)], 0)


def opened(buffer):
    power = buffer[-1:].astype(F32)
    return buffer[:-TAIL].astype(F32) * jnp.exp2(power), power


def ring(axes, sends, pass_on, keeps, powers):
    got = [(opened(shifted(r, a, 1)), opened(shifted(l, a, -1))) for a, (r, l) in zip(axes, sends)]
    late = []
    for a, ((left, p_left), (right, p_right)), (to_right, to_left), power in zip(axes, got, pass_on, powers):
        mid = left.shape[0] // 2
        go_right = packed([to_right + left[:mid]], power + [p_left])
        go_left = packed([to_left + right[:mid]], power + [p_right])
        late.append((opened(shifted(go_right, a, 1)), opened(shifted(go_left, a, -1))))
    sums, all_powers = [], []
    for near_far, one, two, power in zip(keeps, got, late, powers):
        (left, p_left), (right, p_right) = one
        (left_2, p_left_2), (right_2, p_right_2) = two
        mid = left.shape[0] // 2
        sums.append((near_far[0] + right[mid:] + left_2, near_far[1] + left[mid:] + right_2))
        all_powers.append(power + [p_left, p_right, p_left_2, p_right_2])
    return sums, all_powers


def local(weights, stash_in, stash_grad, head_grad, pending):
    weight = weights[0]
    inputs, grads = stash_in[0], stash_grad[0]

    first, small = chain_call(first_kernel, (F32, BF16), head_grad, weight)
    rel = []
    for by in range(RING):
        pairs = [(RING + i, (i + by) % RING) for i in range(RING)]
        rel.append(lax.ppermute(small, ("section", "z_lo"), pairs))
    rel = jnp.stack(rel, 0)

    args = (pending, inputs, grads, head_grad, rel)
    first_out = products(FIRST, True, *args)
    sends = [[b.astype(F16) for b in first_out[2 * p:2 * p + 2]] for p in (0, 1)]
    power = first_out[0][-1:]
    own = products(OWN, False, *args)
    (second,) = chain_call(second_kernel, (F32,), rel, weight, first)
    own, second = lax.optimization_barrier((own, second))
    powers = [[power], [power]]
    sums, powers = ring(("x", "y"), sends, [own[0:2], own[4:6]], [own[2:4], own[6:8]], powers)

    size = sums[0][0].shape[0] // RING
    cut = [[[v[j * size:(j + 1) * size] for j in range(RING)] for v in pair] for pair in sums]
    sends = [
        (packed([near[2], far[1]], p), packed([far[2], near[3]], p)) for (near, far), p in zip(cut, powers)
    ]
    powers = [[functools.reduce(jnp.maximum, p) + 3] for p in powers]
    pass_on = [(near[1], far[3]) for near, far in cut]
    keeps = [(near[0], far[0]) for near, far in cut]
    sums, powers = ring(("y", "x"), sends, pass_on, keeps, powers)

    far = packed([pair[1] for pair in sums], [functools.reduce(jnp.maximum, p) + 3 for p in powers])
    near = jnp.concatenate([pair[0] for pair in sums], 0)
    other, _ = opened(lax.ppermute(far, "z_hi", [(0, 1), (1, 0)]))
    return (second[None], (near + other)[None])


def solution(mesh):
    fine = Mesh(mesh.devices.reshape(2, 4, 2, 4, 4), ("section", "z_lo", "z_hi", "y", "x"))
    dp = ("z_hi", "y", "x")
    return jax.shard_map(
        local,
        mesh=fine,
        in_specs=(
            P("section", "z_lo", None),
            P("section", None, dp, "z_lo"),
            P("section", None, dp, None),
            P(dp, None),
            P(),
        ),
        out_specs=(P("section", dp, "z_lo"), P("section", "z_lo", dp)),
        check_vma=False,
    )
```

```python
import functools

import jax
import jax.numpy as jnp
from jax import lax
from jax.experimental import pallas as pl
from jax.experimental.pallas import tpu as pltpu
from jax.sharding import Mesh
from jax.sharding import PartitionSpec as P

F32 = jnp.float32
F16 = jnp.float16
BF16 = jnp.bfloat16
RING = 4
LANES = 128
TAIL = 16
TOP = 15
TINY = 1e-30


def section():
    return lax.axis_index("section")


def on_last():
    return section() == lax.axis_size("section") - 1


def block_start(z_off, along, across):
    first = section() == 0
    y_off, x_off = jnp.where(first, across, along), jnp.where(first, along, across)
    z = lax.rem(lax.axis_index("z_hi") + z_off, 2)
    y = lax.rem(lax.axis_index("y") + y_off, RING)
    x = lax.rem(lax.axis_index("x") + x_off, RING)
    return pl.multiple_of((z * (RING * RING) + y * RING + x) * LANES, LANES)


def pairs_over(along, by):
    size, pairs = RING * RING, []
    for s in range(2):
        for y in range(RING):
            for x in range(RING):
                on_x = (s == 0) == along
                there = (y, (x + by) % RING) if on_x else ((y + by) % RING, x)
                pairs.append((s * size + y * RING + x, s * size + there[0] * RING + there[1]))
    return pairs


def shifted(value, along, by):
    return lax.ppermute(value, ("section", "y", "x"), pairs_over(along, by))


def whole(n=1):
    return [pl.BlockSpec(memory_space=pltpu.VMEM)] * n


def call(kernel, out_shapes, operands, specs, scratch=(), flops=0, moved=0, limit=32):
    return pl.pallas_call(
        kernel,
        out_shape=[jax.ShapeDtypeStruct(s, t) for s, t in out_shapes],
        in_specs=specs,
        out_specs=whole(len(out_shapes)),
        scratch_shapes=list(scratch),
        compiler_params=pltpu.CompilerParams(vmem_limit_bytes=limit * 2**20),
        cost_estimate=pl.CostEstimate(flops=flops, bytes_accessed=moved, transcendentals=0),
    )(*operands)


def pack_stash_kernel(pending_ref, x_ref, stash_ref, right_ref, left_ref, own_ref):
    micro, rows, width = x_ref.shape
    count = pending_ref[section()]
    for m in range(micro):
        turned = jnp.where(m >= micro - count, x_ref[m].astype(F32), 0.0).T.astype(BF16)
        right_ref[:width, m * rows:(m + 1) * rows] = turned
        left_ref[:width, m * rows:(m + 1) * rows] = turned
    depth = stash_ref.shape[0] * rows
    for out, base, along in ((right_ref, width, 1), (left_ref, width, RING - 1), (own_ref, 0, 0)):
        for z in range(2):
            for b in range(RING):
                at = block_start(z, along, b)
                for m in range(stash_ref.shape[0]):
                    top = base + z * depth + m * rows
                    out[top:top + rows, b * LANES:(b + 1) * LANES] = stash_ref[m, :, pl.ds(at, LANES)]


def pack_last_kernel(stash_ref, head_ref, rel_ref, right_ref, left_ref, own_ref, far_ref):
    tensor = lax.axis_index("z_lo")
    rows, share = rel_ref.shape[1], rel_ref.shape[2]
    earlier = stash_ref.shape[0]

    def last(at):
        owner = lax.div(at, share)
        inner = pl.multiple_of(lax.rem(at, share), LANES)
        chained = rel_ref[lax.rem(tensor - owner + RING, RING), :, pl.ds(inner, LANES)]
        return jnp.where(on_last(), head_ref[:, pl.ds(at, LANES)], chained)

    for z in range(2):
        for b in range(RING):
            lanes = slice(b * LANES, (b + 1) * LANES)
            for out, along in ((right_ref, 1), (left_ref, RING - 1), (own_ref, 0)):
                out[z * rows:(z + 1) * rows, lanes] = last(block_start(z, along, b))
            at = block_start(z, 2, b)
            top = z * (earlier + 1) * rows
            for m in range(earlier):
                far_ref[top + m * rows:top + (m + 1) * rows, lanes] = stash_ref[m, :, pl.ds(at, LANES)]
            far_ref[top + earlier * rows:top + (earlier + 1) * rows, lanes] = last(at)


def early_kernel(mine_ref, own_ref, left_ref, right_ref, acc_ref):
    width, depth = acc_ref.shape[0], own_ref.shape[0] // 2
    half = acc_ref.shape[1] // 2
    step = width // 2
    for r in range(0, width, step):
        lhs = jnp.concatenate([ref[r:r + step, :depth] for ref in (mine_ref, left_ref, right_ref)], axis=1)
        for z in range(2):
            sides = [own_ref[z * depth:(z + 1) * depth, :]]
            sides += [ref[width + z * depth:width + (z + 1) * depth, :] for ref in (left_ref, right_ref)]
            rhs = jnp.concatenate(sides, axis=0)
            acc_ref[r:r + step, z * half:(z + 1) * half] = jnp.dot(lhs, rhs, preferred_element_type=F32)


def late_kernel(acc_ref, mine_ref, left_ref, right_ref, top_ref, low_ref, own_last_ref, left_last_ref, right_last_ref,
                far_ref, keep_ref, *rest):
    sends, sum_ref = rest[:-1], rest[-1]
    width, rows = acc_ref.shape[0], own_last_ref.shape[0] // 2
    half = acc_ref.shape[1] // 2
    step = width // 2
    full = far_ref.shape[0] // 2
    largest = jnp.full((1, half), TINY, F32)
    for r, there in ((0, top_ref), (step, low_ref)):
        lhs = [ref[r:r + step, full - rows:] for ref in (mine_ref, left_ref, right_ref)]
        lhs = jnp.concatenate(lhs + [there[...]], axis=1)
        for z in range(2):
            rhs = [ref[z * rows:(z + 1) * rows, :] for ref in (own_last_ref, left_last_ref, right_last_ref)]
            rhs = jnp.concatenate(rhs + [far_ref[z * full:(z + 1) * full, :]], axis=0)
            total = acc_ref[r:r + step, z * half:(z + 1) * half] + jnp.dot(lhs, rhs, preferred_element_type=F32)
            largest = jnp.maximum(largest, jnp.max(jnp.abs(total), axis=0, keepdims=True))
            sum_ref[r:r + step, z * half:(z + 1) * half] = total
    power = jnp.ceil(jnp.log2(jnp.max(largest, axis=1, keepdims=True))) - TOP
    power = jnp.broadcast_to(power, (1, LANES))
    factor = jnp.exp2(-power)
    for z in range(2):
        keep_ref[z * width:(z + 1) * width, :] = sum_ref[:, z * half:z * half + LANES]
        for b, out in enumerate(sends, 1):
            lanes = slice(z * half + b * LANES, z * half + (b + 1) * LANES)
            out[z * width:(z + 1) * width, :] = sum_ref[:, lanes] * factor
    for out in sends:
        out[2 * width:, :] = jnp.broadcast_to(power, (TAIL, LANES))


def combine_kernel(keep_ref, one_ref, two_ref, three_ref, near_ref, far_ref):
    rows = near_ref.shape[0]
    totals = []
    for z in range(2):
        total = keep_ref[z * rows:(z + 1) * rows, :]
        for ref in (one_ref, two_ref, three_ref):
            total = total + ref[z * rows:(z + 1) * rows, :] * jnp.exp2(ref[2 * rows:2 * rows + 1, :])
        totals.append(total)
    near_ref[...] = totals[0]
    largest = jnp.maximum(jnp.max(jnp.abs(totals[1]), axis=0, keepdims=True), TINY)
    power = jnp.ceil(jnp.log2(jnp.max(largest, axis=1, keepdims=True))) - TOP
    power = jnp.broadcast_to(power, (1, LANES))
    far_ref[:rows, :] = totals[1] * jnp.exp2(-power)
    far_ref[rows:, :] = jnp.broadcast_to(power, (TAIL, LANES))


CONTRACT_LAST = (((1,), (1,)), ((), ()))


def weight_copies(weight_ref, held_ref, sems):
    copies = [pltpu.make_async_copy(weight_ref.at[pl.ds(i * held_ref.shape[1], held_ref.shape[1])], held_ref.at[i], sems.at[i])
              for i in range(held_ref.shape[0])]
    for copy in copies:
        copy.start()
    return copies


def first_kernel(grad_ref, weight_ref, out_ref, small_ref, held_ref, sems):
    step = held_ref.shape[1]
    for i, copy in enumerate(weight_copies(weight_ref, held_ref, sems)):
        copy.wait()
        out = lax.dot_general(grad_ref[...], held_ref[i], CONTRACT_LAST, preferred_element_type=F32)
        out_ref[:, i * step:(i + 1) * step] = out
        small_ref[:, i * step:(i + 1) * step] = out.astype(BF16)


def second_kernel(rel_ref, first_ref, weight_ref, out_ref, held_ref, sems):
    step, share = held_ref.shape[1], rel_ref.shape[2]
    tensor = lax.axis_index("z_lo")
    for i, copy in enumerate(weight_copies(weight_ref, held_ref, sems)):
        copy.wait()
        total = jnp.zeros((rel_ref.shape[1], step), F32)
        for k in range(RING):
            owner = lax.rem(tensor - k + RING, RING)
            cols = held_ref[i, :, pl.ds(pl.multiple_of(owner * share, share), share)]
            total = total + lax.dot_general(rel_ref[k], cols, CONTRACT_LAST, preferred_element_type=F32)
        lanes = slice(i * step, (i + 1) * step)
        out_ref[:, lanes] = jnp.where(on_last(), first_ref[:, lanes], total)


def chain_call(kernel, out_types, operands, weight, rows):
    width, depth = weight.shape
    parts = 4
    return call(
        kernel,
        [((rows, width), t) for t in out_types],
        operands + [weight],
        whole(len(operands)) + [pl.BlockSpec(memory_space=pltpu.HBM)],
        scratch=[pltpu.VMEM((parts, width // parts, depth), weight.dtype), pltpu.SemaphoreType.DMA((parts,))],
        flops=2 * rows * width * depth,
        moved=2 * width * depth, limit=48,
    )


def local(weights, stash_in, stash_grad, head_grad, pending):
    weight = weights[0]
    inputs, grads = stash_in[0], stash_grad[0]
    micro, rows, width = inputs.shape
    depth = (micro - 1) * rows
    half = RING * LANES
    smem = [pl.BlockSpec(memory_space=pltpu.SMEM)]

    side = ((width + 2 * depth, half), BF16)
    right, left, own = call(
        pack_stash_kernel, [side, side, ((2 * depth, half), BF16)], (pending, inputs, grads), smem + whole(2),
        moved=12 * 2**20,
    )
    right, left, head = lax.optimization_barrier((right, left, head_grad))
    from_left, from_right = shifted(right, True, 1), shifted(left, True, -1)

    first, small = chain_call(first_kernel, (F32, BF16), [head], weight, rows)
    shard = lax.ppermute(small, "section", [(1, 0)])
    rel = [shard]
    for by in range(1, RING):
        rel.append(lax.ppermute(shard, ("section", "z_lo"), [(i, (i + by) % RING) for i in range(RING)]))
    rel = jnp.stack(rel, 0)

    edge = ((2 * rows, half), BF16)
    edge_right, edge_left, own_last, far = call(
        pack_last_kernel, [edge, edge, edge, ((2 * micro * rows, half), BF16)], (grads, head_grad, rel), whole(3),
        moved=8 * 2**20,
    )
    from_left, from_right, edge_right, edge_left, far = lax.optimization_barrier(
        (from_left, from_right, edge_right, edge_left, far)
    )
    top = shifted(from_left[:width // 2], True, 1)
    low = shifted(from_right[width // 2:width], True, -1)
    last_left, last_right = shifted(edge_right, True, 1), shifted(edge_left, True, -1)
    far = shifted(far, True, 2)
    (acc,) = call(
        early_kernel, [((width, 2 * half), F32)], (right, own, from_left, from_right), whole(4),
        flops=2 * width * 2 * half * 3 * depth, moved=12 * 2**20,
    )
    (second,) = chain_call(second_kernel, (F32,), [rel, first], weight, rows)
    acc, second = lax.optimization_barrier((acc, second))
    send = ((2 * width + TAIL, LANES), F32)
    keep, *sends = call(
        late_kernel, [((2 * width, LANES), F32)] + [send] * 3,
        (acc, right, from_left, from_right, top, low, own_last, last_left, last_right, far), whole(10),
        scratch=[pltpu.VMEM((width, 2 * half), F32)],
        flops=2 * width * 2 * half * (3 * rows + micro * rows), moved=12 * 2**20,
    )
    got = [shifted(s.astype(F16), False, by).astype(F32) for by, s in enumerate(sends, 1)]
    near, far = call(
        combine_kernel, [((width, LANES), F32), ((width + TAIL, LANES), F32)], (keep, *got), whole(4), moved=6 * 2**20,
    )
    other = lax.ppermute(far.astype(F16), "z_hi", [(0, 1), (1, 0)])
    block = near + other[:width].astype(F32) * jnp.exp2(other[width:width + 1].astype(F32))
    return (second[None], block[None])


def solution(mesh):
    fine = Mesh(mesh.devices.reshape(2, 4, 2, 4, 4), ("section", "z_lo", "z_hi", "y", "x"))
    dp = ("z_hi", "y", "x")
    return jax.shard_map(
        local,
        mesh=fine,
        in_specs=(
            P("section", "z_lo", None),
            P("section", None, dp, "z_lo"),
            P("section", None, dp, None),
            P(dp, None),
            P(),
        ),
        out_specs=(P("section", dp, "z_lo"), P("section", "z_lo", dp)),
        check_vma=False,
    )
```

```python
import functools

import jax
import jax.numpy as jnp
from jax import lax
from jax.experimental import pallas as pl
from jax.experimental.pallas import tpu as pltpu
from jax.sharding import Mesh
from jax.sharding import PartitionSpec as P

F32 = jnp.float32
F16 = jnp.float16
BF16 = jnp.bfloat16
RING = 4
LANES = 128
TAIL = 16
TOP = 15
TINY = 1e-30
ENTRY_LIMIT = 40
SECOND_LIMIT = 40


def section():
    return lax.axis_index("section")


def on_last():
    return section() == lax.axis_size("section") - 1


def block_start(z_off, along, across):
    first = section() == 0
    y_off, x_off = jnp.where(first, across, along), jnp.where(first, along, across)
    z = lax.rem(lax.axis_index("z_hi") + z_off, 2)
    y = lax.rem(lax.axis_index("y") + y_off, RING)
    x = lax.rem(lax.axis_index("x") + x_off, RING)
    return pl.multiple_of((z * (RING * RING) + y * RING + x) * LANES, LANES)


def pairs_over(along, by):
    size, pairs = RING * RING, []
    for s in range(2):
        for y in range(RING):
            for x in range(RING):
                on_x = (s == 0) == along
                there = (y, (x + by) % RING) if on_x else ((y + by) % RING, x)
                pairs.append((s * size + y * RING + x, s * size + there[0] * RING + there[1]))
    return pairs


def shifted(value, along, by):
    return lax.ppermute(value, ("section", "y", "x"), pairs_over(along, by))


def whole(n=1):
    return [pl.BlockSpec(memory_space=pltpu.VMEM)] * n


def in_hbm(value):
    return pltpu.with_memory_space_constraint(value, pltpu.HBM)


def call(kernel, out_shapes, operands, specs, scratch=(), flops=0, moved=0, limit=32):
    return pl.pallas_call(
        kernel,
        out_shape=[jax.ShapeDtypeStruct(s, t) for s, t in out_shapes],
        in_specs=specs,
        out_specs=whole(len(out_shapes)),
        scratch_shapes=list(scratch),
        compiler_params=pltpu.CompilerParams(vmem_limit_bytes=limit * 2**20),
        cost_estimate=pl.CostEstimate(flops=flops, bytes_accessed=moved, transcendentals=0),
    )(*operands)


CONTRACT_LAST = (((1,), (1,)), ((), ()))


def entry_kernel(pending_ref, x_ref, stash_ref, head_ref, weight_ref, right_ref, left_ref, own_ref, first_ref, pieces_ref,
                 x_in, stash_in, head_in, weight_in, sems, count_in):
    micro, rows, width = x_ref.shape
    half = width // 2
    counts = pltpu.make_async_copy(pending_ref, count_in, sems.at[micro + 5])
    counts.start()
    pieces = [(x_ref, x_in)]
    pieces += [(stash_ref.at[m], stash_in.at[m]) for m in range(micro - 1)] + [(head_ref, head_in)]
    parts = 4
    share = width // parts
    pieces += [(weight_ref.at[pl.ds(i * share, share)], weight_in.at[i]) for i in range(parts)]
    copies = [pltpu.make_async_copy(a, b, sems.at[i]) for i, (a, b) in enumerate(pieces)]
    stashes, weights = copies[1:1 + micro], copies[1 + micro:]
    for copy in copies[:1 + micro]:
        copy.start()
    copies[0].wait()
    weights[0].start()
    counts.wait()
    count = count_in[section()]
    for m in range(micro):
        turned = jnp.where(m >= micro - count, x_in[m].astype(F32), 0.0).T.astype(BF16)
        lanes = slice(m * rows, (m + 1) * rows)
        for out, order in ((right_ref, (half, 0)), (left_ref, (0, half))):
            for at, top in zip((0, half), order):
                out[at:at + half, lanes] = turned[top:top + half]
    full = micro * rows
    plans = [(right_ref, width, 0, 2), (left_ref, width, 1, 2)]
    for z in range(2):
        plans += [(right_ref, width + (1 + z) * full, z, 1), (left_ref, width + (1 + z) * full, z, RING - 1), (own_ref, z * full, z, 0)]
    for m in range(micro):
        stashes[m].wait()
        if m < parts - 1:
            weights[m + 1].start()
        source = stash_in.at[m] if m < micro - 1 else head_in
        for out, base, z, along in plans:
            for b in range(RING):
                top = base + m * rows
                out[top:top + rows, b * LANES:(b + 1) * LANES] = source[:, pl.ds(block_start(z, along, b), LANES)]
    for i in range(parts):
        weights[i].wait()
        out = lax.dot_general(head_in[...], weight_in[i], CONTRACT_LAST, preferred_element_type=F32)
        first_ref[:, i * share:(i + 1) * share] = out
    for p in range(RING):
        x_at = lax.rem(lax.axis_index("x") + p, RING)
        for inner in range(2):
            cols = pl.ds(pl.multiple_of((inner * RING + x_at) * LANES, LANES), LANES)
            pieces_ref[p * rows:(p + 1) * rows, inner * LANES:(inner + 1) * LANES] = first_ref[:, cols].astype(BF16)


def halves(ref, half, swapped):
    return (ref.at[half:2 * half], ref.at[0:half]) if swapped else (ref.at[0:half], ref.at[half:2 * half])


def early_kernel(depth, mine_ref, own_ref, left_ref, right_ref, acc_ref):
    width, full = acc_ref.shape[0], own_ref.shape[0] // 2
    half, lanes = width // 2, acc_ref.shape[1] // 2
    sides = [halves(mine_ref, half, True), halves(left_ref, half, True), halves(right_ref, half, False)]
    for r in range(2):
        lhs = jnp.concatenate([side[r][:, :depth] for side in sides], axis=1)
        for z in range(2):
            rhs = [own_ref[z * full:z * full + depth, :]]
            at = width + (1 + z) * full
            rhs = jnp.concatenate(rhs + [ref[at:at + depth, :] for ref in (left_ref, right_ref)], axis=0)
            acc_ref[r * half:(r + 1) * half, z * lanes:(z + 1) * lanes] = jnp.dot(lhs, rhs, preferred_element_type=F32)


def late_kernel(depth, acc_ref, mine_ref, own_ref, left_ref, right_ref, upper_ref, lower_ref, chain_ref, keep_ref, *rest):
    sends, sum_ref, last_ref = rest[:-2], rest[-2], rest[-1]
    width, full = acc_ref.shape[0], own_ref.shape[0] // 2
    half, lanes, rows = width // 2, acc_ref.shape[1] // 2, own_ref.shape[0] // 2 - depth
    tensor = lax.axis_index("z_lo")
    far = (upper_ref, lower_ref)
    for z in range(2):
        at = width + (1 + z) * full
        given = [own_ref[z * full + depth:(z + 1) * full, :], left_ref[at + depth:at + full, :],
                 far[z][half + depth:half + full, :], right_ref[at + depth:at + full, :]]
        for b in range(RING):
            z_at = lax.rem(lax.axis_index("z_hi") + z, 2)
            y_at = lax.rem(lax.axis_index("y") + b, RING)
            turn = lax.rem(tensor - (z_at * 2 + lax.div(y_at, 2)) + RING, RING)
            inner = pl.multiple_of(lax.rem(y_at, 2) * LANES, LANES)
            cols = slice(b * LANES, (b + 1) * LANES)
            for p in range(RING):
                chained = chain_ref[turn, p * rows:(p + 1) * rows, pl.ds(inner, LANES)]
                last_ref[z, p * rows:(p + 1) * rows, cols] = jnp.where(on_last(), given[p][:, cols], chained)
    mine, left, right = halves(mine_ref, half, True), halves(left_ref, half, True), halves(right_ref, half, False)
    largest = jnp.full((1, lanes), TINY, F32)
    for r in range(2):
        lhs = [mine[r][:, depth:], left[r][:, depth:], far[r][:half, depth:], right[r][:, depth:], far[r][:half, :depth]]
        lhs = jnp.concatenate(lhs, axis=1)
        for z in range(2):
            rhs = jnp.concatenate([last_ref[z], far[z][half:half + depth, :]], axis=0)
            total = acc_ref[r * half:(r + 1) * half, z * lanes:(z + 1) * lanes]
            total = total + jnp.dot(lhs, rhs, preferred_element_type=F32)
            largest = jnp.maximum(largest, jnp.max(jnp.abs(total), axis=0, keepdims=True))
            sum_ref[r * half:(r + 1) * half, z * lanes:(z + 1) * lanes] = total
    power = jnp.ceil(jnp.log2(jnp.max(largest, axis=1, keepdims=True))) - TOP
    power = jnp.broadcast_to(power, (1, LANES))
    factor = jnp.exp2(-power)
    for z in range(2):
        keep_ref[z * width:(z + 1) * width, :] = sum_ref[:, z * lanes:z * lanes + LANES]
        for b, out in enumerate(sends, 1):
            cols = slice(z * lanes + b * LANES, z * lanes + (b + 1) * LANES)
            out[z * width:(z + 1) * width, :] = sum_ref[:, cols] * factor
    for out in sends:
        out[2 * width:, :] = jnp.broadcast_to(power, (TAIL, LANES))


def combine_kernel(keep_ref, one_ref, two_ref, three_ref, near_ref, far_ref):
    rows = near_ref.shape[0]
    totals = []
    for z in range(2):
        total = keep_ref[z * rows:(z + 1) * rows, :]
        for ref in (one_ref, two_ref, three_ref):
            total = total + ref[z * rows:(z + 1) * rows, :] * jnp.exp2(ref[2 * rows:2 * rows + 1, :])
        totals.append(total)
    near_ref[...] = totals[0]
    largest = jnp.maximum(jnp.max(jnp.abs(totals[1]), axis=0, keepdims=True), TINY)
    power = jnp.ceil(jnp.log2(jnp.max(largest, axis=1, keepdims=True))) - TOP
    power = jnp.broadcast_to(power, (1, LANES))
    far_ref[:rows, :] = totals[1] * jnp.exp2(-power)
    far_ref[rows:, :] = jnp.broadcast_to(power, (TAIL, LANES))


def second_kernel(own_ref, near_ref, far_ref, first_ref, weight_ref, out_ref, whole_ref, weight_in, sems):
    rows, size = out_ref.shape[0], own_ref.shape[0]
    parts, share = weight_in.shape[:2]
    copies = [pltpu.make_async_copy(weight_ref.at[pl.ds(i * share, share)], weight_in.at[i], sems.at[i]) for i in range(parts)]
    for copy in copies:
        copy.start()
    for j in range(RING):
        ref, base = ((own_ref, 0), (near_ref, 0), (far_ref, 0), (far_ref, size))[j]
        owner = jnp.bitwise_xor(lax.axis_index("z_lo"), j)
        for p in range(RING):
            x_at = lax.rem(lax.axis_index("x") + p, RING)
            for inner in range(2):
                at = pl.multiple_of(((owner * 2 + inner) * RING + x_at) * LANES, LANES)
                piece = ref[base + p * rows:base + (p + 1) * rows, inner * LANES:(inner + 1) * LANES]
                whole_ref[:, pl.ds(at, LANES)] = piece
    for i in range(parts):
        copies[i].wait()
        out = lax.dot_general(whole_ref[...], weight_in[i], CONTRACT_LAST, preferred_element_type=F32)
        cols = slice(i * share, (i + 1) * share)
        out_ref[:, cols] = jnp.where(on_last(), first_ref[:, cols], out)


def on_first(value, axis, by):
    return lax.ppermute(value, ("section", axis), [(i, (i + by) % RING) for i in range(RING)])


def swapped(value, bit):
    return lax.ppermute(value, ("section", "z_lo"), [(i, i ^ bit) for i in range(RING)])


def local(weights, stash_in, stash_grad, head_grad, pending):
    inputs, grads = stash_in[0], stash_grad[0]
    micro, rows, width = inputs.shape
    full, depth, half, lanes = micro * rows, (micro - 1) * rows, width // 2, RING * LANES
    columns = head_grad.shape[1]
    hbm = pl.BlockSpec(memory_space=pltpu.HBM)

    held = [pltpu.VMEM((4, width // 4, columns), BF16), pltpu.SemaphoreType.DMA((micro + 6,))]
    matmul = dict(flops=2 * rows * width * columns, moved=10 * 2**20)
    side = ((width + 3 * full, lanes), BF16)
    right, left, own, first, pieces = call(
        entry_kernel, [side, side, ((2 * full, lanes), BF16), ((rows, width), F32), ((full, 2 * LANES), BF16)],
        [in_hbm(v) for v in (pending, inputs, grads, head_grad, weights[0])], [hbm] * 5,
        scratch=[pltpu.VMEM(inputs.shape, BF16), pltpu.VMEM(grads.shape, BF16), pltpu.VMEM(head_grad.shape, BF16)] + held
        + [pltpu.SMEM(pending.shape, pending.dtype)],
        limit=ENTRY_LIMIT, **matmul,
    )
    from_left, from_right = shifted(right, True, 1), shifted(left, True, -1)

    pieces = lax.ppermute(pieces, "section", [(1, 0)])
    gathered = [pieces[:rows]]
    for by in range(1, RING):
        gathered.append(on_first(pieces[by * rows:(by + 1) * rows], "x", by))
    gathered = jnp.concatenate(gathered, 0)
    chain = [gathered] + [on_first(gathered, "z_lo", by) for by in range(1, RING)]
    from_left, from_right, *chain = lax.optimization_barrier((from_left, from_right, *chain))

    upper = shifted(from_left[half:width + full], True, 1)
    lower = shifted(from_right[half:width + full], True, -1)
    (acc,) = call(
        functools.partial(early_kernel, depth), [((width, 2 * lanes), F32)], (right, own, from_left, from_right), whole(4),
        flops=2 * width * 2 * lanes * 3 * depth, moved=12 * 2**20,
    )
    acc, pieces, *chain = lax.optimization_barrier((acc, pieces, *chain))
    near_pieces = swapped(pieces, 1)
    far_pieces = swapped(jnp.concatenate([pieces, near_pieces], 0), 2)
    send = ((2 * width + TAIL, LANES), F32)
    keep, *sends = call(
        functools.partial(late_kernel, depth), [((2 * width, LANES), F32)] + [send] * 3,
        (acc, right, own, from_left, from_right, upper, lower, jnp.stack(chain, 0)), whole(8),
        scratch=[pltpu.VMEM((width, 2 * lanes), F32), pltpu.VMEM((2, full, lanes), BF16)],
        flops=2 * width * 2 * lanes * (3 * rows + full), moved=12 * 2**20,
    )
    got = [shifted(s.astype(F16), False, by).astype(F32) for by, s in enumerate(sends, 1)]
    near, far = call(
        combine_kernel, [((width, LANES), F32), ((width + TAIL, LANES), F32)], (keep, *got), whole(4), moved=6 * 2**20,
    )
    far = far.astype(F16)
    far, pieces, near_pieces, far_pieces = lax.optimization_barrier((far, pieces, near_pieces, far_pieces))
    other = lax.ppermute(far, "z_hi", [(0, 1), (1, 0)])
    (second,) = call(
        second_kernel, [((rows, width), F32)], (pieces, near_pieces, far_pieces, first, in_hbm(weights[0])), whole(4) + [hbm],
        scratch=[pltpu.VMEM((rows, columns), BF16)] + held, limit=SECOND_LIMIT, **matmul,
    )
    block = near + other[:width].astype(F32) * jnp.exp2(other[width:width + 1].astype(F32))
    return (second[None], block[None])


def solution(mesh):
    fine = Mesh(mesh.devices.reshape(2, 4, 2, 4, 4), ("section", "z_lo", "z_hi", "y", "x"))
    dp = ("z_hi", "y", "x")
    return jax.shard_map(
        local,
        mesh=fine,
        in_specs=(
            P("section", "z_lo", None),
            P("section", None, dp, "z_lo"),
            P("section", None, dp, None),
            P(dp, None),
            P(),
        ),
        out_specs=(P("section", dp, "z_lo"), P("section", "z_lo", dp)),
        check_vma=False,
    )
```

```python
import functools

import jax
import jax.numpy as jnp
from jax import lax
from jax.experimental import pallas as pl
from jax.experimental.pallas import tpu as pltpu
from jax.sharding import Mesh
from jax.sharding import PartitionSpec as P

F32 = jnp.float32
F16 = jnp.float16
BF16 = jnp.bfloat16
RING = 4
LANES = 128
TAIL = 16
TOP = 15
TINY = 1e-30
ENTRY_LIMIT = 26


def section():
    return lax.axis_index("section")


def on_last():
    return section() == lax.axis_size("section") - 1


def block_start(z_off, along, across):
    first = section() == 0
    y_off, x_off = jnp.where(first, across, along), jnp.where(first, along, across)
    z = lax.rem(lax.axis_index("z_hi") + z_off, 2)
    y = lax.rem(lax.axis_index("y") + y_off, RING)
    x = lax.rem(lax.axis_index("x") + x_off, RING)
    return pl.multiple_of((z * (RING * RING) + y * RING + x) * LANES, LANES)


def pairs_over(along, by):
    size, pairs = RING * RING, []
    for s in range(2):
        for y in range(RING):
            for x in range(RING):
                on_x = (s == 0) == along
                there = (y, (x + by) % RING) if on_x else ((y + by) % RING, x)
                pairs.append((s * size + y * RING + x, s * size + there[0] * RING + there[1]))
    return pairs


def shifted(value, along, by):
    return lax.ppermute(value, ("section", "y", "x"), pairs_over(along, by))


def whole(n=1):
    return [pl.BlockSpec(memory_space=pltpu.VMEM)] * n


def in_hbm(value):
    return pltpu.with_memory_space_constraint(value, pltpu.HBM)


def call(kernel, out_shapes, operands, specs, scratch=(), flops=0, moved=0, limit=20):
    return pl.pallas_call(
        kernel,
        out_shape=[jax.ShapeDtypeStruct(s, t) for s, t in out_shapes],
        in_specs=specs,
        out_specs=whole(len(out_shapes)),
        scratch_shapes=list(scratch),
        compiler_params=pltpu.CompilerParams(vmem_limit_bytes=limit * 2**20),
        cost_estimate=pl.CostEstimate(flops=flops, bytes_accessed=moved, transcendentals=0),
    )(*operands)


CONTRACT_LAST = (((1,), (1,)), ((), ()))


def entry_kernel(pending_ref, x_ref, stash_ref, head_ref, weight_ref, right_ref, left_ref, own_ref, head_out, weight_out,
                 x_in, stash_in, count_in, sems):
    micro, rows, width = x_ref.shape
    half, depth = width // 2, (micro - 1) * rows
    pieces = [(pending_ref, count_in), (x_ref, x_in)]
    pieces += [(stash_ref.at[m], stash_in.at[m]) for m in range(micro - 1)]
    pieces += [(head_ref, head_out)]
    parts = 4
    share = width // parts
    pieces += [(weight_ref.at[pl.ds(i * share, share)], weight_out.at[pl.ds(i * share, share)]) for i in range(parts)]
    copies = [pltpu.make_async_copy(a, b, sems.at[i]) for i, (a, b) in enumerate(pieces)]
    for copy in copies:
        copy.start()
    copies[0].wait()
    copies[1].wait()
    count = count_in[section()]
    for m in range(micro):
        turned = jnp.where(m >= micro - count, x_in[m].astype(F32), 0.0).T.astype(BF16)
        lanes = slice(m * rows, (m + 1) * rows)
        for out, order in ((right_ref, (half, 0)), (left_ref, (0, half))):
            for at, top in zip((0, half), order):
                out[at:at + half, lanes] = turned[top:top + half]
    plans = [(right_ref, width, 0, 2), (left_ref, width, 1, 2)]
    for z in range(2):
        at = width + (1 + z) * depth
        plans += [(right_ref, at, z, 1), (left_ref, at, z, RING - 1), (own_ref, z * depth, z, 0)]
    for m in range(micro - 1):
        copies[2 + m].wait()
        for out, base, z, along in plans:
            for b in range(RING):
                top = base + m * rows
                source = stash_in[m, :, pl.ds(block_start(z, along, b), LANES)]
                out[top:top + rows, b * LANES:(b + 1) * LANES] = source
    for copy in copies[1 + micro:]:
        copy.wait()


def first_kernel(grad_ref, weight_ref, out_ref, small_ref):
    step = 256
    for i in range(0, weight_ref.shape[0], step):
        out = lax.dot_general(grad_ref[...], weight_ref[i:i + step, :], CONTRACT_LAST, preferred_element_type=F32)
        out_ref[:, i:i + step] = out
        small_ref[:, i:i + step] = out.astype(BF16)


def second_kernel(rel_ref, first_ref, weight_ref, out_ref):
    step, share = 256, rel_ref.shape[2]
    tensor = lax.axis_index("z_lo")
    for i in range(0, weight_ref.shape[0], step):
        total = jnp.zeros((rel_ref.shape[1], step), F32)
        for k in range(RING):
            owner = lax.rem(tensor - k + RING, RING)
            cols = weight_ref[i:i + step, pl.ds(pl.multiple_of(owner * share, share), share)]
            total = total + lax.dot_general(rel_ref[k], cols, CONTRACT_LAST, preferred_element_type=F32)
        out_ref[:, i:i + step] = jnp.where(on_last(), first_ref[:, i:i + step], total)


def pack_last_kernel(head_ref, rel_ref, right_ref, left_ref, own_ref, far_ref):
    tensor = lax.axis_index("z_lo")
    rows, share = rel_ref.shape[1], rel_ref.shape[2]
    for z in range(2):
        for b in range(RING):
            for out, along in ((right_ref, 1), (left_ref, RING - 1), (own_ref, 0), (far_ref, 2)):
                at = block_start(z, along, b)
                inner = pl.multiple_of(lax.rem(at, share), LANES)
                chained = rel_ref[lax.rem(tensor - lax.div(at, share) + RING, RING), :, pl.ds(inner, LANES)]
                last = jnp.where(on_last(), head_ref[:, pl.ds(at, LANES)], chained)
                out[z * rows:(z + 1) * rows, b * LANES:(b + 1) * LANES] = last


def halves(ref, half, swapped):
    return (ref.at[half:2 * half], ref.at[0:half]) if swapped else (ref.at[0:half], ref.at[half:2 * half])


def early_kernel(mine_ref, own_ref, left_ref, right_ref, acc_ref):
    width, depth = acc_ref.shape[0], own_ref.shape[0] // 2
    half, lanes = width // 2, acc_ref.shape[1] // 2
    sides = [halves(mine_ref, half, True), halves(left_ref, half, True), halves(right_ref, half, False)]
    for r in range(2):
        lhs = jnp.concatenate([side[r][:, :depth] for side in sides], axis=1)
        for z in range(2):
            at = width + (1 + z) * depth
            rhs = [own_ref[z * depth:(z + 1) * depth, :], left_ref[at:at + depth, :], right_ref[at:at + depth, :]]
            rhs = jnp.concatenate(rhs, axis=0)
            acc_ref[r * half:(r + 1) * half, z * lanes:(z + 1) * lanes] = jnp.dot(lhs, rhs, preferred_element_type=F32)


def late_kernel(acc_ref, mine_ref, left_ref, right_ref, upper_ref, lower_ref, own_last, left_last, right_last, far_last,
                keep_far, keep_near, *rest):
    sends, sum_ref = rest[:-1], rest[-1]
    width, rows = acc_ref.shape[0], own_last.shape[0] // 2
    half, lanes = width // 2, acc_ref.shape[1] // 2
    depth = mine_ref.shape[1] - rows
    mine, left, right = halves(mine_ref, half, True), halves(left_ref, half, True), halves(right_ref, half, False)
    far = (upper_ref, lower_ref)
    largest = jnp.full((1, lanes), TINY, F32)
    for r in range(2):
        lhs = [mine[r][:, depth:], left[r][:, depth:], right[r][:, depth:], far[r][:half, depth:], far[r][:half, :depth]]
        lhs = jnp.concatenate(lhs, axis=1)
        for z in range(2):
            rhs = [ref[z * rows:(z + 1) * rows, :] for ref in (own_last, left_last, right_last, far_last)]
            rhs = jnp.concatenate(rhs + [far[z][half:, :]], axis=0)
            total = acc_ref[r * half:(r + 1) * half, z * lanes:(z + 1) * lanes]
            total = total + jnp.dot(lhs, rhs, preferred_element_type=F32)
            largest = jnp.maximum(largest, jnp.max(jnp.abs(total), axis=0, keepdims=True))
            sum_ref[r * half:(r + 1) * half, z * lanes:(z + 1) * lanes] = total
    power = jnp.ceil(jnp.log2(jnp.max(largest, axis=1, keepdims=True))) - TOP
    power = jnp.broadcast_to(power, (1, LANES))
    factor = jnp.exp2(-power)
    for z, keep, outs in ((1, keep_far, sends[:RING - 1]), (0, keep_near, sends[RING - 1:])):
        keep[...] = sum_ref[:, z * lanes:z * lanes + LANES]
        for b, out in enumerate(outs, 1):
            cols = slice(z * lanes + b * LANES, z * lanes + (b + 1) * LANES)
            out[:width, :] = sum_ref[:, cols] * factor
            out[width:, :] = jnp.broadcast_to(power, (TAIL, LANES))


def summed(keep_ref, refs):
    rows = keep_ref.shape[0]
    total = keep_ref[...]
    for ref in refs:
        total = total + ref[:rows, :] * jnp.exp2(ref[rows:rows + 1, :])
    return total


def far_kernel(keep_ref, one_ref, two_ref, three_ref, out_ref):
    rows = keep_ref.shape[0]
    total = summed(keep_ref, (one_ref, two_ref, three_ref))
    largest = jnp.maximum(jnp.max(jnp.abs(total), axis=0, keepdims=True), TINY)
    power = jnp.ceil(jnp.log2(jnp.max(largest, axis=1, keepdims=True))) - TOP
    power = jnp.broadcast_to(power, (1, LANES))
    out_ref[:rows, :] = total * jnp.exp2(-power)
    out_ref[rows:, :] = jnp.broadcast_to(power, (TAIL, LANES))


def near_kernel(keep_ref, one_ref, two_ref, three_ref, other_ref, out_ref):
    out_ref[...] = summed(keep_ref, (one_ref, two_ref, three_ref, other_ref))


def on_first(value, by):
    return lax.ppermute(value, ("section", "z_lo"), [(i, (i + by) % RING) for i in range(RING)])


def local(weights, stash_in, stash_grad, head_grad, pending):
    inputs, grads = stash_in[0], stash_grad[0]
    micro, rows, width = inputs.shape
    depth, half, lanes = (micro - 1) * rows, width // 2, RING * LANES
    columns = head_grad.shape[1]
    matmul = dict(flops=2 * rows * width * columns, moved=2 * 2**20)

    side = ((width + 3 * depth, lanes), BF16)
    right, left, own, head, weight = call(
        entry_kernel, [side, side, ((2 * depth, lanes), BF16), (head_grad.shape, BF16), ((width, columns), BF16)],
        [in_hbm(v) for v in (pending, inputs, grads, head_grad, weights[0])], [pl.BlockSpec(memory_space=pltpu.HBM)] * 5,
        scratch=[pltpu.VMEM(inputs.shape, BF16), pltpu.VMEM(grads.shape, BF16), pltpu.SMEM(pending.shape, pending.dtype),
                 pltpu.SemaphoreType.DMA((micro + 6,))],
        moved=13 * 2**20, limit=ENTRY_LIMIT,
    )
    from_left, from_right = shifted(right, True, 1), shifted(left, True, -1)

    first, small = call(first_kernel, [((rows, width), F32), ((rows, width), BF16)], (head, weight), whole(2), **matmul)
    shard = lax.ppermute(small, "section", [(1, 0)])
    rel = [shard] + [on_first(shard, by) for by in range(1, RING)]
    from_left, from_right, *rel = lax.optimization_barrier((from_left, from_right, *rel))
    rel = jnp.stack(rel, 0)

    upper = shifted(from_left[half:width + depth], True, 1)
    lower = shifted(from_right[half:width + depth], True, -1)
    edge = ((2 * rows, lanes), BF16)
    last_right, last_left, last_own, last_far = call(
        pack_last_kernel, [edge] * 4, (head, rel), whole(2), moved=4 * 2**20
    )
    last = [last_own, shifted(last_right, True, 1), shifted(last_left, True, -1), shifted(last_far, True, 2)]
    (acc,) = call(
        early_kernel, [((width, 2 * lanes), F32)], (right, own, from_left, from_right), whole(4),
        flops=2 * width * 2 * lanes * 3 * depth, moved=12 * 2**20,
    )
    send = ((width + TAIL, LANES), F32)
    keep_far, keep_near, *sends = call(
        late_kernel, [((width, LANES), F32)] * 2 + [send] * 6,
        (acc, right, from_left, from_right, upper, lower, *last), whole(10),
        scratch=[pltpu.VMEM((width, 2 * lanes), F32)],
        flops=2 * width * 2 * lanes * (3 * rows + micro * rows), moved=12 * 2**20,
    )
    keep_far, rel = lax.optimization_barrier((keep_far, rel))
    (second,) = call(second_kernel, [((rows, width), F32)], (rel, first, weights[0]), whole(3), **matmul)
    got = [shifted(s.astype(F16), False, by).astype(F32) for by, s in zip((1, 2, 3, 1, 2, 3), sends)]
    (far,) = call(far_kernel, [send], (keep_far, *got[:3]), whole(4), moved=4 * 2**20)
    other = lax.ppermute(far.astype(F16), "z_hi", [(0, 1), (1, 0)]).astype(F32)
    (block,) = call(near_kernel, [((width, LANES), F32)], (keep_near, *got[3:], other), whole(5), moved=4 * 2**20)
    return (second[None], block[None])


def solution(mesh):
    fine = Mesh(mesh.devices.reshape(2, 4, 2, 4, 4), ("section", "z_lo", "z_hi", "y", "x"))
    dp = ("z_hi", "y", "x")
    return jax.shard_map(
        local,
        mesh=fine,
        in_specs=(
            P("section", "z_lo", None),
            P("section", None, dp, "z_lo"),
            P("section", None, dp, None),
            P(dp, None),
            P(),
        ),
        out_specs=(P("section", dp, "z_lo"), P("section", "z_lo", dp)),
        check_vma=False,
    )
```

```python
import functools

import jax
import jax.numpy as jnp
from jax import lax
from jax.experimental import pallas as pl
from jax.experimental.pallas import tpu as pltpu
from jax.sharding import Mesh
from jax.sharding import PartitionSpec as P

F32 = jnp.float32
F16 = jnp.float16
BF16 = jnp.bfloat16
RING = 4
LANES = 128
TAIL = 16
TOP = 15
TINY = 1e-30
ENTRY_LIMIT = 26


def section():
    return lax.axis_index("section")


def on_last():
    return section() == lax.axis_size("section") - 1


def block_start(z_off, along, across):
    first = section() == 0
    y_off, x_off = jnp.where(first, across, along), jnp.where(first, along, across)
    z = lax.rem(lax.axis_index("z_hi") + z_off, 2)
    y = lax.rem(lax.axis_index("y") + y_off, RING)
    x = lax.rem(lax.axis_index("x") + x_off, RING)
    return pl.multiple_of((z * (RING * RING) + y * RING + x) * LANES, LANES)


def pairs_over(along, by):
    size, pairs = RING * RING, []
    for s in range(2):
        for y in range(RING):
            for x in range(RING):
                on_x = (s == 0) == along
                there = (y, (x + by) % RING) if on_x else ((y + by) % RING, x)
                pairs.append((s * size + y * RING + x, s * size + there[0] * RING + there[1]))
    return pairs


def shifted(value, along, by):
    return lax.ppermute(value, ("section", "y", "x"), pairs_over(along, by))


def whole(n=1):
    return [pl.BlockSpec(memory_space=pltpu.VMEM)] * n


def in_hbm(value):
    return pltpu.with_memory_space_constraint(value, pltpu.HBM)


def call(kernel, out_shapes, operands, specs, scratch=(), flops=0, moved=0, limit=20):
    return pl.pallas_call(
        kernel,
        out_shape=[jax.ShapeDtypeStruct(s, t) for s, t in out_shapes],
        in_specs=specs,
        out_specs=whole(len(out_shapes)),
        scratch_shapes=list(scratch),
        compiler_params=pltpu.CompilerParams(vmem_limit_bytes=limit * 2**20),
        cost_estimate=pl.CostEstimate(flops=flops, bytes_accessed=moved, transcendentals=0),
    )(*operands)


CONTRACT_LAST = (((1,), (1,)), ((), ()))


def entry_kernel(pending_ref, x_ref, stash_ref, head_ref, weight_ref, right_ref, left_ref, own_ref, two_ref, head_out,
                 weight_out, x_in, stash_in, count_in, sems):
    micro, rows, width = x_ref.shape
    half, depth = width // 2, (micro - 1) * rows
    pieces = [(pending_ref, count_in), (x_ref, x_in)]
    pieces += [(stash_ref.at[m], stash_in.at[m]) for m in range(micro - 1)]
    pieces += [(head_ref, head_out)]
    parts = 4
    share = width // parts
    pieces += [(weight_ref.at[pl.ds(i * share, share)], weight_out.at[pl.ds(i * share, share)]) for i in range(parts)]
    copies = [pltpu.make_async_copy(a, b, sems.at[i]) for i, (a, b) in enumerate(pieces)]
    for copy in copies:
        copy.start()
    copies[0].wait()
    copies[1].wait()
    count = count_in[section()]
    for m in range(micro):
        turned = jnp.where(m >= micro - count, x_in[m].astype(F32), 0.0).T.astype(BF16)
        lanes = slice(m * rows, (m + 1) * rows)
        for out, order in ((right_ref, (half, 0)), (left_ref, (0, half))):
            for at, top in zip((0, half), order):
                out[at:at + half, lanes] = turned[top:top + half]
    share = depth // 2
    plans = [(right_ref, width, 1, 2, 0, share), (left_ref, width, 1, 2, share, depth), (two_ref, 0, 0, 2, 0, depth)]
    for z in range(2):
        at = width + share + z * depth
        plans += [(right_ref, at, z, 1, 0, depth), (left_ref, at, z, RING - 1, 0, depth), (own_ref, z * depth, z, 0, 0, depth)]
    for m in range(micro - 1):
        copies[2 + m].wait()
        for out, base, z, along, begin, end in plans:
            begin_m, end_m = max(begin, m * rows), min(end, (m + 1) * rows)
            if begin_m >= end_m:
                continue
            for b in range(RING):
                source = stash_in[m, begin_m - m * rows:end_m - m * rows, pl.ds(block_start(z, along, b), LANES)]
                out[base + begin_m - begin:base + end_m - begin, b * LANES:(b + 1) * LANES] = source
    for copy in copies[1 + micro:]:
        copy.wait()


def first_kernel(grad_ref, weight_ref, out_ref, small_ref):
    step = 256
    for i in range(0, weight_ref.shape[0], step):
        out = lax.dot_general(grad_ref[...], weight_ref[i:i + step, :], CONTRACT_LAST, preferred_element_type=F32)
        out_ref[:, i:i + step] = out
        small_ref[:, i:i + step] = out.astype(BF16)


def second_kernel(rel_ref, first_ref, weight_ref, out_ref):
    step, share = 256, rel_ref.shape[2]
    tensor = lax.axis_index("z_lo")
    for i in range(0, weight_ref.shape[0], step):
        total = jnp.zeros((rel_ref.shape[1], step), F32)
        for k in range(RING):
            owner = lax.rem(tensor - k + RING, RING)
            cols = weight_ref[i:i + step, pl.ds(pl.multiple_of(owner * share, share), share)]
            total = total + lax.dot_general(rel_ref[k], cols, CONTRACT_LAST, preferred_element_type=F32)
        out_ref[:, i:i + step] = jnp.where(on_last(), first_ref[:, i:i + step], total)


def pack_last_kernel(head_ref, rel_ref, two_ref, right_ref, left_ref, own_ref, far_ref, direct_ref):
    tensor = lax.axis_index("z_lo")
    rows, share = rel_ref.shape[1], rel_ref.shape[2]
    depth = two_ref.shape[0]
    direct_ref[:depth, :] = two_ref[...]
    for z in range(2):
        for b in range(RING):
            two, base = ((direct_ref, depth), (far_ref, 0))[z]
            for out, top, along in ((right_ref, z * rows, 1), (left_ref, z * rows, RING - 1), (own_ref, z * rows, 0), (two, base, 2)):
                at = block_start(z, along, b)
                inner = pl.multiple_of(lax.rem(at, share), LANES)
                chained = rel_ref[lax.rem(tensor - lax.div(at, share) + RING, RING), :, pl.ds(inner, LANES)]
                last = jnp.where(on_last(), head_ref[:, pl.ds(at, LANES)], chained)
                out[top:top + rows, b * LANES:(b + 1) * LANES] = last


def halves(ref, half, swapped):
    return (ref.at[half:2 * half], ref.at[0:half]) if swapped else (ref.at[0:half], ref.at[half:2 * half])


def early_kernel(mine_ref, own_ref, left_ref, right_ref, acc_ref):
    width, depth = acc_ref.shape[0], own_ref.shape[0] // 2
    half, lanes = width // 2, acc_ref.shape[1] // 2
    sides = [halves(mine_ref, half, True), halves(left_ref, half, True), halves(right_ref, half, False)]
    for r in range(2):
        lhs = jnp.concatenate([side[r][:, :depth] for side in sides], axis=1)
        for z in range(2):
            at = width + depth // 2 + z * depth
            rhs = [own_ref[z * depth:(z + 1) * depth, :], left_ref[at:at + depth, :], right_ref[at:at + depth, :]]
            rhs = jnp.concatenate(rhs, axis=0)
            acc_ref[r * half:(r + 1) * half, z * lanes:(z + 1) * lanes] = jnp.dot(lhs, rhs, preferred_element_type=F32)


def late_kernel(z, acc_ref, mine_ref, left_ref, right_ref, upper_ref, lower_ref, own_last, left_last, right_last, two_ref,
                keep_ref, *rest):
    sends, sum_ref = rest[:-1], rest[-1]
    width, rows = acc_ref.shape[0], own_last.shape[0] // 2
    half, lanes = width // 2, acc_ref.shape[1] // 2
    depth = mine_ref.shape[1] - rows
    mine, left, right = halves(mine_ref, half, True), halves(left_ref, half, True), halves(right_ref, half, False)
    far = (upper_ref, lower_ref)
    rhs = [ref[z * rows:(z + 1) * rows, :] for ref in (own_last, left_last, right_last)]
    if z:
        rhs += [two_ref[...], upper_ref[half:, :], lower_ref[half:, :]]
    else:
        rhs += [two_ref[depth:, :], two_ref[:depth, :]]
    rhs = jnp.concatenate(rhs, axis=0)
    largest = jnp.full((1, lanes), TINY, F32)
    for r in range(2):
        lhs = [mine[r][:, depth:], left[r][:, depth:], right[r][:, depth:], far[r][:half, depth:], far[r][:half, :depth]]
        total = jnp.dot(jnp.concatenate(lhs, axis=1), rhs, preferred_element_type=F32)
        total = total + acc_ref[r * half:(r + 1) * half, z * lanes:(z + 1) * lanes]
        largest = jnp.maximum(largest, jnp.max(jnp.abs(total), axis=0, keepdims=True))
        sum_ref[r * half:(r + 1) * half, :] = total
    power = jnp.ceil(jnp.log2(jnp.max(largest, axis=1, keepdims=True))) - TOP
    power = jnp.broadcast_to(power, (1, LANES))
    factor = jnp.exp2(-power)
    keep_ref[...] = sum_ref[:, :LANES]
    for b, out in enumerate(sends, 1):
        out[:width, :] = sum_ref[:, b * LANES:(b + 1) * LANES] * factor
        out[width:, :] = jnp.broadcast_to(power, (TAIL, LANES))


def summed(keep_ref, refs):
    rows = keep_ref.shape[0]
    total = keep_ref[...]
    for ref in refs:
        total = total + ref[:rows, :] * jnp.exp2(ref[rows:rows + 1, :])
    return total


def far_kernel(keep_ref, one_ref, two_ref, three_ref, out_ref):
    rows = keep_ref.shape[0]
    total = summed(keep_ref, (one_ref, two_ref, three_ref))
    largest = jnp.maximum(jnp.max(jnp.abs(total), axis=0, keepdims=True), TINY)
    power = jnp.ceil(jnp.log2(jnp.max(largest, axis=1, keepdims=True))) - TOP
    power = jnp.broadcast_to(power, (1, LANES))
    out_ref[:rows, :] = total * jnp.exp2(-power)
    out_ref[rows:, :] = jnp.broadcast_to(power, (TAIL, LANES))


def near_kernel(keep_ref, one_ref, two_ref, three_ref, other_ref, out_ref):
    out_ref[...] = summed(keep_ref, (one_ref, two_ref, three_ref, other_ref))


def on_first(value, by):
    return lax.ppermute(value, ("section", "z_lo"), [(i, (i + by) % RING) for i in range(RING)])


def local(weights, stash_in, stash_grad, head_grad, pending):
    inputs, grads = stash_in[0], stash_grad[0]
    micro, rows, width = inputs.shape
    depth, half, lanes = (micro - 1) * rows, width // 2, RING * LANES
    columns = head_grad.shape[1]
    matmul = dict(flops=2 * rows * width * columns, moved=2 * 2**20)

    side = ((width + depth // 2 + 2 * depth, lanes), BF16)
    right, left, own, two, head, weight = call(
        entry_kernel,
        [side, side, ((2 * depth, lanes), BF16), ((depth, lanes), BF16), (head_grad.shape, BF16), ((width, columns), BF16)],
        [in_hbm(v) for v in (pending, inputs, grads, head_grad, weights[0])], [pl.BlockSpec(memory_space=pltpu.HBM)] * 5,
        scratch=[pltpu.VMEM(inputs.shape, BF16), pltpu.VMEM(grads.shape, BF16), pltpu.SMEM(pending.shape, pending.dtype),
                 pltpu.SemaphoreType.DMA((micro + 6,))],
        moved=13 * 2**20, limit=ENTRY_LIMIT,
    )
    from_left, from_right = shifted(right, True, 1), shifted(left, True, -1)

    first, small = call(first_kernel, [((rows, width), F32), ((rows, width), BF16)], (head, weight), whole(2), **matmul)
    shard = lax.ppermute(small, "section", [(1, 0)])
    rel = [shard] + [on_first(shard, by) for by in range(1, RING)]
    from_left, from_right, *rel = lax.optimization_barrier((from_left, from_right, *rel))
    rel = jnp.stack(rel, 0)

    passed = half + depth // 2
    upper = shifted(from_left[half:half + passed], True, 1)
    lower = shifted(from_right[half:half + passed], True, -1)
    edge = ((2 * rows, lanes), BF16)
    last_right, last_left, last_own, last_far, direct = call(
        pack_last_kernel, [edge] * 3 + [((rows, lanes), BF16), ((micro * rows, lanes), BF16)], (head, rel, two), whole(3),
        moved=4 * 2**20,
    )
    last = [last_own, shifted(last_right, True, 1), shifted(last_left, True, -1)]
    last_far = shifted(last_far, True, 2)
    (acc,) = call(
        early_kernel, [((width, 2 * lanes), F32)], (right, own, from_left, from_right), whole(4),
        flops=2 * width * 2 * lanes * 3 * depth, moved=12 * 2**20,
    )
    upper, lower, direct = lax.optimization_barrier((upper, lower, direct))
    direct = shifted(direct, True, 2)
    send = ((width + TAIL, LANES), F32)

    def late(z, two):
        return call(
            functools.partial(late_kernel, z), [((width, LANES), F32)] + [send] * 3,
            (acc, right, from_left, from_right, upper, lower, *last, two), whole(10),
            scratch=[pltpu.VMEM((width, lanes), F32)],
            flops=2 * width * lanes * (3 * rows + micro * rows), moved=8 * 2**20,
        )

    keep_far, *far_sends = late(1, last_far)
    keep_near, *near_sends = late(0, direct)
    sends = far_sends + near_sends
    keep_far, keep_near, rel = lax.optimization_barrier((keep_far, keep_near, rel))
    (second,) = call(second_kernel, [((rows, width), F32)], (rel, first, weights[0]), whole(3), **matmul)
    got = [shifted(s.astype(F16), False, by).astype(F32) for by, s in zip((1, 2, 3, 1, 2, 3), sends)]
    (far,) = call(far_kernel, [send], (keep_far, *got[:3]), whole(4), moved=4 * 2**20)
    other = lax.ppermute(far.astype(F16), "z_hi", [(0, 1), (1, 0)]).astype(F32)
    (block,) = call(near_kernel, [((width, LANES), F32)], (keep_near, *got[3:], other), whole(5), moved=4 * 2**20)
    return (second[None], block[None])


def solution(mesh):
    fine = Mesh(mesh.devices.reshape(2, 4, 2, 4, 4), ("section", "z_lo", "z_hi", "y", "x"))
    dp = ("z_hi", "y", "x")
    return jax.shard_map(
        local,
        mesh=fine,
        in_specs=(
            P("section", "z_lo", None),
            P("section", None, dp, "z_lo"),
            P("section", None, dp, None),
            P(dp, None),
            P(),
        ),
        out_specs=(P("section", dp, "z_lo"), P("section", "z_lo", dp)),
        check_vma=False,
    )
```

```python
import functools

import jax
import jax.numpy as jnp
from jax import lax
from jax.experimental import pallas as pl
from jax.experimental.pallas import tpu as pltpu
from jax.sharding import Mesh
from jax.sharding import PartitionSpec as P

F32 = jnp.float32
F16 = jnp.float16
BF16 = jnp.bfloat16
RING = 4
LANES = 128
TAIL = 16
TOP = 15
TINY = 1e-30
ENTRY_LIMIT = 26
ENTRY_FLOPS = 10**10


def section():
    return lax.axis_index("section")


def on_last():
    return section() == lax.axis_size("section") - 1


def block_start(z_off, along, across):
    first = section() == 0
    y_off, x_off = jnp.where(first, across, along), jnp.where(first, along, across)
    z = lax.rem(lax.axis_index("z_hi") + z_off, 2)
    y = lax.rem(lax.axis_index("y") + y_off, RING)
    x = lax.rem(lax.axis_index("x") + x_off, RING)
    return pl.multiple_of((z * (RING * RING) + y * RING + x) * LANES, LANES)


def pairs_over(along, by):
    size, pairs = RING * RING, []
    for s in range(2):
        for y in range(RING):
            for x in range(RING):
                on_x = (s == 0) == along
                there = (y, (x + by) % RING) if on_x else ((y + by) % RING, x)
                pairs.append((s * size + y * RING + x, s * size + there[0] * RING + there[1]))
    return pairs


def shifted(value, along, by):
    return lax.ppermute(value, ("section", "y", "x"), pairs_over(along, by))


def whole(n=1):
    return [pl.BlockSpec(memory_space=pltpu.VMEM)] * n


def in_hbm(value):
    return pltpu.with_memory_space_constraint(value, pltpu.HBM)


def call(kernel, out_shapes, operands, specs, scratch=(), flops=0, moved=0, limit=20):
    return pl.pallas_call(
        kernel,
        out_shape=[jax.ShapeDtypeStruct(s, t) for s, t in out_shapes],
        in_specs=specs,
        out_specs=whole(len(out_shapes)),
        scratch_shapes=list(scratch),
        compiler_params=pltpu.CompilerParams(vmem_limit_bytes=limit * 2**20),
        cost_estimate=pl.CostEstimate(flops=flops, bytes_accessed=moved, transcendentals=0),
    )(*operands)


CONTRACT_LAST = (((1,), (1,)), ((), ()))


def entry_kernel(pending_ref, x_ref, stash_ref, right_ref, left_ref, own_ref, two_ref, x_in, stash_in, count_in, sems):
    micro, rows, width = x_ref.shape
    half, depth = width // 2, (micro - 1) * rows
    pieces = [(pending_ref, count_in), (x_ref, x_in)]
    pieces += [(stash_ref.at[m], stash_in.at[m]) for m in range(micro - 1)]
    copies = [pltpu.make_async_copy(a, b, sems.at[i]) for i, (a, b) in enumerate(pieces)]
    for copy in copies:
        copy.start()
    copies[0].wait()
    copies[1].wait()
    count = count_in[section()]
    for m in range(micro):
        turned = jnp.where(m >= micro - count, x_in[m].astype(F32), 0.0).T.astype(BF16)
        lanes = slice(m * rows, (m + 1) * rows)
        for out, order in ((right_ref, (half, 0)), (left_ref, (0, half))):
            for at, top in zip((0, half), order):
                out[at:at + half, lanes] = turned[top:top + half]
    share = depth // 2
    plans = [(right_ref, width, 1, 2, 0, share), (left_ref, width, 1, 2, share, depth), (two_ref, 0, 0, 2, 0, depth)]
    for z in range(2):
        at = width + share + z * depth
        plans += [(right_ref, at, z, 1, 0, depth), (left_ref, at, z, RING - 1, 0, depth), (own_ref, z * depth, z, 0, 0, depth)]
    for m in range(micro - 1):
        copies[2 + m].wait()
        for out, base, z, along, begin, end in plans:
            begin_m, end_m = max(begin, m * rows), min(end, (m + 1) * rows)
            if begin_m >= end_m:
                continue
            for b in range(RING):
                source = stash_in[m, begin_m - m * rows:end_m - m * rows, pl.ds(block_start(z, along, b), LANES)]
                out[base + begin_m - begin:base + end_m - begin, b * LANES:(b + 1) * LANES] = source


def first_kernel(grad_ref, weight_ref, out_ref, small_ref):
    step = 256
    for i in range(0, weight_ref.shape[0], step):
        out = lax.dot_general(grad_ref[...], weight_ref[i:i + step, :], CONTRACT_LAST, preferred_element_type=F32)
        out_ref[:, i:i + step] = out
        small_ref[:, i:i + step] = out.astype(BF16)


def second_kernel(rel_ref, first_ref, weight_ref, out_ref):
    step, share = 256, rel_ref.shape[2]
    tensor = lax.axis_index("z_lo")
    for i in range(0, weight_ref.shape[0], step):
        total = jnp.zeros((rel_ref.shape[1], step), F32)
        for k in range(RING):
            owner = lax.rem(tensor - k + RING, RING)
            cols = weight_ref[i:i + step, pl.ds(pl.multiple_of(owner * share, share), share)]
            total = total + lax.dot_general(rel_ref[k], cols, CONTRACT_LAST, preferred_element_type=F32)
        out_ref[:, i:i + step] = jnp.where(on_last(), first_ref[:, i:i + step], total)


def pack_last_kernel(head_ref, rel_ref, two_ref, right_ref, left_ref, own_ref, far_ref, direct_ref):
    tensor = lax.axis_index("z_lo")
    rows, share = rel_ref.shape[1], rel_ref.shape[2]
    depth = two_ref.shape[0]
    direct_ref[:depth, :] = two_ref[...]
    for z in range(2):
        for b in range(RING):
            two, base = ((direct_ref, depth), (far_ref, 0))[z]
            for out, top, along in ((right_ref, z * rows, 1), (left_ref, z * rows, RING - 1), (own_ref, z * rows, 0), (two, base, 2)):
                at = block_start(z, along, b)
                inner = pl.multiple_of(lax.rem(at, share), LANES)
                chained = rel_ref[lax.rem(tensor - lax.div(at, share) + RING, RING), :, pl.ds(inner, LANES)]
                last = jnp.where(on_last(), head_ref[:, pl.ds(at, LANES)], chained)
                out[top:top + rows, b * LANES:(b + 1) * LANES] = last


def halves(ref, half, swapped):
    return (ref.at[half:2 * half], ref.at[0:half]) if swapped else (ref.at[0:half], ref.at[half:2 * half])


def early_kernel(mine_ref, own_ref, left_ref, right_ref, acc_ref):
    width, depth = acc_ref.shape[0], own_ref.shape[0] // 2
    half, lanes = width // 2, acc_ref.shape[1] // 2
    sides = [halves(mine_ref, half, True), halves(left_ref, half, True), halves(right_ref, half, False)]
    for r in range(2):
        lhs = jnp.concatenate([side[r][:, :depth] for side in sides], axis=1)
        for z in range(2):
            at = width + depth // 2 + z * depth
            rhs = [own_ref[z * depth:(z + 1) * depth, :], left_ref[at:at + depth, :], right_ref[at:at + depth, :]]
            rhs = jnp.concatenate(rhs, axis=0)
            acc_ref[r * half:(r + 1) * half, z * lanes:(z + 1) * lanes] = jnp.dot(lhs, rhs, preferred_element_type=F32)


def late_kernel(z, acc_ref, mine_ref, left_ref, right_ref, upper_ref, lower_ref, own_last, left_last, right_last, two_ref,
                keep_ref, *rest):
    sends, sum_ref = rest[:-1], rest[-1]
    width, rows = acc_ref.shape[0], own_last.shape[0] // 2
    half, lanes = width // 2, acc_ref.shape[1] // 2
    depth = mine_ref.shape[1] - rows
    mine, left, right = halves(mine_ref, half, True), halves(left_ref, half, True), halves(right_ref, half, False)
    far = (upper_ref, lower_ref)
    rhs = [ref[z * rows:(z + 1) * rows, :] for ref in (own_last, left_last, right_last)]
    if z:
        rhs += [two_ref[...], upper_ref[half:, :], lower_ref[half:, :]]
    else:
        rhs += [two_ref[depth:, :], two_ref[:depth, :]]
    rhs = jnp.concatenate(rhs, axis=0)
    largest = jnp.full((1, lanes), TINY, F32)
    for r in range(2):
        lhs = [mine[r][:, depth:], left[r][:, depth:], right[r][:, depth:], far[r][:half, depth:], far[r][:half, :depth]]
        total = jnp.dot(jnp.concatenate(lhs, axis=1), rhs, preferred_element_type=F32)
        total = total + acc_ref[r * half:(r + 1) * half, z * lanes:(z + 1) * lanes]
        largest = jnp.maximum(largest, jnp.max(jnp.abs(total), axis=0, keepdims=True))
        sum_ref[r * half:(r + 1) * half, :] = total
    power = jnp.ceil(jnp.log2(jnp.max(largest, axis=1, keepdims=True))) - TOP
    power = jnp.broadcast_to(power, (1, LANES))
    factor = jnp.exp2(-power)
    keep_ref[...] = sum_ref[:, :LANES]
    for b, out in enumerate(sends, 1):
        out[:width, :] = sum_ref[:, b * LANES:(b + 1) * LANES] * factor
        out[width:, :] = jnp.broadcast_to(power, (TAIL, LANES))


def summed(keep_ref, refs):
    rows = keep_ref.shape[0]
    total = keep_ref[...]
    for ref in refs:
        total = total + ref[:rows, :] * jnp.exp2(ref[rows:rows + 1, :])
    return total


def far_kernel(keep_ref, one_ref, two_ref, three_ref, out_ref):
    rows = keep_ref.shape[0]
    total = summed(keep_ref, (one_ref, two_ref, three_ref))
    largest = jnp.maximum(jnp.max(jnp.abs(total), axis=0, keepdims=True), TINY)
    power = jnp.ceil(jnp.log2(jnp.max(largest, axis=1, keepdims=True))) - TOP
    power = jnp.broadcast_to(power, (1, LANES))
    out_ref[:rows, :] = total * jnp.exp2(-power)
    out_ref[rows:, :] = jnp.broadcast_to(power, (TAIL, LANES))


def near_kernel(keep_ref, one_ref, two_ref, three_ref, other_ref, out_ref):
    out_ref[...] = summed(keep_ref, (one_ref, two_ref, three_ref, other_ref))


def on_first(value, by):
    return lax.ppermute(value, ("section", "z_lo"), [(i, (i + by) % RING) for i in range(RING)])


def local(weights, stash_in, stash_grad, head_grad, pending):
    inputs, grads = stash_in[0], stash_grad[0]
    micro, rows, width = inputs.shape
    depth, half, lanes = (micro - 1) * rows, width // 2, RING * LANES
    columns = head_grad.shape[1]
    matmul = dict(flops=2 * rows * width * columns, moved=2 * 2**20)

    side = ((width + depth // 2 + 2 * depth, lanes), BF16)
    right, left, own, two = call(
        entry_kernel,
        [side, side, ((2 * depth, lanes), BF16), ((depth, lanes), BF16)],
        [in_hbm(v) for v in (pending, inputs, grads)], [pl.BlockSpec(memory_space=pltpu.HBM)] * 3,
        scratch=[pltpu.VMEM(inputs.shape, BF16), pltpu.VMEM(grads.shape, BF16), pltpu.SMEM(pending.shape, pending.dtype),
                 pltpu.SemaphoreType.DMA((micro + 6,))],
        flops=ENTRY_FLOPS, moved=12 * 2**20, limit=ENTRY_LIMIT,
    )
    from_left, from_right = shifted(right, True, 1), shifted(left, True, -1)

    first, small = call(first_kernel, [((rows, width), F32), ((rows, width), BF16)], (head_grad, weights[0]), whole(2), **matmul)
    shard = lax.ppermute(small, "section", [(1, 0)])
    rel = [shard] + [on_first(shard, by) for by in range(1, RING)]
    from_left, from_right, *rel = lax.optimization_barrier((from_left, from_right, *rel))
    rel = jnp.stack(rel, 0)

    passed = half + depth // 2
    upper = shifted(from_left[half:half + passed], True, 1)
    lower = shifted(from_right[half:half + passed], True, -1)
    edge = ((2 * rows, lanes), BF16)
    last_right, last_left, last_own, last_far, direct = call(
        pack_last_kernel, [edge] * 3 + [((rows, lanes), BF16), ((micro * rows, lanes), BF16)], (head_grad, rel, two), whole(3),
        moved=4 * 2**20,
    )
    last = [last_own, shifted(last_right, True, 1), shifted(last_left, True, -1)]
    last_far = shifted(last_far, True, 2)
    (acc,) = call(
        early_kernel, [((width, 2 * lanes), F32)], (right, own, from_left, from_right), whole(4),
        flops=2 * width * 2 * lanes * 3 * depth, moved=12 * 2**20,
    )
    acc, upper, lower, last_far, direct, *last = lax.optimization_barrier((acc, upper, lower, last_far, direct, *last))
    direct = shifted(direct, True, 2)
    send = ((width + TAIL, LANES), F32)

    def late(z, two):
        return call(
            functools.partial(late_kernel, z), [((width, LANES), F32)] + [send] * 3,
            (acc, right, from_left, from_right, upper, lower, *last, two), whole(10),
            scratch=[pltpu.VMEM((width, lanes), F32)],
            flops=2 * width * lanes * (3 * rows + micro * rows), moved=8 * 2**20,
        )

    keep_far, *far_sends = late(1, last_far)
    keep_near, *near_sends = late(0, direct)
    sends = far_sends + near_sends
    got = [shifted(s.astype(F16), False, by) for by, s in zip((1, 2, 3, 1, 2, 3), sends)]
    rel, *got[:4] = lax.optimization_barrier((rel, *got[:4]))
    got = [v.astype(F32) for v in got]
    (second,) = call(second_kernel, [((rows, width), F32)], (rel, first, weights[0]), whole(3), **matmul)
    (far,) = call(far_kernel, [send], (keep_far, *got[:3]), whole(4), moved=4 * 2**20)
    other = lax.ppermute(far.astype(F16), "z_hi", [(0, 1), (1, 0)]).astype(F32)
    (block,) = call(near_kernel, [((width, LANES), F32)], (keep_near, *got[3:], other), whole(5), moved=4 * 2**20)
    return (second[None], block[None])


def solution(mesh):
    fine = Mesh(mesh.devices.reshape(2, 4, 2, 4, 4), ("section", "z_lo", "z_hi", "y", "x"))
    dp = ("z_hi", "y", "x")
    return jax.shard_map(
        local,
        mesh=fine,
        in_specs=(
            P("section", "z_lo", None),
            P("section", None, dp, "z_lo"),
            P("section", None, dp, None),
            P(dp, None),
            P(),
        ),
        out_specs=(P("section", dp, "z_lo"), P("section", "z_lo", dp)),
        check_vma=False,
    )
```

```python
import functools

import jax
import jax.numpy as jnp
from jax import lax
from jax.experimental import pallas as pl
from jax.experimental.pallas import tpu as pltpu
from jax.sharding import Mesh
from jax.sharding import PartitionSpec as P

F32 = jnp.float32
F16 = jnp.float16
BF16 = jnp.bfloat16
RING = 4
LANES = 128
TAIL = 16
TOP = 15
TINY = 1e-30
ENTRY_LIMIT = 26
ENTRY_FLOPS = 10**10


def section():
    return lax.axis_index("section")


def on_last():
    return section() == lax.axis_size("section") - 1


def block_start(z_off, along, across):
    first = section() == 0
    y_off, x_off = jnp.where(first, across, along), jnp.where(first, along, across)
    z = lax.rem(lax.axis_index("z_hi") + z_off, 2)
    y = lax.rem(lax.axis_index("y") + y_off, RING)
    x = lax.rem(lax.axis_index("x") + x_off, RING)
    return pl.multiple_of((z * (RING * RING) + y * RING + x) * LANES, LANES)


def pairs_over(along, by):
    size, pairs = RING * RING, []
    for s in range(2):
        for y in range(RING):
            for x in range(RING):
                on_x = (s == 0) == along
                there = (y, (x + by) % RING) if on_x else ((y + by) % RING, x)
                pairs.append((s * size + y * RING + x, s * size + there[0] * RING + there[1]))
    return pairs


def shifted(value, along, by):
    return lax.ppermute(value, ("section", "y", "x"), pairs_over(along, by))


def whole(n=1):
    return [pl.BlockSpec(memory_space=pltpu.VMEM)] * n


def in_hbm(value):
    return pltpu.with_memory_space_constraint(value, pltpu.HBM)


def call(kernel, out_shapes, operands, specs, scratch=(), flops=0, moved=0, limit=20):
    return pl.pallas_call(
        kernel,
        out_shape=[jax.ShapeDtypeStruct(s, t) for s, t in out_shapes],
        in_specs=specs,
        out_specs=whole(len(out_shapes)),
        scratch_shapes=list(scratch),
        compiler_params=pltpu.CompilerParams(vmem_limit_bytes=limit * 2**20),
        cost_estimate=pl.CostEstimate(flops=flops, bytes_accessed=moved, transcendentals=0),
    )(*operands)


CONTRACT_LAST = (((1,), (1,)), ((), ()))


def entry_kernel(pending_ref, x_ref, stash_ref, right_ref, left_ref, own_ref, two_ref, x_in, stash_in, count_in, sems):
    micro, rows, width = x_ref.shape
    half, depth = width // 2, (micro - 1) * rows
    pieces = [(pending_ref, count_in), (x_ref, x_in)]
    pieces += [(stash_ref.at[m], stash_in.at[m]) for m in range(micro - 1)]
    copies = [pltpu.make_async_copy(a, b, sems.at[i]) for i, (a, b) in enumerate(pieces)]
    for copy in copies:
        copy.start()
    copies[0].wait()
    copies[1].wait()
    count = count_in[section()]
    for m in range(micro):
        turned = jnp.where(m >= micro - count, x_in[m].astype(F32), 0.0).T.astype(BF16)
        lanes = slice(m * rows, (m + 1) * rows)
        for out, order in ((right_ref, (half, 0)), (left_ref, (0, half))):
            for at, top in zip((0, half), order):
                out[at:at + half, lanes] = turned[top:top + half]
    share = depth // 2
    plans = [(right_ref, width, 1, 2, 0, share), (left_ref, width, 1, 2, share, depth), (two_ref, 0, 0, 2, 0, depth)]
    for z in range(2):
        at = width + share + z * depth
        plans += [(right_ref, at, z, 1, 0, depth), (left_ref, at, z, RING - 1, 0, depth), (own_ref, z * depth, z, 0, 0, depth)]
    for m in range(micro - 1):
        copies[2 + m].wait()
        for out, base, z, along, begin, end in plans:
            begin_m, end_m = max(begin, m * rows), min(end, (m + 1) * rows)
            if begin_m >= end_m:
                continue
            for b in range(RING):
                source = stash_in[m, begin_m - m * rows:end_m - m * rows, pl.ds(block_start(z, along, b), LANES)]
                out[base + begin_m - begin:base + end_m - begin, b * LANES:(b + 1) * LANES] = source


def first_kernel(grad_ref, weight_ref, out_ref, small_ref):
    step = 256
    for i in range(0, weight_ref.shape[0], step):
        out = lax.dot_general(grad_ref[...], weight_ref[i:i + step, :], CONTRACT_LAST, preferred_element_type=F32)
        out_ref[:, i:i + step] = out
        small_ref[:, i:i + step] = out.astype(BF16)


def second_kernel(rel_ref, first_ref, weight_ref, out_ref):
    step, share = 256, rel_ref.shape[2]
    tensor = lax.axis_index("z_lo")
    for i in range(0, weight_ref.shape[0], step):
        total = jnp.zeros((rel_ref.shape[1], step), F32)
        for k in range(RING):
            owner = lax.rem(tensor - k + RING, RING)
            cols = weight_ref[i:i + step, pl.ds(pl.multiple_of(owner * share, share), share)]
            total = total + lax.dot_general(rel_ref[k], cols, CONTRACT_LAST, preferred_element_type=F32)
        out_ref[:, i:i + step] = jnp.where(on_last(), first_ref[:, i:i + step], total)


def pack_last_kernel(head_ref, rel_ref, right_ref, left_ref, own_ref, two_ref):
    tensor = lax.axis_index("z_lo")
    rows, share = rel_ref.shape[1], rel_ref.shape[2]
    for z in range(2):
        for b in range(RING):
            for out, along in ((right_ref, 1), (left_ref, RING - 1), (own_ref, 0), (two_ref, 2)):
                at = block_start(z, along, b)
                inner = pl.multiple_of(lax.rem(at, share), LANES)
                chained = rel_ref[lax.rem(tensor - lax.div(at, share) + RING, RING), :, pl.ds(inner, LANES)]
                last = jnp.where(on_last(), head_ref[:, pl.ds(at, LANES)], chained)
                out[z * rows:(z + 1) * rows, b * LANES:(b + 1) * LANES] = last


def halves(ref, half, swapped):
    return (ref.at[half:2 * half], ref.at[0:half]) if swapped else (ref.at[0:half], ref.at[half:2 * half])


def early_kernel(mine_ref, own_ref, left_ref, right_ref, acc_ref):
    width, depth = acc_ref.shape[0], own_ref.shape[0] // 2
    half, lanes = width // 2, acc_ref.shape[1] // 2
    sides = [halves(mine_ref, half, True), halves(left_ref, half, True), halves(right_ref, half, False)]
    for r in range(2):
        lhs = jnp.concatenate([side[r][:, :depth] for side in sides], axis=1)
        for z in range(2):
            at = width + depth // 2 + z * depth
            rhs = [own_ref[z * depth:(z + 1) * depth, :], left_ref[at:at + depth, :], right_ref[at:at + depth, :]]
            rhs = jnp.concatenate(rhs, axis=0)
            acc_ref[r * half:(r + 1) * half, z * lanes:(z + 1) * lanes] = jnp.dot(lhs, rhs, preferred_element_type=F32)


def late_kernel(z, acc_ref, mine_ref, left_ref, right_ref, upper_ref, lower_ref, own_last, left_last, right_last, two_last,
                *rest):
    earlier = (upper_ref, lower_ref) if z else rest[:1]
    keep_ref, *sends, sum_ref = rest[1 - z:]
    width, rows = acc_ref.shape[0], own_last.shape[0] // 2
    half, lanes = width // 2, acc_ref.shape[1] // 2
    depth = mine_ref.shape[1] - rows
    mine, left, right = halves(mine_ref, half, True), halves(left_ref, half, True), halves(right_ref, half, False)
    far = (upper_ref, lower_ref)
    rhs = [ref[z * rows:(z + 1) * rows, :] for ref in (own_last, left_last, right_last, two_last)]
    rhs += [ref[half if z else 0:, :] for ref in earlier]
    rhs = jnp.concatenate(rhs, axis=0)
    largest = jnp.full((1, lanes), TINY, F32)
    for r in range(2):
        lhs = [mine[r][:, depth:], left[r][:, depth:], right[r][:, depth:], far[r][:half, depth:], far[r][:half, :depth]]
        total = jnp.dot(jnp.concatenate(lhs, axis=1), rhs, preferred_element_type=F32)
        total = total + acc_ref[r * half:(r + 1) * half, z * lanes:(z + 1) * lanes]
        largest = jnp.maximum(largest, jnp.max(jnp.abs(total), axis=0, keepdims=True))
        sum_ref[r * half:(r + 1) * half, :] = total
    power = jnp.ceil(jnp.log2(jnp.max(largest, axis=1, keepdims=True))) - TOP
    power = jnp.broadcast_to(power, (1, LANES))
    factor = jnp.exp2(-power)
    keep_ref[...] = sum_ref[:, :LANES]
    for b, out in enumerate(sends, 1):
        out[:width, :] = sum_ref[:, b * LANES:(b + 1) * LANES] * factor
        out[width:, :] = jnp.broadcast_to(power, (TAIL, LANES))


def summed(keep_ref, refs):
    rows = keep_ref.shape[0]
    total = keep_ref[...]
    for ref in refs:
        total = total + ref[:rows, :] * jnp.exp2(ref[rows:rows + 1, :])
    return total


def far_kernel(keep_ref, one_ref, two_ref, three_ref, out_ref):
    rows = keep_ref.shape[0]
    total = summed(keep_ref, (one_ref, two_ref, three_ref))
    largest = jnp.maximum(jnp.max(jnp.abs(total), axis=0, keepdims=True), TINY)
    power = jnp.ceil(jnp.log2(jnp.max(largest, axis=1, keepdims=True))) - TOP
    power = jnp.broadcast_to(power, (1, LANES))
    out_ref[:rows, :] = total * jnp.exp2(-power)
    out_ref[rows:, :] = jnp.broadcast_to(power, (TAIL, LANES))


def near_kernel(keep_ref, one_ref, two_ref, three_ref, other_ref, out_ref):
    out_ref[...] = summed(keep_ref, (one_ref, two_ref, three_ref, other_ref))


def on_first(value, by):
    return lax.ppermute(value, ("section", "z_lo"), [(i, (i + by) % RING) for i in range(RING)])


def local(weights, stash_in, stash_grad, head_grad, pending):
    inputs, grads = stash_in[0], stash_grad[0]
    micro, rows, width = inputs.shape
    depth, half, lanes = (micro - 1) * rows, width // 2, RING * LANES
    columns = head_grad.shape[1]
    matmul = dict(flops=2 * rows * width * columns, moved=2 * 2**20)

    side = ((width + depth // 2 + 2 * depth, lanes), BF16)
    right, left, own, two = call(
        entry_kernel,
        [side, side, ((2 * depth, lanes), BF16), ((depth, lanes), BF16)],
        [in_hbm(v) for v in (pending, inputs, grads)], [pl.BlockSpec(memory_space=pltpu.HBM)] * 3,
        scratch=[pltpu.VMEM(inputs.shape, BF16), pltpu.VMEM(grads.shape, BF16), pltpu.SMEM(pending.shape, pending.dtype),
                 pltpu.SemaphoreType.DMA((micro + 6,))],
        flops=ENTRY_FLOPS, moved=12 * 2**20, limit=ENTRY_LIMIT,
    )
    from_left, from_right, two = shifted(right, True, 1), shifted(left, True, -1), shifted(two, True, 2)

    first, small = call(first_kernel, [((rows, width), F32), ((rows, width), BF16)], (head_grad, weights[0]), whole(2), **matmul)
    shard = lax.ppermute(small, "section", [(1, 0)])
    one, three = on_first(shard, 1), on_first(shard, 3)
    shard, one = lax.optimization_barrier((shard, one))
    rel = [shard, one, on_first(shard, 2), three]
    from_left, from_right, two, *rel = lax.optimization_barrier((from_left, from_right, two, *rel))
    rel = jnp.stack(rel, 0)

    passed = half + depth // 2
    upper = shifted(from_left[half:half + passed], True, 1)
    lower = shifted(from_right[half:half + passed], True, -1)
    edge = ((2 * rows, lanes), BF16)
    last_right, last_left, last_own, last_two = call(
        pack_last_kernel, [edge] * 4, (head_grad, rel), whole(2), moved=4 * 2**20
    )
    last = [last_own, shifted(last_right, True, 1), shifted(last_left, True, -1), shifted(last_two, True, 2)]
    (acc,) = call(
        early_kernel, [((width, 2 * lanes), F32)], (right, own, from_left, from_right), whole(4),
        flops=2 * width * 2 * lanes * 3 * depth, moved=12 * 2**20,
    )
    acc, upper, lower, *last = lax.optimization_barrier((acc, upper, lower, *last))
    send = ((width + TAIL, LANES), F32)

    def late(z, *more):
        return call(
            functools.partial(late_kernel, z), [((width, LANES), F32)] + [send] * 3,
            (acc, right, from_left, from_right, upper, lower, *last, *more), whole(10 + len(more)),
            scratch=[pltpu.VMEM((width, lanes), F32)],
            flops=2 * width * lanes * (3 * rows + micro * rows), moved=8 * 2**20,
        )

    keep_far, *far_sends = late(1)
    keep_near, *near_sends = late(0, two)
    sends = far_sends + near_sends
    got = [shifted(s.astype(F16), False, by) for by, s in zip((1, 2, 3, 1, 2, 3), sends)]
    rel, *got[:3] = lax.optimization_barrier((rel, *got[:3]))
    got = [v.astype(F32) for v in got]
    (second,) = call(second_kernel, [((rows, width), F32)], (rel, first, weights[0]), whole(3), **matmul)
    (far,) = call(far_kernel, [send], (keep_far, *got[:3]), whole(4), moved=4 * 2**20)
    other = lax.ppermute(far.astype(F16), "z_hi", [(0, 1), (1, 0)]).astype(F32)
    (block,) = call(near_kernel, [((width, LANES), F32)], (keep_near, *got[3:], other), whole(5), moved=4 * 2**20)
    return (second[None], block[None])


def solution(mesh):
    fine = Mesh(mesh.devices.reshape(2, 4, 2, 4, 4), ("section", "z_lo", "z_hi", "y", "x"))
    dp = ("z_hi", "y", "x")
    return jax.shard_map(
        local,
        mesh=fine,
        in_specs=(
            P("section", "z_lo", None),
            P("section", None, dp, "z_lo"),
            P("section", None, dp, None),
            P(dp, None),
            P(),
        ),
        out_specs=(P("section", dp, "z_lo"), P("section", "z_lo", dp)),
        check_vma=False,
    )
```

```python
import functools

import jax
import jax.numpy as jnp
from jax import lax
from jax.experimental import pallas as pl
from jax.experimental.pallas import tpu as pltpu
from jax.sharding import Mesh
from jax.sharding import PartitionSpec as P

F32 = jnp.float32
F16 = jnp.float16
BF16 = jnp.bfloat16
RING = 4
LANES = 128
TAIL = 16
TOP = 15
TINY = 1e-30
ENTRY_LIMIT = 26
ENTRY_FLOPS = 10**10


def section():
    return lax.axis_index("section")


def on_last():
    return section() == lax.axis_size("section") - 1


def block_start(z_off, along, across):
    first = section() == 0
    y_off, x_off = jnp.where(first, across, along), jnp.where(first, along, across)
    z = lax.rem(lax.axis_index("z_hi") + z_off, 2)
    y = lax.rem(lax.axis_index("y") + y_off, RING)
    x = lax.rem(lax.axis_index("x") + x_off, RING)
    return pl.multiple_of((z * (RING * RING) + y * RING + x) * LANES, LANES)


def pairs_over(along, by):
    size, pairs = RING * RING, []
    for s in range(2):
        for y in range(RING):
            for x in range(RING):
                on_x = (s == 0) == along
                there = (y, (x + by) % RING) if on_x else ((y + by) % RING, x)
                pairs.append((s * size + y * RING + x, s * size + there[0] * RING + there[1]))
    return pairs


def shifted(value, along, by):
    return lax.ppermute(value, ("section", "y", "x"), pairs_over(along, by))


def whole(n=1):
    return [pl.BlockSpec(memory_space=pltpu.VMEM)] * n


def in_hbm(value):
    return pltpu.with_memory_space_constraint(value, pltpu.HBM)


def call(kernel, out_shapes, operands, specs, scratch=(), flops=0, moved=0, limit=20):
    return pl.pallas_call(
        kernel,
        out_shape=[jax.ShapeDtypeStruct(s, t) for s, t in out_shapes],
        in_specs=specs,
        out_specs=whole(len(out_shapes)),
        scratch_shapes=list(scratch),
        compiler_params=pltpu.CompilerParams(vmem_limit_bytes=limit * 2**20),
        cost_estimate=pl.CostEstimate(flops=flops, bytes_accessed=moved, transcendentals=0),
    )(*operands)


CONTRACT_LAST = (((1,), (1,)), ((), ()))


def entry_kernel(pending_ref, x_ref, stash_ref, right_ref, left_ref, own_ref, x_in, stash_in, count_in, sems):
    micro, rows, width = x_ref.shape
    half, depth = width // 2, (micro - 1) * rows
    pieces = [(pending_ref, count_in), (x_ref, x_in)]
    pieces += [(stash_ref.at[m], stash_in.at[m]) for m in range(micro - 1)]
    copies = [pltpu.make_async_copy(a, b, sems.at[i]) for i, (a, b) in enumerate(pieces)]
    for copy in copies:
        copy.start()
    copies[0].wait()
    copies[1].wait()
    count = count_in[section()]
    for m in range(micro):
        turned = jnp.where(m >= micro - count, x_in[m].astype(F32), 0.0).T.astype(BF16)
        lanes = slice(m * rows, (m + 1) * rows)
        for out, order in ((right_ref, (half, 0)), (left_ref, (0, half))):
            for at, top in zip((0, half), order):
                out[at:at + half, lanes] = turned[top:top + half]
    share = depth // 2
    plans = []
    for z in range(2):
        at = width + z * share
        plans += [(right_ref, at, z, 2, 0, share), (left_ref, at, z, 2, share, depth)]
        at = width + (1 + z) * depth
        plans += [(right_ref, at, z, 1, 0, depth), (left_ref, at, z, RING - 1, 0, depth), (own_ref, z * depth, z, 0, 0, depth)]
    for m in range(micro - 1):
        copies[2 + m].wait()
        for out, base, z, along, begin, end in plans:
            begin_m, end_m = max(begin, m * rows), min(end, (m + 1) * rows)
            if begin_m >= end_m:
                continue
            for b in range(RING):
                source = stash_in[m, begin_m - m * rows:end_m - m * rows, pl.ds(block_start(z, along, b), LANES)]
                out[base + begin_m - begin:base + end_m - begin, b * LANES:(b + 1) * LANES] = source


def first_kernel(grad_ref, weight_ref, out_ref, small_ref):
    step = 256
    for i in range(0, weight_ref.shape[0], step):
        out = lax.dot_general(grad_ref[...], weight_ref[i:i + step, :], CONTRACT_LAST, preferred_element_type=F32)
        out_ref[:, i:i + step] = out
        small_ref[:, i:i + step] = out.astype(BF16)


def second_kernel(rel_ref, first_ref, weight_ref, out_ref):
    step, share = 256, rel_ref.shape[2]
    tensor = lax.axis_index("z_lo")
    for i in range(0, weight_ref.shape[0], step):
        total = jnp.zeros((rel_ref.shape[1], step), F32)
        for k in range(RING):
            owner = lax.rem(tensor - k + RING, RING)
            cols = weight_ref[i:i + step, pl.ds(pl.multiple_of(owner * share, share), share)]
            total = total + lax.dot_general(rel_ref[k], cols, CONTRACT_LAST, preferred_element_type=F32)
        out_ref[:, i:i + step] = jnp.where(on_last(), first_ref[:, i:i + step], total)


def pack_last_kernel(head_ref, rel_ref, right_ref, left_ref, own_ref, two_ref):
    tensor = lax.axis_index("z_lo")
    rows, share = rel_ref.shape[1], rel_ref.shape[2]
    for z in range(2):
        for b in range(RING):
            for out, along in ((right_ref, 1), (left_ref, RING - 1), (own_ref, 0), (two_ref, 2)):
                at = block_start(z, along, b)
                inner = pl.multiple_of(lax.rem(at, share), LANES)
                chained = rel_ref[lax.rem(tensor - lax.div(at, share) + RING, RING), :, pl.ds(inner, LANES)]
                last = jnp.where(on_last(), head_ref[:, pl.ds(at, LANES)], chained)
                out[z * rows:(z + 1) * rows, b * LANES:(b + 1) * LANES] = last


def halves(ref, half, swapped):
    return (ref.at[half:2 * half], ref.at[0:half]) if swapped else (ref.at[0:half], ref.at[half:2 * half])


def early_kernel(mine_ref, own_ref, left_ref, right_ref, acc_ref):
    width, depth = acc_ref.shape[0], own_ref.shape[0] // 2
    half, lanes = width // 2, acc_ref.shape[1] // 2
    sides = [halves(mine_ref, half, True), halves(left_ref, half, True), halves(right_ref, half, False)]
    for r in range(2):
        lhs = jnp.concatenate([side[r][:, :depth] for side in sides], axis=1)
        for z in range(2):
            at = width + (1 + z) * depth
            rhs = [own_ref[z * depth:(z + 1) * depth, :], left_ref[at:at + depth, :], right_ref[at:at + depth, :]]
            rhs = jnp.concatenate(rhs, axis=0)
            acc_ref[r * half:(r + 1) * half, z * lanes:(z + 1) * lanes] = jnp.dot(lhs, rhs, preferred_element_type=F32)


def late_kernel(z, acc_ref, mine_ref, left_ref, right_ref, upper_ref, lower_ref, own_last, left_last, right_last, two_last,
                keep_ref, *rest):
    sends, sum_ref = rest[:-1], rest[-1]
    width, rows = acc_ref.shape[0], own_last.shape[0] // 2
    half, lanes = width // 2, acc_ref.shape[1] // 2
    depth = mine_ref.shape[1] - rows
    mine, left, right = halves(mine_ref, half, True), halves(left_ref, half, True), halves(right_ref, half, False)
    far = (upper_ref, lower_ref)
    rhs = [ref[z * rows:(z + 1) * rows, :] for ref in (own_last, left_last, right_last, two_last)]
    at = half + z * depth // 2
    rhs += [ref[at:at + depth // 2, :] for ref in far]
    rhs = jnp.concatenate(rhs, axis=0)
    largest = jnp.full((1, lanes), TINY, F32)
    for r in range(2):
        lhs = [mine[r][:, depth:], left[r][:, depth:], right[r][:, depth:], far[r][:half, depth:], far[r][:half, :depth]]
        total = jnp.dot(jnp.concatenate(lhs, axis=1), rhs, preferred_element_type=F32)
        total = total + acc_ref[r * half:(r + 1) * half, z * lanes:(z + 1) * lanes]
        largest = jnp.maximum(largest, jnp.max(jnp.abs(total), axis=0, keepdims=True))
        sum_ref[r * half:(r + 1) * half, :] = total
    power = jnp.ceil(jnp.log2(jnp.max(largest, axis=1, keepdims=True))) - TOP
    power = jnp.broadcast_to(power, (1, LANES))
    factor = jnp.exp2(-power)
    keep_ref[...] = sum_ref[:, :LANES]
    for b, out in enumerate(sends, 1):
        out[:width, :] = sum_ref[:, b * LANES:(b + 1) * LANES] * factor
        out[width:, :] = jnp.broadcast_to(power, (TAIL, LANES))


def summed(keep_ref, refs):
    rows = keep_ref.shape[0]
    total = keep_ref[...]
    for ref in refs:
        total = total + ref[:rows, :] * jnp.exp2(ref[rows:rows + 1, :])
    return total


def far_kernel(keep_ref, one_ref, two_ref, three_ref, out_ref):
    rows = keep_ref.shape[0]
    total = summed(keep_ref, (one_ref, two_ref, three_ref))
    largest = jnp.maximum(jnp.max(jnp.abs(total), axis=0, keepdims=True), TINY)
    power = jnp.ceil(jnp.log2(jnp.max(largest, axis=1, keepdims=True))) - TOP
    power = jnp.broadcast_to(power, (1, LANES))
    out_ref[:rows, :] = total * jnp.exp2(-power)
    out_ref[rows:, :] = jnp.broadcast_to(power, (TAIL, LANES))


def near_kernel(keep_ref, one_ref, two_ref, three_ref, other_ref, out_ref):
    out_ref[...] = summed(keep_ref, (one_ref, two_ref, three_ref, other_ref))


def on_first(value, by):
    return lax.ppermute(value, ("section", "z_lo"), [(i, (i + by) % RING) for i in range(RING)])


def local(weights, stash_in, stash_grad, head_grad, pending):
    inputs, grads = stash_in[0], stash_grad[0]
    micro, rows, width = inputs.shape
    depth, half, lanes = (micro - 1) * rows, width // 2, RING * LANES
    columns = head_grad.shape[1]
    matmul = dict(flops=2 * rows * width * columns, moved=2 * 2**20)

    side = ((width + 3 * depth, lanes), BF16)
    right, left, own = call(
        entry_kernel,
        [side, side, ((2 * depth, lanes), BF16)],
        [in_hbm(v) for v in (pending, inputs, grads)], [pl.BlockSpec(memory_space=pltpu.HBM)] * 3,
        scratch=[pltpu.VMEM(inputs.shape, BF16), pltpu.VMEM(grads.shape, BF16), pltpu.SMEM(pending.shape, pending.dtype),
                 pltpu.SemaphoreType.DMA((micro + 6,))],
        flops=ENTRY_FLOPS, moved=12 * 2**20, limit=ENTRY_LIMIT,
    )
    from_left, from_right = shifted(right, True, 1), shifted(left, True, -1)

    first, small = call(first_kernel, [((rows, width), F32), ((rows, width), BF16)], (head_grad, weights[0]), whole(2), **matmul)
    shard = lax.ppermute(small, "section", [(1, 0)])
    rel = [shard] + [on_first(shard, by) for by in range(1, RING)]
    from_left, from_right, *rel = lax.optimization_barrier((from_left, from_right, *rel))
    rel = jnp.stack(rel, 0)

    passed = half + depth
    upper = shifted(from_left[half:half + passed], True, 1)
    lower = shifted(from_right[half:half + passed], True, -1)
    edge = ((2 * rows, lanes), BF16)
    last_right, last_left, last_own, last_two = call(
        pack_last_kernel, [edge] * 4, (head_grad, rel), whole(2), moved=4 * 2**20
    )
    last = [last_own, shifted(last_right, True, 1), shifted(last_left, True, -1), shifted(last_two, True, 2)]
    (acc,) = call(
        early_kernel, [((width, 2 * lanes), F32)], (right, own, from_left, from_right), whole(4),
        flops=2 * width * 2 * lanes * 3 * depth, moved=12 * 2**20,
    )
    acc, upper, lower, *last = lax.optimization_barrier((acc, upper, lower, *last))
    send = ((width + TAIL, LANES), F32)

    def late(z):
        return call(
            functools.partial(late_kernel, z), [((width, LANES), F32)] + [send] * 3,
            (acc, right, from_left, from_right, upper, lower, *last), whole(10),
            scratch=[pltpu.VMEM((width, lanes), F32)],
            flops=2 * width * lanes * (3 * rows + micro * rows), moved=8 * 2**20,
        )

    keep_far, *far_sends = late(1)
    keep_near, *near_sends = late(0)
    sends = far_sends + near_sends
    got = [shifted(s.astype(F16), False, by) for by, s in zip((1, 2, 3, 1, 2, 3), sends)]
    rel, *got[:3] = lax.optimization_barrier((rel, *got[:3]))
    got = [v.astype(F32) for v in got]
    (second,) = call(second_kernel, [((rows, width), F32)], (rel, first, weights[0]), whole(3), **matmul)
    (far,) = call(far_kernel, [send], (keep_far, *got[:3]), whole(4), moved=4 * 2**20)
    other = lax.ppermute(far.astype(F16), "z_hi", [(0, 1), (1, 0)]).astype(F32)
    (block,) = call(near_kernel, [((width, LANES), F32)], (keep_near, *got[3:], other), whole(5), moved=4 * 2**20)
    return (second[None], block[None])


def solution(mesh):
    fine = Mesh(mesh.devices.reshape(2, 4, 2, 4, 4), ("section", "z_lo", "z_hi", "y", "x"))
    dp = ("z_hi", "y", "x")
    return jax.shard_map(
        local,
        mesh=fine,
        in_specs=(
            P("section", "z_lo", None),
            P("section", None, dp, "z_lo"),
            P("section", None, dp, None),
            P(dp, None),
            P(),
        ),
        out_specs=(P("section", dp, "z_lo"), P("section", "z_lo", dp)),
        check_vma=False,
    )
```

```python
import functools

import jax
import jax.numpy as jnp
from jax import lax
from jax.experimental import pallas as pl
from jax.experimental.pallas import tpu as pltpu
from jax.sharding import Mesh
from jax.sharding import PartitionSpec as P

F32 = jnp.float32
F16 = jnp.float16
BF16 = jnp.bfloat16
RING = 4
LANES = 128
TAIL = 16
TOP = 15
TINY = 1e-30
ENTRY_LIMIT = 26
ENTRY_FLOPS = 10**10


def section():
    return lax.axis_index("section")


def on_last():
    return section() == lax.axis_size("section") - 1


def block_start(z_off, along, across):
    first = section() == 0
    y_off, x_off = jnp.where(first, across, along), jnp.where(first, along, across)
    z = lax.rem(lax.axis_index("z_hi") + z_off, 2)
    y = lax.rem(lax.axis_index("y") + y_off, RING)
    x = lax.rem(lax.axis_index("x") + x_off, RING)
    return pl.multiple_of((z * (RING * RING) + y * RING + x) * LANES, LANES)


def pairs_over(along, by):
    size, pairs = RING * RING, []
    for s in range(2):
        for y in range(RING):
            for x in range(RING):
                on_x = (s == 0) == along
                there = (y, (x + by) % RING) if on_x else ((y + by) % RING, x)
                pairs.append((s * size + y * RING + x, s * size + there[0] * RING + there[1]))
    return pairs


def shifted(value, along, by):
    return lax.ppermute(value, ("section", "y", "x"), pairs_over(along, by))


def whole(n=1):
    return [pl.BlockSpec(memory_space=pltpu.VMEM)] * n


def in_hbm(value):
    return pltpu.with_memory_space_constraint(value, pltpu.HBM)


def call(kernel, out_shapes, operands, specs, scratch=(), flops=0, moved=0, limit=20):
    return pl.pallas_call(
        kernel,
        out_shape=[jax.ShapeDtypeStruct(s, t) for s, t in out_shapes],
        in_specs=specs,
        out_specs=whole(len(out_shapes)),
        scratch_shapes=list(scratch),
        compiler_params=pltpu.CompilerParams(vmem_limit_bytes=limit * 2**20),
        cost_estimate=pl.CostEstimate(flops=flops, bytes_accessed=moved, transcendentals=0),
    )(*operands)


CONTRACT_LAST = (((1,), (1,)), ((), ()))


def entry_kernel(pending_ref, x_ref, stash_ref, right_on, left_on, right_ref, left_ref, own_ref, x_in, stash_in, count_in, sems):
    micro, rows, width = x_ref.shape
    half, depth = width // 2, (micro - 1) * rows
    pieces = [(pending_ref, count_in), (x_ref, x_in)]
    pieces += [(stash_ref.at[m], stash_in.at[m]) for m in range(micro - 1)]
    copies = [pltpu.make_async_copy(a, b, sems.at[i]) for i, (a, b) in enumerate(pieces)]
    for copy in copies:
        copy.start()
    copies[0].wait()
    copies[1].wait()
    count = count_in[section()]
    for m in range(micro):
        turned = jnp.where(m >= micro - count, x_in[m].astype(F32), 0.0).T.astype(BF16)
        lanes = slice(m * rows, (m + 1) * rows)
        for out, top in ((right_on, 0), (right_ref, half), (left_on, half), (left_ref, 0)):
            out[:half, lanes] = turned[top:top + half]
    share = depth // 2
    plans = []
    for z in range(2):
        at = half + z * share
        plans += [(right_on, at, z, 2, 0, share), (left_on, at, z, 2, share, depth)]
        at = half + z * depth
        plans += [(right_ref, at, z, 1, 0, depth), (left_ref, at, z, RING - 1, 0, depth), (own_ref, z * depth, z, 0, 0, depth)]
    for m in range(micro - 1):
        copies[2 + m].wait()
        for out, base, z, along, begin, end in plans:
            begin_m, end_m = max(begin, m * rows), min(end, (m + 1) * rows)
            if begin_m >= end_m:
                continue
            for b in range(RING):
                source = stash_in[m, begin_m - m * rows:end_m - m * rows, pl.ds(block_start(z, along, b), LANES)]
                out[base + begin_m - begin:base + end_m - begin, b * LANES:(b + 1) * LANES] = source


def first_kernel(grad_ref, weight_ref, out_ref, small_ref):
    step = 256
    for i in range(0, weight_ref.shape[0], step):
        out = lax.dot_general(grad_ref[...], weight_ref[i:i + step, :], CONTRACT_LAST, preferred_element_type=F32)
        out_ref[:, i:i + step] = out
        small_ref[:, i:i + step] = out.astype(BF16)


def second_kernel(rel_ref, first_ref, weight_ref, out_ref):
    step, share = 256, rel_ref.shape[2]
    tensor = lax.axis_index("z_lo")
    for i in range(0, weight_ref.shape[0], step):
        total = jnp.zeros((rel_ref.shape[1], step), F32)
        for k in range(RING):
            owner = lax.rem(tensor - k + RING, RING)
            cols = weight_ref[i:i + step, pl.ds(pl.multiple_of(owner * share, share), share)]
            total = total + lax.dot_general(rel_ref[k], cols, CONTRACT_LAST, preferred_element_type=F32)
        out_ref[:, i:i + step] = jnp.where(on_last(), first_ref[:, i:i + step], total)


def pack_last_kernel(head_ref, rel_ref, right_ref, left_ref, own_ref, two_ref):
    tensor = lax.axis_index("z_lo")
    rows, share = rel_ref.shape[1], rel_ref.shape[2]
    for z in range(2):
        for b in range(RING):
            for out, along in ((right_ref, 1), (left_ref, RING - 1), (own_ref, 0), (two_ref, 2)):
                at = block_start(z, along, b)
                inner = pl.multiple_of(lax.rem(at, share), LANES)
                chained = rel_ref[lax.rem(tensor - lax.div(at, share) + RING, RING), :, pl.ds(inner, LANES)]
                last = jnp.where(on_last(), head_ref[:, pl.ds(at, LANES)], chained)
                out[z * rows:(z + 1) * rows, b * LANES:(b + 1) * LANES] = last


def early_kernel(mine_on, mine_ref, own_ref, left_on, left_ref, right_on, right_ref, acc_ref):
    width, depth = acc_ref.shape[0], own_ref.shape[0] // 2
    half, lanes = width // 2, acc_ref.shape[1] // 2
    sides = [(mine_on, mine_ref), (left_on, left_ref), (right_ref, right_on)]
    for r in range(2):
        lhs = jnp.concatenate([side[r][:half, :depth] for side in sides], axis=1)
        for z in range(2):
            at = half + z * depth
            rhs = [own_ref[z * depth:(z + 1) * depth, :], left_ref[at:at + depth, :], right_ref[at:at + depth, :]]
            rhs = jnp.concatenate(rhs, axis=0)
            acc_ref[r * half:(r + 1) * half, z * lanes:(z + 1) * lanes] = jnp.dot(lhs, rhs, preferred_element_type=F32)


def late_kernel(z, acc_ref, mine_on, mine_ref, left_on, left_ref, right_on, right_ref, upper_ref, lower_ref,
                two_last, left_last, right_last, own_last, keep_ref, *rest):
    sends, sum_ref = rest[:-1], rest[-1]
    width, rows = acc_ref.shape[0], own_last.shape[0] // 2
    half, lanes = width // 2, acc_ref.shape[1] // 2
    depth = mine_ref.shape[1] - rows
    mine, left, right, far = (mine_on, mine_ref), (left_on, left_ref), (right_ref, right_on), (upper_ref, lower_ref)
    rhs = [ref[z * rows:(z + 1) * rows, :] for ref in (own_last, left_last, right_last, two_last)]
    at = half + z * depth // 2
    rhs += [ref[at:at + depth // 2, :] for ref in far]
    rhs = jnp.concatenate(rhs, axis=0)
    largest = jnp.full((1, lanes), TINY, F32)
    for r in range(2):
        lhs = [side[r][:half, depth:] for side in (mine, left, right, far)] + [far[r][:half, :depth]]
        total = jnp.dot(jnp.concatenate(lhs, axis=1), rhs, preferred_element_type=F32)
        total = total + acc_ref[r * half:(r + 1) * half, z * lanes:(z + 1) * lanes]
        largest = jnp.maximum(largest, jnp.max(jnp.abs(total), axis=0, keepdims=True))
        sum_ref[r * half:(r + 1) * half, :] = total
    power = jnp.ceil(jnp.log2(jnp.max(largest, axis=1, keepdims=True))) - TOP
    power = jnp.broadcast_to(power, (1, LANES))
    factor = jnp.exp2(-power)
    keep_ref[...] = sum_ref[:, :LANES]
    for b, out in enumerate(sends, 1):
        out[:width, :] = sum_ref[:, b * LANES:(b + 1) * LANES] * factor
        out[width:, :] = jnp.broadcast_to(power, (TAIL, LANES))


def summed(keep_ref, refs):
    rows = keep_ref.shape[0]
    total = keep_ref[...]
    for ref in refs:
        total = total + ref[:rows, :] * jnp.exp2(ref[rows:rows + 1, :])
    return total


def far_kernel(keep_ref, one_ref, two_ref, three_ref, out_ref):
    rows = keep_ref.shape[0]
    total = summed(keep_ref, (one_ref, two_ref, three_ref))
    largest = jnp.maximum(jnp.max(jnp.abs(total), axis=0, keepdims=True), TINY)
    power = jnp.ceil(jnp.log2(jnp.max(largest, axis=1, keepdims=True))) - TOP
    power = jnp.broadcast_to(power, (1, LANES))
    out_ref[:rows, :] = total * jnp.exp2(-power)
    out_ref[rows:, :] = jnp.broadcast_to(power, (TAIL, LANES))


def near_kernel(keep_ref, one_ref, two_ref, three_ref, other_ref, out_ref):
    out_ref[...] = summed(keep_ref, (one_ref, two_ref, three_ref, other_ref))


def on_first(value, by):
    return lax.ppermute(value, ("section", "z_lo"), [(i, (i + by) % RING) for i in range(RING)])


def local(weights, stash_in, stash_grad, head_grad, pending):
    inputs, grads = stash_in[0], stash_grad[0]
    micro, rows, width = inputs.shape
    depth, half, lanes = (micro - 1) * rows, width // 2, RING * LANES
    columns = head_grad.shape[1]
    matmul = dict(flops=2 * rows * width * columns, moved=2 * 2**20)

    going, staying = ((half + depth, lanes), BF16), ((half + 2 * depth, lanes), BF16)
    right_on, left_on, right, left, own = call(
        entry_kernel, [going, going, staying, staying, ((2 * depth, lanes), BF16)],
        [in_hbm(v) for v in (pending, inputs, grads)], [pl.BlockSpec(memory_space=pltpu.HBM)] * 3,
        scratch=[pltpu.VMEM(inputs.shape, BF16), pltpu.VMEM(grads.shape, BF16), pltpu.SMEM(pending.shape, pending.dtype),
                 pltpu.SemaphoreType.DMA((micro + 6,))],
        flops=ENTRY_FLOPS, moved=12 * 2**20, limit=ENTRY_LIMIT,
    )
    from_left_on, from_right_on = shifted(right_on, True, 1), shifted(left_on, True, -1)

    first, small = call(first_kernel, [((rows, width), F32), ((rows, width), BF16)], (head_grad, weights[0]), whole(2), **matmul)
    shard = lax.ppermute(small, "section", [(1, 0)])
    staying_right, staying_left, shard = lax.optimization_barrier((right, left, shard))
    from_left, from_right = shifted(staying_right, True, 1), shifted(staying_left, True, -1)
    one = on_first(shard, 1)
    shard, one, from_left_on, from_right_on = lax.optimization_barrier((shard, one, from_left_on, from_right_on))
    upper, lower = shifted(from_left_on, True, 1), shifted(from_right_on, True, -1)
    rel = [shard, one, on_first(shard, 2), on_first(shard, 3)]
    rel = jnp.stack(rel, 0)

    edge = ((2 * rows, lanes), BF16)
    last_right, last_left, last_own, last_two = call(
        pack_last_kernel, [edge] * 4, (head_grad, rel), whole(2), moved=4 * 2**20
    )
    last = [shifted(last_two, True, 2), shifted(last_right, True, 1), shifted(last_left, True, -1), last_own]
    (acc,) = call(
        early_kernel, [((width, 2 * lanes), F32)], (right_on, right, own, from_left_on, from_left, from_right_on, from_right), whole(7),
        flops=2 * width * 2 * lanes * 3 * depth, moved=12 * 2**20,
    )
    acc, upper, lower, *last = lax.optimization_barrier((acc, upper, lower, *last))
    send = ((width + TAIL, LANES), F32)

    def late(z):
        return call(
            functools.partial(late_kernel, z), [((width, LANES), F32)] + [send] * 3,
            (acc, right_on, right, from_left_on, from_left, from_right_on, from_right, upper, lower, *last), whole(13),
            scratch=[pltpu.VMEM((width, lanes), F32)],
            flops=2 * width * lanes * (3 * rows + micro * rows), moved=8 * 2**20,
        )

    keep_far, *far_sends = late(1)
    keep_near, *near_sends = late(0)
    sends = far_sends + near_sends
    got = [shifted(sends[i].astype(F16), False, 1 + i % 3) for i in (1, 0, 2, 4, 3, 5)]
    rel, *got[:3] = lax.optimization_barrier((rel, *got[:3]))
    got = [v.astype(F32) for v in got]
    (second,) = call(second_kernel, [((rows, width), F32)], (rel, first, weights[0]), whole(3), **matmul)
    (far,) = call(far_kernel, [send], (keep_far, *got[:3]), whole(4), moved=4 * 2**20)
    other = lax.ppermute(far.astype(F16), "z_hi", [(0, 1), (1, 0)]).astype(F32)
    (block,) = call(near_kernel, [((width, LANES), F32)], (keep_near, *got[3:], other), whole(5), moved=4 * 2**20)
    return (second[None], block[None])


def solution(mesh):
    fine = Mesh(mesh.devices.reshape(2, 4, 2, 4, 4), ("section", "z_lo", "z_hi", "y", "x"))
    dp = ("z_hi", "y", "x")
    return jax.shard_map(
        local,
        mesh=fine,
        in_specs=(
            P("section", "z_lo", None),
            P("section", None, dp, "z_lo"),
            P("section", None, dp, None),
            P(dp, None),
            P(),
        ),
        out_specs=(P("section", dp, "z_lo"), P("section", "z_lo", dp)),
        check_vma=False,
    )
```

```python
import functools

import jax
import jax.numpy as jnp
from jax import lax
from jax.experimental import pallas as pl
from jax.experimental.pallas import tpu as pltpu
from jax.sharding import Mesh
from jax.sharding import PartitionSpec as P

F32 = jnp.float32
F16 = jnp.float16
BF16 = jnp.bfloat16
RING = 4
LANES = 128
TAIL = 16
TOP = 15
TINY = 1e-30
ENTRY_LIMIT = 26
ENTRY_FLOPS = 10**10


def section():
    return lax.axis_index("section")


def on_last():
    return section() == lax.axis_size("section") - 1


def block_start(z_off, along, across):
    first = section() == 0
    y_off, x_off = jnp.where(first, across, along), jnp.where(first, along, across)
    z = lax.rem(lax.axis_index("z_hi") + z_off, 2)
    y = lax.rem(lax.axis_index("y") + y_off, RING)
    x = lax.rem(lax.axis_index("x") + x_off, RING)
    return pl.multiple_of((z * (RING * RING) + y * RING + x) * LANES, LANES)


def pairs_over(along, by):
    size, pairs = RING * RING, []
    for s in range(2):
        for y in range(RING):
            for x in range(RING):
                on_x = (s == 0) == along
                there = (y, (x + by) % RING) if on_x else ((y + by) % RING, x)
                pairs.append((s * size + y * RING + x, s * size + there[0] * RING + there[1]))
    return pairs


def shifted(value, along, by):
    return lax.ppermute(value, ("section", "y", "x"), pairs_over(along, by))


def whole(n=1):
    return [pl.BlockSpec(memory_space=pltpu.VMEM)] * n


def in_hbm(value):
    return pltpu.with_memory_space_constraint(value, pltpu.HBM)


def call(kernel, out_shapes, operands, specs, scratch=(), flops=0, moved=0, limit=20):
    return pl.pallas_call(
        kernel,
        out_shape=[jax.ShapeDtypeStruct(s, t) for s, t in out_shapes],
        in_specs=specs,
        out_specs=whole(len(out_shapes)),
        scratch_shapes=list(scratch),
        compiler_params=pltpu.CompilerParams(vmem_limit_bytes=limit * 2**20),
        cost_estimate=pl.CostEstimate(flops=flops, bytes_accessed=moved, transcendentals=0),
    )(*operands)


CONTRACT_LAST = (((1,), (1,)), ((), ()))


def entry_kernel(pending_ref, x_ref, stash_ref, right_on, left_on, right_ref, left_ref, own_ref, x_in, stash_in, count_in, sems):
    micro, rows, width = x_ref.shape
    half, depth = width // 2, (micro - 1) * rows
    pieces = [(pending_ref, count_in), (x_ref, x_in)]
    pieces += [(stash_ref.at[m], stash_in.at[m]) for m in range(micro - 1)]
    copies = [pltpu.make_async_copy(a, b, sems.at[i]) for i, (a, b) in enumerate(pieces)]
    for copy in copies:
        copy.start()
    copies[0].wait()
    copies[1].wait()
    count = count_in[section()]
    for m in range(micro):
        turned = jnp.where(m >= micro - count, x_in[m].astype(F32), 0.0).T.astype(BF16)
        lanes = slice(m * rows, (m + 1) * rows)
        for out, top in ((right_on, 0), (right_ref, half), (left_on, half), (left_ref, 0)):
            out[:half, lanes] = turned[top:top + half]
    share = depth // 2
    plans = []
    for z in range(2):
        at = half + z * share
        plans += [(right_on, at, z, 2, 0, share), (left_on, at, z, 2, share, depth)]
        at = half + z * depth
        plans += [(right_ref, at, z, 1, 0, depth), (left_ref, at, z, RING - 1, 0, depth), (own_ref, z * depth, z, 0, 0, depth)]
    for m in range(micro - 1):
        copies[2 + m].wait()
        for out, base, z, along, begin, end in plans:
            begin_m, end_m = max(begin, m * rows), min(end, (m + 1) * rows)
            if begin_m >= end_m:
                continue
            for b in range(RING):
                source = stash_in[m, begin_m - m * rows:end_m - m * rows, pl.ds(block_start(z, along, b), LANES)]
                out[base + begin_m - begin:base + end_m - begin, b * LANES:(b + 1) * LANES] = source


def first_kernel(grad_ref, weight_ref, out_ref, small_ref):
    step = 256
    for i in range(0, weight_ref.shape[0], step):
        out = lax.dot_general(grad_ref[...], weight_ref[i:i + step, :], CONTRACT_LAST, preferred_element_type=F32)
        out_ref[:, i:i + step] = out
        small_ref[:, i:i + step] = out.astype(BF16)


def second_kernel(rel_ref, first_ref, weight_ref, out_ref):
    step, share = 256, rel_ref.shape[2]
    tensor = lax.axis_index("z_lo")
    for i in range(0, weight_ref.shape[0], step):
        total = jnp.zeros((rel_ref.shape[1], step), F32)
        for k in range(RING):
            owner = lax.rem(tensor - k + RING, RING)
            cols = weight_ref[i:i + step, pl.ds(pl.multiple_of(owner * share, share), share)]
            total = total + lax.dot_general(rel_ref[k], cols, CONTRACT_LAST, preferred_element_type=F32)
        out_ref[:, i:i + step] = jnp.where(on_last(), first_ref[:, i:i + step], total)


def pack_last_kernel(head_ref, rel_ref, right_ref, left_ref, own_ref, two_ref):
    tensor = lax.axis_index("z_lo")
    rows, share = rel_ref.shape[1], rel_ref.shape[2]
    for z in range(2):
        for b in range(RING):
            for out, along in ((right_ref, 1), (left_ref, RING - 1), (own_ref, 0), (two_ref, 2)):
                at = block_start(z, along, b)
                inner = pl.multiple_of(lax.rem(at, share), LANES)
                chained = rel_ref[lax.rem(tensor - lax.div(at, share) + RING, RING), :, pl.ds(inner, LANES)]
                last = jnp.where(on_last(), head_ref[:, pl.ds(at, LANES)], chained)
                out[z * rows:(z + 1) * rows, b * LANES:(b + 1) * LANES] = last


def early_kernel(mine_on, mine_ref, own_ref, left_on, left_ref, right_on, right_ref, acc_ref):
    width, depth = acc_ref.shape[0], own_ref.shape[0] // 2
    half, lanes = width // 2, acc_ref.shape[1] // 2
    sides = [(mine_on, mine_ref), (left_on, left_ref), (right_ref, right_on)]
    for r in range(2):
        lhs = jnp.concatenate([side[r][:half, :depth] for side in sides], axis=1)
        for z in range(2):
            at = half + z * depth
            rhs = [own_ref[z * depth:(z + 1) * depth, :], left_ref[at:at + depth, :], right_ref[at:at + depth, :]]
            rhs = jnp.concatenate(rhs, axis=0)
            acc_ref[r * half:(r + 1) * half, z * lanes:(z + 1) * lanes] = jnp.dot(lhs, rhs, preferred_element_type=F32)


def late_kernel(z, acc_ref, mine_on, mine_ref, left_on, left_ref, right_on, right_ref, upper_ref, lower_ref,
                two_last, left_last, right_last, own_last, keep_ref, *rest):
    sends, sum_ref = rest[:-1], rest[-1]
    width, rows = acc_ref.shape[0], own_last.shape[0] // 2
    half, lanes = width // 2, acc_ref.shape[1] // 2
    depth = mine_ref.shape[1] - rows
    mine, left, right, far = (mine_on, mine_ref), (left_on, left_ref), (right_ref, right_on), (upper_ref, lower_ref)
    rhs = [ref[z * rows:(z + 1) * rows, :] for ref in (own_last, left_last, right_last, two_last)]
    at = half + z * depth // 2
    rhs += [ref[at:at + depth // 2, :] for ref in far]
    rhs = jnp.concatenate(rhs, axis=0)
    largest = jnp.full((1, lanes), TINY, F32)
    for r in range(2):
        lhs = [side[r][:half, depth:] for side in (mine, left, right, far)] + [far[r][:half, :depth]]
        total = jnp.dot(jnp.concatenate(lhs, axis=1), rhs, preferred_element_type=F32)
        total = total + acc_ref[r * half:(r + 1) * half, z * lanes:(z + 1) * lanes]
        largest = jnp.maximum(largest, jnp.max(jnp.abs(total), axis=0, keepdims=True))
        sum_ref[r * half:(r + 1) * half, :] = total
    power = jnp.ceil(jnp.log2(jnp.max(largest, axis=1, keepdims=True))) - TOP
    power = jnp.broadcast_to(power, (1, LANES))
    factor = jnp.exp2(-power)
    keep_ref[...] = sum_ref[:, :LANES]
    for b, out in enumerate(sends, 1):
        out[:width, :] = sum_ref[:, b * LANES:(b + 1) * LANES] * factor
        out[width:, :] = jnp.broadcast_to(power, (TAIL, LANES))


def summed(keep_ref, refs):
    rows = keep_ref.shape[0]
    total = keep_ref[...]
    for ref in refs:
        total = total + ref[:rows, :] * jnp.exp2(ref[rows:rows + 1, :])
    return total


def far_kernel(keep_ref, one_ref, two_ref, three_ref, out_ref):
    rows = keep_ref.shape[0]
    total = summed(keep_ref, (one_ref, two_ref, three_ref))
    largest = jnp.maximum(jnp.max(jnp.abs(total), axis=0, keepdims=True), TINY)
    power = jnp.ceil(jnp.log2(jnp.max(largest, axis=1, keepdims=True))) - TOP
    power = jnp.broadcast_to(power, (1, LANES))
    out_ref[:rows, :] = total * jnp.exp2(-power)
    out_ref[rows:, :] = jnp.broadcast_to(power, (TAIL, LANES))


def near_kernel(keep_ref, one_ref, two_ref, three_ref, other_ref, out_ref):
    out_ref[...] = summed(keep_ref, (one_ref, two_ref, three_ref, other_ref))


def on_line(value, pairs):
    pairs = [(s * RING + i, t * RING + j % RING) for (s, i), (t, j) in pairs]
    return lax.ppermute(value, ("section", "z_lo"), pairs)


def local(weights, stash_in, stash_grad, head_grad, pending):
    inputs, grads = stash_in[0], stash_grad[0]
    micro, rows, width = inputs.shape
    depth, half, lanes = (micro - 1) * rows, width // 2, RING * LANES
    columns = head_grad.shape[1]
    matmul = dict(flops=2 * rows * width * columns, moved=2 * 2**20)

    going, staying = ((half + depth, lanes), BF16), ((half + 2 * depth, lanes), BF16)
    right_on, left_on, right, left, own = call(
        entry_kernel, [going, going, staying, staying, ((2 * depth, lanes), BF16)],
        [in_hbm(v) for v in (pending, inputs, grads)], [pl.BlockSpec(memory_space=pltpu.HBM)] * 3,
        scratch=[pltpu.VMEM(inputs.shape, BF16), pltpu.VMEM(grads.shape, BF16), pltpu.SMEM(pending.shape, pending.dtype),
                 pltpu.SemaphoreType.DMA((micro + 6,))],
        flops=ENTRY_FLOPS, moved=12 * 2**20, limit=ENTRY_LIMIT,
    )
    from_left_on, from_right_on = shifted(right_on, True, 1), shifted(left_on, True, -1)

    first, small = call(first_kernel, [((rows, width), F32), ((rows, width), BF16)], (head_grad, weights[0]), whole(2), **matmul)
    shard = lax.ppermute(small, "section", [(1, 0)])
    staying_right, staying_left, shard = lax.optimization_barrier((right, left, shard))
    from_left, from_right = shifted(staying_right, True, 1), shifted(staying_left, True, -1)
    places = range(RING)
    both = jnp.where(on_last(), small, shard)
    passed = on_line(both, [((0, i), (0, i - 1)) for i in places] + [((1, i), (1, i + 1)) for i in places])
    passed, from_left_on, from_right_on = lax.optimization_barrier((passed, from_left_on, from_right_on))
    upper = shifted(from_left_on, True, 1)
    behind_two = on_line(passed, [((1, i), (0, i + 1)) for i in places])
    passed, behind_two = lax.optimization_barrier((passed, behind_two))
    behind = on_line(passed, [((1, i), (0, i)) for i in places])
    lower = shifted(from_right_on, True, -1)
    rel = [shard, behind, behind_two, passed]
    rel = jnp.stack(rel, 0)

    edge = ((2 * rows, lanes), BF16)
    last_right, last_left, last_own, last_two = call(
        pack_last_kernel, [edge] * 4, (head_grad, rel), whole(2), moved=4 * 2**20
    )
    last = [shifted(last_two, True, 2), shifted(last_right, True, 1), shifted(last_left, True, -1), last_own]
    (acc,) = call(
        early_kernel, [((width, 2 * lanes), F32)], (right_on, right, own, from_left_on, from_left, from_right_on, from_right), whole(7),
        flops=2 * width * 2 * lanes * 3 * depth, moved=12 * 2**20,
    )
    acc, upper, lower, *last = lax.optimization_barrier((acc, upper, lower, *last))
    send = ((width + TAIL, LANES), F32)

    def late(z):
        return call(
            functools.partial(late_kernel, z), [((width, LANES), F32)] + [send] * 3,
            (acc, right_on, right, from_left_on, from_left, from_right_on, from_right, upper, lower, *last), whole(13),
            scratch=[pltpu.VMEM((width, lanes), F32)],
            flops=2 * width * lanes * (3 * rows + micro * rows), moved=8 * 2**20,
        )

    keep_far, *far_sends = late(1)
    keep_near, *near_sends = late(0)
    sends = far_sends + near_sends
    got = [shifted(sends[i].astype(F16), False, 1 + i % 3) for i in (1, 0, 2, 4, 3, 5)]
    rel, *got[:3] = lax.optimization_barrier((rel, *got[:3]))
    got = [v.astype(F32) for v in got]
    (second,) = call(second_kernel, [((rows, width), F32)], (rel, first, weights[0]), whole(3), **matmul)
    (far,) = call(far_kernel, [send], (keep_far, *got[:3]), whole(4), moved=4 * 2**20)
    other = lax.ppermute(far.astype(F16), "z_hi", [(0, 1), (1, 0)]).astype(F32)
    (block,) = call(near_kernel, [((width, LANES), F32)], (keep_near, *got[3:], other), whole(5), moved=4 * 2**20)
    return (second[None], block[None])


def solution(mesh):
    fine = Mesh(mesh.devices.reshape(2, 4, 2, 4, 4), ("section", "z_lo", "z_hi", "y", "x"))
    dp = ("z_hi", "y", "x")
    return jax.shard_map(
        local,
        mesh=fine,
        in_specs=(
            P("section", "z_lo", None),
            P("section", None, dp, "z_lo"),
            P("section", None, dp, None),
            P(dp, None),
            P(),
        ),
        out_specs=(P("section", dp, "z_lo"), P("section", "z_lo", dp)),
        check_vma=False,
    )
```

```python
import functools

import jax
import jax.numpy as jnp
from jax import lax
from jax.experimental import pallas as pl
from jax.experimental.pallas import tpu as pltpu
from jax.sharding import Mesh
from jax.sharding import PartitionSpec as P

F32 = jnp.float32
F16 = jnp.float16
BF16 = jnp.bfloat16
RING = 4
LANES = 128
TAIL = 16
TOP = 15
TINY = 1e-30
ENTRY_LIMIT = 26
ENTRY_FLOPS = 10**10


def section():
    return lax.axis_index("section")


def on_last():
    return section() == lax.axis_size("section") - 1


def block_start(z_off, along, across):
    first = section() == 0
    y_off, x_off = jnp.where(first, across, along), jnp.where(first, along, across)
    z = lax.rem(lax.axis_index("z_hi") + z_off, 2)
    y = lax.rem(lax.axis_index("y") + y_off, RING)
    x = lax.rem(lax.axis_index("x") + x_off, RING)
    return pl.multiple_of((z * (RING * RING) + y * RING + x) * LANES, LANES)


def pairs_over(along, by):
    size, pairs = RING * RING, []
    for s in range(2):
        for y in range(RING):
            for x in range(RING):
                on_x = (s == 0) == along
                there = (y, (x + by) % RING) if on_x else ((y + by) % RING, x)
                pairs.append((s * size + y * RING + x, s * size + there[0] * RING + there[1]))
    return pairs


def shifted(value, along, by):
    return lax.ppermute(value, ("section", "y", "x"), pairs_over(along, by))


def whole(n=1):
    return [pl.BlockSpec(memory_space=pltpu.VMEM)] * n


def in_hbm(value):
    return pltpu.with_memory_space_constraint(value, pltpu.HBM)


def call(kernel, out_shapes, operands, specs, scratch=(), flops=0, moved=0, limit=20):
    return pl.pallas_call(
        kernel,
        out_shape=[jax.ShapeDtypeStruct(s, t) for s, t in out_shapes],
        in_specs=specs,
        out_specs=whole(len(out_shapes)),
        scratch_shapes=list(scratch),
        compiler_params=pltpu.CompilerParams(vmem_limit_bytes=limit * 2**20),
        cost_estimate=pl.CostEstimate(flops=flops, bytes_accessed=moved, transcendentals=0),
    )(*operands)


CONTRACT_LAST = (((1,), (1,)), ((), ()))


def entry_kernel(pending_ref, x_ref, stash_ref, right_on, left_on, right_ref, left_ref, own_ref, x_in, stash_in, count_in, sems):
    micro, rows, width = x_ref.shape
    half, depth = width // 2, (micro - 1) * rows
    pieces = [(pending_ref, count_in), (x_ref, x_in)]
    pieces += [(stash_ref.at[m], stash_in.at[m]) for m in range(micro - 1)]
    copies = [pltpu.make_async_copy(a, b, sems.at[i]) for i, (a, b) in enumerate(pieces)]
    for copy in copies:
        copy.start()
    copies[0].wait()
    copies[1].wait()
    count = count_in[section()]
    for m in range(micro):
        turned = jnp.where(m >= micro - count, x_in[m].astype(F32), 0.0).T.astype(BF16)
        lanes = slice(m * rows, (m + 1) * rows)
        for out, top in ((right_on, 0), (right_ref, half), (left_on, half), (left_ref, 0)):
            out[:half, lanes] = turned[top:top + half]
    share = depth // 2
    plans = []
    for z in range(2):
        at = half + z * share
        plans += [(right_on, at, z, 2, 0, share), (left_on, at, z, 2, share, depth)]
        at = half + z * depth
        plans += [(right_ref, at, z, 1, 0, depth), (left_ref, at, z, RING - 1, 0, depth), (own_ref, z * depth, z, 0, 0, depth)]
    for m in range(micro - 1):
        copies[2 + m].wait()
        for out, base, z, along, begin, end in plans:
            begin_m, end_m = max(begin, m * rows), min(end, (m + 1) * rows)
            if begin_m >= end_m:
                continue
            for b in range(RING):
                source = stash_in[m, begin_m - m * rows:end_m - m * rows, pl.ds(block_start(z, along, b), LANES)]
                out[base + begin_m - begin:base + end_m - begin, b * LANES:(b + 1) * LANES] = source


def first_kernel(grad_ref, weight_ref, out_ref, small_ref):
    step = 256
    for i in range(0, weight_ref.shape[0], step):
        out = lax.dot_general(grad_ref[...], weight_ref[i:i + step, :], CONTRACT_LAST, preferred_element_type=F32)
        out_ref[:, i:i + step] = out
        small_ref[:, i:i + step] = jnp.where(on_last(), out, 0.0).astype(BF16)


def second_kernel(rel_ref, first_ref, weight_ref, out_ref):
    step, share = 256, rel_ref.shape[2]
    tensor = lax.axis_index("z_lo")
    for i in range(0, weight_ref.shape[0], step):
        total = jnp.zeros((rel_ref.shape[1], step), F32)
        for k in range(RING):
            owner = lax.rem(tensor - k + RING, RING)
            cols = weight_ref[i:i + step, pl.ds(pl.multiple_of(owner * share, share), share)]
            total = total + lax.dot_general(rel_ref[k], cols, CONTRACT_LAST, preferred_element_type=F32)
        out_ref[:, i:i + step] = jnp.where(on_last(), first_ref[:, i:i + step], total)


def pack_last_kernel(head_ref, rel_ref, right_ref, left_ref, own_ref, two_ref):
    tensor = lax.axis_index("z_lo")
    rows, share = rel_ref.shape[1], rel_ref.shape[2]
    for z in range(2):
        for b in range(RING):
            for out, along in ((right_ref, 1), (left_ref, RING - 1), (own_ref, 0), (two_ref, 2)):
                at = block_start(z, along, b)
                inner = pl.multiple_of(lax.rem(at, share), LANES)
                chained = rel_ref[lax.rem(tensor - lax.div(at, share) + RING, RING), :, pl.ds(inner, LANES)]
                last = jnp.where(on_last(), head_ref[:, pl.ds(at, LANES)], chained)
                out[z * rows:(z + 1) * rows, b * LANES:(b + 1) * LANES] = last


def early_kernel(mine_on, mine_ref, own_ref, left_on, left_ref, right_on, right_ref, acc_ref):
    width, depth = acc_ref.shape[0], own_ref.shape[0] // 2
    half, lanes = width // 2, acc_ref.shape[1] // 2
    sides = [(mine_on, mine_ref), (left_on, left_ref), (right_ref, right_on)]
    for r in range(2):
        lhs = jnp.concatenate([side[r][:half, :depth] for side in sides], axis=1)
        for z in range(2):
            at = half + z * depth
            rhs = [own_ref[z * depth:(z + 1) * depth, :], left_ref[at:at + depth, :], right_ref[at:at + depth, :]]
            rhs = jnp.concatenate(rhs, axis=0)
            acc_ref[r * half:(r + 1) * half, z * lanes:(z + 1) * lanes] = jnp.dot(lhs, rhs, preferred_element_type=F32)


def late_kernel(z, acc_ref, mine_on, mine_ref, left_on, left_ref, right_on, right_ref, upper_ref, lower_ref,
                two_last, left_last, right_last, own_last, keep_ref, *rest):
    sends, sum_ref = rest[:-1], rest[-1]
    width, rows = acc_ref.shape[0], own_last.shape[0] // 2
    half, lanes = width // 2, acc_ref.shape[1] // 2
    depth = mine_ref.shape[1] - rows
    mine, left, right, far = (mine_on, mine_ref), (left_on, left_ref), (right_ref, right_on), (upper_ref, lower_ref)
    rhs = [ref[z * rows:(z + 1) * rows, :] for ref in (own_last, left_last, right_last, two_last)]
    at = half + z * depth // 2
    rhs += [ref[at:at + depth // 2, :] for ref in far]
    rhs = jnp.concatenate(rhs, axis=0)
    largest = jnp.full((1, lanes), TINY, F32)
    for r in range(2):
        lhs = [side[r][:half, depth:] for side in (mine, left, right, far)] + [far[r][:half, :depth]]
        total = jnp.dot(jnp.concatenate(lhs, axis=1), rhs, preferred_element_type=F32)
        total = total + acc_ref[r * half:(r + 1) * half, z * lanes:(z + 1) * lanes]
        largest = jnp.maximum(largest, jnp.max(jnp.abs(total), axis=0, keepdims=True))
        sum_ref[r * half:(r + 1) * half, :] = total
    power = jnp.ceil(jnp.log2(jnp.max(largest, axis=1, keepdims=True))) - TOP
    power = jnp.broadcast_to(power, (1, LANES))
    factor = jnp.exp2(-power)
    keep_ref[...] = sum_ref[:, :LANES]
    for b, out in enumerate(sends, 1):
        out[:width, :] = sum_ref[:, b * LANES:(b + 1) * LANES] * factor
        out[width:, :] = jnp.broadcast_to(power, (TAIL, LANES))


def summed(keep_ref, refs):
    rows = keep_ref.shape[0]
    total = keep_ref[...]
    for ref in refs:
        total = total + ref[:rows, :] * jnp.exp2(ref[rows:rows + 1, :])
    return total


def far_kernel(keep_ref, one_ref, two_ref, three_ref, out_ref):
    rows = keep_ref.shape[0]
    total = summed(keep_ref, (one_ref, two_ref, three_ref))
    largest = jnp.maximum(jnp.max(jnp.abs(total), axis=0, keepdims=True), TINY)
    power = jnp.ceil(jnp.log2(jnp.max(largest, axis=1, keepdims=True))) - TOP
    power = jnp.broadcast_to(power, (1, LANES))
    out_ref[:rows, :] = total * jnp.exp2(-power)
    out_ref[rows:, :] = jnp.broadcast_to(power, (TAIL, LANES))


def near_kernel(keep_ref, one_ref, two_ref, three_ref, other_ref, out_ref):
    out_ref[...] = summed(keep_ref, (one_ref, two_ref, three_ref, other_ref))


def on_line(value, pairs):
    pairs = [(s * RING + i, t * RING + j % RING) for (s, i), (t, j) in pairs]
    return lax.ppermute(value, ("section", "z_lo"), pairs)


def local(weights, stash_in, stash_grad, head_grad, pending):
    inputs, grads = stash_in[0], stash_grad[0]
    micro, rows, width = inputs.shape
    depth, half, lanes = (micro - 1) * rows, width // 2, RING * LANES
    columns = head_grad.shape[1]
    matmul = dict(flops=2 * rows * width * columns, moved=2 * 2**20)

    going, staying = ((half + depth, lanes), BF16), ((half + 2 * depth, lanes), BF16)
    right_on, left_on, right, left, own = call(
        entry_kernel, [going, going, staying, staying, ((2 * depth, lanes), BF16)],
        [in_hbm(v) for v in (pending, inputs, grads)], [pl.BlockSpec(memory_space=pltpu.HBM)] * 3,
        scratch=[pltpu.VMEM(inputs.shape, BF16), pltpu.VMEM(grads.shape, BF16), pltpu.SMEM(pending.shape, pending.dtype),
                 pltpu.SemaphoreType.DMA((micro + 6,))],
        flops=ENTRY_FLOPS, moved=12 * 2**20, limit=ENTRY_LIMIT,
    )
    from_left_on, from_right_on = shifted(right_on, True, 1), shifted(left_on, True, -1)

    first, small = call(first_kernel, [((rows, width), F32), ((rows, width), BF16)], (head_grad, weights[0]), whole(2), **matmul)
    shard = lax.ppermute(small, "section", [(1, 0)])
    staying_right, staying_left, shard = lax.optimization_barrier((right, left, shard))
    from_left, from_right = shifted(staying_right, True, 1), shifted(staying_left, True, -1)
    places = range(RING)
    both = small + shard
    passed = on_line(both, [((0, i), (0, i - 1)) for i in places] + [((1, i), (1, i + 1)) for i in places])
    passed, from_left_on, from_right_on = lax.optimization_barrier((passed, from_left_on, from_right_on))
    upper = shifted(from_left_on, True, 1)
    behind_two = on_line(passed, [((1, i), (0, i + 1)) for i in places])
    passed, behind_two = lax.optimization_barrier((passed, behind_two))
    behind = on_line(passed, [((1, i), (0, i)) for i in places])
    lower = shifted(from_right_on, True, -1)
    rel = [shard, behind, behind_two, passed]
    rel = jnp.stack(rel, 0)

    edge = ((2 * rows, lanes), BF16)
    last_right, last_left, last_own, last_two = call(
        pack_last_kernel, [edge] * 4, (head_grad, rel), whole(2), moved=4 * 2**20
    )
    last = [shifted(last_two, True, 2), shifted(last_right, True, 1), shifted(last_left, True, -1), last_own]
    (acc,) = call(
        early_kernel, [((width, 2 * lanes), F32)], (right_on, right, own, from_left_on, from_left, from_right_on, from_right), whole(7),
        flops=2 * width * 2 * lanes * 3 * depth, moved=12 * 2**20,
    )
    acc, upper, lower, *last = lax.optimization_barrier((acc, upper, lower, *last))
    send = ((width + TAIL, LANES), F32)

    def late(z):
        return call(
            functools.partial(late_kernel, z), [((width, LANES), F32)] + [send] * 3,
            (acc, right_on, right, from_left_on, from_left, from_right_on, from_right, upper, lower, *last), whole(13),
            scratch=[pltpu.VMEM((width, lanes), F32)],
            flops=2 * width * lanes * (3 * rows + micro * rows), moved=8 * 2**20,
        )

    keep_far, *far_sends = late(1)
    keep_near, *near_sends = late(0)
    sends = far_sends + near_sends
    got = [shifted(sends[i].astype(F16), False, 1 + i % 3) for i in (1, 0, 2, 4, 3, 5)]
    rel, *got[:3] = lax.optimization_barrier((rel, *got[:3]))
    got = [v.astype(F32) for v in got]
    (second,) = call(second_kernel, [((rows, width), F32)], (rel, first, weights[0]), whole(3), **matmul)
    (far,) = call(far_kernel, [send], (keep_far, *got[:3]), whole(4), moved=4 * 2**20)
    other = lax.ppermute(far.astype(F16), "z_hi", [(0, 1), (1, 0)]).astype(F32)
    (block,) = call(near_kernel, [((width, LANES), F32)], (keep_near, *got[3:], other), whole(5), moved=4 * 2**20)
    return (second[None], block[None])


def solution(mesh):
    fine = Mesh(mesh.devices.reshape(2, 4, 2, 4, 4), ("section", "z_lo", "z_hi", "y", "x"))
    dp = ("z_hi", "y", "x")
    return jax.shard_map(
        local,
        mesh=fine,
        in_specs=(
            P("section", "z_lo", None),
            P("section", None, dp, "z_lo"),
            P("section", None, dp, None),
            P(dp, None),
            P(),
        ),
        out_specs=(P("section", dp, "z_lo"), P("section", "z_lo", dp)),
        check_vma=False,
    )
```

```python
import functools

import jax
import jax.numpy as jnp
from jax import lax
from jax.experimental import pallas as pl
from jax.experimental.pallas import tpu as pltpu
from jax.sharding import Mesh
from jax.sharding import PartitionSpec as P

F32 = jnp.float32
F16 = jnp.float16
BF16 = jnp.bfloat16
RING = 4
LANES = 128
TAIL = 16
TOP = 15
TINY = 1e-30
ENTRY_LIMIT = 26
ENTRY_FLOPS = 10**10


def section():
    return lax.axis_index("section")


def on_last():
    return section() == lax.axis_size("section") - 1


def block_start(z_off, along, across):
    first = section() == 0
    y_off, x_off = jnp.where(first, across, along), jnp.where(first, along, across)
    z = lax.rem(lax.axis_index("z_hi") + z_off, 2)
    y = lax.rem(lax.axis_index("y") + y_off, RING)
    x = lax.rem(lax.axis_index("x") + x_off, RING)
    return pl.multiple_of((z * (RING * RING) + y * RING + x) * LANES, LANES)


def pairs_over(along, by):
    size, pairs = RING * RING, []
    for s in range(2):
        for y in range(RING):
            for x in range(RING):
                on_x = (s == 0) == along
                there = (y, (x + by) % RING) if on_x else ((y + by) % RING, x)
                pairs.append((s * size + y * RING + x, s * size + there[0] * RING + there[1]))
    return pairs


def shifted(value, along, by):
    return lax.ppermute(value, ("section", "y", "x"), pairs_over(along, by))


def whole(n=1):
    return [pl.BlockSpec(memory_space=pltpu.VMEM)] * n


def in_hbm(value):
    return pltpu.with_memory_space_constraint(value, pltpu.HBM)


def call(kernel, out_shapes, operands, specs, scratch=(), flops=0, moved=0, limit=20):
    return pl.pallas_call(
        kernel,
        out_shape=[jax.ShapeDtypeStruct(s, t) for s, t in out_shapes],
        in_specs=specs,
        out_specs=whole(len(out_shapes)),
        scratch_shapes=list(scratch),
        compiler_params=pltpu.CompilerParams(vmem_limit_bytes=limit * 2**20),
        cost_estimate=pl.CostEstimate(flops=flops, bytes_accessed=moved, transcendentals=0),
    )(*operands)


CONTRACT_LAST = (((1,), (1,)), ((), ()))


def entry_kernel(pending_ref, x_ref, stash_ref, right_on, left_on, right_ref, left_ref, own_ref, x_in, stash_in, count_in, sems):
    micro, rows, width = x_ref.shape
    half, depth = width // 2, (micro - 1) * rows
    pieces = [(pending_ref, count_in), (x_ref, x_in)]
    pieces += [(stash_ref.at[m], stash_in.at[m]) for m in range(micro - 1)]
    copies = [pltpu.make_async_copy(a, b, sems.at[i]) for i, (a, b) in enumerate(pieces)]
    for copy in copies:
        copy.start()
    copies[0].wait()
    copies[1].wait()
    count = count_in[section()]
    for m in range(micro):
        turned = jnp.where(m >= micro - count, x_in[m].astype(F32), 0.0).T.astype(BF16)
        lanes = slice(m * rows, (m + 1) * rows)
        for out, top in ((right_on, 0), (right_ref, half), (left_on, half), (left_ref, 0)):
            out[:half, lanes] = turned[top:top + half]
    share = depth // 2
    plans = []
    for z in range(2):
        at = half + z * share
        plans += [(right_on, at, z, 2, 0, share), (left_on, at, z, 2, share, depth)]
        at = half + z * depth
        plans += [(right_ref, at, z, 1, 0, depth), (left_ref, at, z, RING - 1, 0, depth), (own_ref, z * depth, z, 0, 0, depth)]
    for m in range(micro - 1):
        copies[2 + m].wait()
        for out, base, z, along, begin, end in plans:
            begin_m, end_m = max(begin, m * rows), min(end, (m + 1) * rows)
            if begin_m >= end_m:
                continue
            for b in range(RING):
                source = stash_in[m, begin_m - m * rows:end_m - m * rows, pl.ds(block_start(z, along, b), LANES)]
                out[base + begin_m - begin:base + end_m - begin, b * LANES:(b + 1) * LANES] = source


def first_kernel(grad_ref, weight_ref, out_ref, small_ref):
    step = 256
    for i in range(0, weight_ref.shape[0], step):
        out = lax.dot_general(grad_ref[...], weight_ref[i:i + step, :], CONTRACT_LAST, preferred_element_type=F32)
        out_ref[:, i:i + step] = out
        small_ref[:, i:i + step] = jnp.where(on_last(), out, 0.0).astype(BF16)


def second_kernel(rel_ref, first_ref, weight_ref, out_ref):
    step, share = 256, rel_ref.shape[2]
    tensor = lax.axis_index("z_lo")
    for i in range(0, weight_ref.shape[0], step):
        total = jnp.zeros((rel_ref.shape[1], step), F32)
        for k in range(RING):
            owner = lax.rem(tensor - k + RING, RING)
            cols = weight_ref[i:i + step, pl.ds(pl.multiple_of(owner * share, share), share)]
            total = total + lax.dot_general(rel_ref[k], cols, CONTRACT_LAST, preferred_element_type=F32)
        out_ref[:, i:i + step] = jnp.where(on_last(), first_ref[:, i:i + step], total)


def pack_last_kernel(head_ref, rel_ref, right_ref, left_ref, own_ref, two_ref):
    tensor = lax.axis_index("z_lo")
    rows, share = rel_ref.shape[1], rel_ref.shape[2]
    for z in range(2):
        for b in range(RING):
            for out, along in ((right_ref, 1), (left_ref, RING - 1), (own_ref, 0), (two_ref, 2)):
                at = block_start(z, along, b)
                inner = pl.multiple_of(lax.rem(at, share), LANES)
                chained = rel_ref[lax.rem(tensor - lax.div(at, share) + RING, RING), :, pl.ds(inner, LANES)]
                last = jnp.where(on_last(), head_ref[:, pl.ds(at, LANES)], chained)
                out[z * rows:(z + 1) * rows, b * LANES:(b + 1) * LANES] = last


def early_kernel(mine_on, mine_ref, own_ref, left_on, left_ref, right_on, right_ref, acc_ref):
    width, depth = acc_ref.shape[0], own_ref.shape[0] // 2
    half, lanes = width // 2, acc_ref.shape[1] // 2
    sides = [(mine_on, mine_ref), (left_on, left_ref), (right_ref, right_on)]
    for r in range(2):
        lhs = jnp.concatenate([side[r][:half, :depth] for side in sides], axis=1)
        for z in range(2):
            at = half + z * depth
            rhs = [own_ref[z * depth:(z + 1) * depth, :], left_ref[at:at + depth, :], right_ref[at:at + depth, :]]
            rhs = jnp.concatenate(rhs, axis=0)
            acc_ref[r * half:(r + 1) * half, z * lanes:(z + 1) * lanes] = jnp.dot(lhs, rhs, preferred_element_type=F32)


def late_kernel(z, acc_ref, mine_on, mine_ref, left_on, left_ref, right_on, right_ref, upper_ref, lower_ref,
                two_last, left_last, right_last, own_last, keep_ref, *rest):
    sends, sum_ref = rest[:-1], rest[-1]
    width, rows = acc_ref.shape[0], own_last.shape[0] // 2
    half, lanes = width // 2, acc_ref.shape[1] // 2
    depth = mine_ref.shape[1] - rows
    mine, left, right, far = (mine_on, mine_ref), (left_on, left_ref), (right_ref, right_on), (upper_ref, lower_ref)
    rhs = [ref[z * rows:(z + 1) * rows, :] for ref in (own_last, left_last, right_last, two_last)]
    at = half + z * depth // 2
    rhs += [ref[at:at + depth // 2, :] for ref in far]
    rhs = jnp.concatenate(rhs, axis=0)
    largest = jnp.full((1, lanes), TINY, F32)
    for r in range(2):
        lhs = [side[r][:half, depth:] for side in (mine, left, right, far)] + [far[r][:half, :depth]]
        total = jnp.dot(jnp.concatenate(lhs, axis=1), rhs, preferred_element_type=F32)
        total = total + acc_ref[r * half:(r + 1) * half, z * lanes:(z + 1) * lanes]
        largest = jnp.maximum(largest, jnp.max(jnp.abs(total), axis=0, keepdims=True))
        sum_ref[r * half:(r + 1) * half, :] = total
    power = jnp.ceil(jnp.log2(jnp.max(largest, axis=1, keepdims=True))) - TOP
    power = jnp.broadcast_to(power, (1, LANES))
    factor = jnp.exp2(-power)
    keep_ref[...] = sum_ref[:, :LANES]
    for b, out in enumerate(sends, 1):
        out[:width, :] = sum_ref[:, b * LANES:(b + 1) * LANES] * factor
        out[width:, :] = jnp.broadcast_to(power, (TAIL, LANES))


def summed(keep_ref, refs):
    rows = keep_ref.shape[0]
    total = keep_ref[...]
    for ref in refs:
        total = total + ref[:rows, :] * jnp.exp2(ref[rows:rows + 1, :])
    return total


def far_kernel(keep_ref, one_ref, two_ref, three_ref, out_ref):
    rows = keep_ref.shape[0]
    total = summed(keep_ref, (one_ref, two_ref, three_ref))
    largest = jnp.maximum(jnp.max(jnp.abs(total), axis=0, keepdims=True), TINY)
    power = jnp.ceil(jnp.log2(jnp.max(largest, axis=1, keepdims=True))) - TOP
    power = jnp.broadcast_to(power, (1, LANES))
    out_ref[:rows, :] = total * jnp.exp2(-power)
    out_ref[rows:, :] = jnp.broadcast_to(power, (TAIL, LANES))


def near_kernel(keep_ref, *rest):
    rest[-1][...] = summed(keep_ref, rest[:-1])


def on_line(value, pairs):
    pairs = [(s * RING + i, t * RING + j % RING) for (s, i), (t, j) in pairs]
    return lax.ppermute(value, ("section", "z_lo"), pairs)


def local(weights, stash_in, stash_grad, head_grad, pending):
    inputs, grads = stash_in[0], stash_grad[0]
    micro, rows, width = inputs.shape
    depth, half, lanes = (micro - 1) * rows, width // 2, RING * LANES
    columns = head_grad.shape[1]
    matmul = dict(flops=2 * rows * width * columns, moved=2 * 2**20)

    going, staying = ((half + depth, lanes), BF16), ((half + 2 * depth, lanes), BF16)
    right_on, left_on, right, left, own = call(
        entry_kernel, [going, going, staying, staying, ((2 * depth, lanes), BF16)],
        [in_hbm(v) for v in (pending, inputs, grads)], [pl.BlockSpec(memory_space=pltpu.HBM)] * 3,
        scratch=[pltpu.VMEM(inputs.shape, BF16), pltpu.VMEM(grads.shape, BF16), pltpu.SMEM(pending.shape, pending.dtype),
                 pltpu.SemaphoreType.DMA((micro + 6,))],
        flops=ENTRY_FLOPS, moved=12 * 2**20, limit=ENTRY_LIMIT,
    )
    from_left_on, from_right_on = shifted(right_on, True, 1), shifted(left_on, True, -1)

    first, small = call(first_kernel, [((rows, width), F32), ((rows, width), BF16)], (head_grad, weights[0]), whole(2), **matmul)
    shard = lax.ppermute(small, "section", [(1, 0)])
    staying_right, staying_left, shard = lax.optimization_barrier((right, left, shard))
    from_left, from_right = shifted(staying_right, True, 1), shifted(staying_left, True, -1)
    places = range(RING)
    both = small + shard
    passed = on_line(both, [((0, i), (0, i - 1)) for i in places] + [((1, i), (1, i + 1)) for i in places])
    passed, from_left_on, from_right_on = lax.optimization_barrier((passed, from_left_on, from_right_on))
    upper = shifted(from_left_on, True, 1)
    behind_two = on_line(passed, [((1, i), (0, i + 1)) for i in places])
    passed, behind_two = lax.optimization_barrier((passed, behind_two))
    behind = on_line(passed, [((1, i), (0, i)) for i in places])
    lower = shifted(from_right_on, True, -1)
    rel = [shard, behind, behind_two, passed]
    rel = jnp.stack(rel, 0)

    edge = ((2 * rows, lanes), BF16)
    last_right, last_left, last_own, last_two = call(
        pack_last_kernel, [edge] * 4, (head_grad, rel), whole(2), moved=4 * 2**20
    )
    last = [shifted(last_two, True, 2), shifted(last_right, True, 1), shifted(last_left, True, -1), last_own]
    (acc,) = call(
        early_kernel, [((width, 2 * lanes), F32)], (right_on, right, own, from_left_on, from_left, from_right_on, from_right), whole(7),
        flops=2 * width * 2 * lanes * 3 * depth, moved=12 * 2**20,
    )
    acc, upper, lower, *last = lax.optimization_barrier((acc, upper, lower, *last))
    send = ((width + TAIL, LANES), F32)

    def late(z):
        return call(
            functools.partial(late_kernel, z), [((width, LANES), F32)] + [send] * 3,
            (acc, right_on, right, from_left_on, from_left, from_right_on, from_right, upper, lower, *last), whole(13),
            scratch=[pltpu.VMEM((width, lanes), F32)],
            flops=2 * width * lanes * (3 * rows + micro * rows), moved=8 * 2**20,
        )

    keep_far, *far_sends = late(1)
    keep_near, *near_sends = late(0)
    sends = far_sends + near_sends
    got = [shifted(sends[i].astype(F16), False, 1 + i % 3) for i in (1, 0, 2, 4, 3)]
    rel, *got[:3] = lax.optimization_barrier((rel, *got[:3]))
    (far,) = call(far_kernel, [send], (keep_far, *[v.astype(F32) for v in got[:3]]), whole(4), moved=4 * 2**20)
    far, final = lax.optimization_barrier((far.astype(F16), sends[5].astype(F16)))
    other = lax.ppermute(far, "z_hi", [(0, 1), (1, 0)])
    (second,) = call(second_kernel, [((rows, width), F32)], (rel, first, weights[0]), whole(3), **matmul)
    got = [v.astype(F32) for v in (*got[3:], shifted(final, False, 3))]
    (block,) = call(near_kernel, [((width, LANES), F32)], (keep_near, other.astype(F32), *got), whole(5), moved=4 * 2**20)
    return (second[None], block[None])


def solution(mesh):
    fine = Mesh(mesh.devices.reshape(2, 4, 2, 4, 4), ("section", "z_lo", "z_hi", "y", "x"))
    dp = ("z_hi", "y", "x")
    return jax.shard_map(
        local,
        mesh=fine,
        in_specs=(
            P("section", "z_lo", None),
            P("section", None, dp, "z_lo"),
            P("section", None, dp, None),
            P(dp, None),
            P(),
        ),
        out_specs=(P("section", dp, "z_lo"), P("section", "z_lo", dp)),
        check_vma=False,
    )
```

```python
import functools

import jax
import jax.numpy as jnp
from jax import lax
from jax.experimental import pallas as pl
from jax.experimental.pallas import tpu as pltpu
from jax.sharding import Mesh
from jax.sharding import PartitionSpec as P

F32 = jnp.float32
F16 = jnp.float16
BF16 = jnp.bfloat16
RING = 4
LANES = 128
TAIL = 16
TOP = 15
TINY = 1e-30
ENTRY_LIMIT = 26
ENTRY_FLOPS = 10**10


def section():
    return lax.axis_index("section")


def on_last():
    return section() == lax.axis_size("section") - 1


def block_start(z_off, along, across):
    first = section() == 0
    y_off, x_off = jnp.where(first, across, along), jnp.where(first, along, across)
    z = lax.rem(lax.axis_index("z_hi") + z_off, 2)
    y = lax.rem(lax.axis_index("y") + y_off, RING)
    x = lax.rem(lax.axis_index("x") + x_off, RING)
    return pl.multiple_of((z * (RING * RING) + y * RING + x) * LANES, LANES)


def pairs_over(along, by):
    size, pairs = RING * RING, []
    for s in range(2):
        for y in range(RING):
            for x in range(RING):
                on_x = (s == 0) == along
                there = (y, (x + by) % RING) if on_x else ((y + by) % RING, x)
                pairs.append((s * size + y * RING + x, s * size + there[0] * RING + there[1]))
    return pairs


def shifted(value, along, by):
    return lax.ppermute(value, ("section", "y", "x"), pairs_over(along, by))


def whole(n=1):
    return [pl.BlockSpec(memory_space=pltpu.VMEM)] * n


def in_hbm(value):
    return pltpu.with_memory_space_constraint(value, pltpu.HBM)


def call(kernel, out_shapes, operands, specs, scratch=(), flops=0, moved=0, limit=20):
    return pl.pallas_call(
        kernel,
        out_shape=[jax.ShapeDtypeStruct(s, t) for s, t in out_shapes],
        in_specs=specs,
        out_specs=whole(len(out_shapes)),
        scratch_shapes=list(scratch),
        compiler_params=pltpu.CompilerParams(vmem_limit_bytes=limit * 2**20),
        cost_estimate=pl.CostEstimate(flops=flops, bytes_accessed=moved, transcendentals=0),
    )(*operands)


CONTRACT_LAST = (((1,), (1,)), ((), ()))


def entry_kernel(pending_ref, x_ref, stash_ref, right_on, left_on, right_ref, left_ref, own_ref, x_in, stash_in, count_in, sems):
    micro, rows, width = x_ref.shape
    half, depth = width // 2, (micro - 1) * rows
    pieces = [(pending_ref, count_in), (x_ref, x_in)]
    pieces += [(stash_ref.at[m], stash_in.at[m]) for m in range(micro - 1)]
    copies = [pltpu.make_async_copy(a, b, sems.at[i]) for i, (a, b) in enumerate(pieces)]
    for copy in copies:
        copy.start()
    copies[0].wait()
    copies[1].wait()
    count = count_in[section()]
    for m in range(micro):
        turned = jnp.where(m >= micro - count, x_in[m].astype(F32), 0.0).T.astype(BF16)
        lanes = slice(m * rows, (m + 1) * rows)
        for out, top in ((right_on, 0), (right_ref, half), (left_on, half), (left_ref, 0)):
            out[:half, lanes] = turned[top:top + half]
    share = depth // 2
    plans = []
    for z in range(2):
        at = half + z * share
        plans += [(right_on, at, z, 2, 0, share), (left_on, at, z, 2, share, depth)]
        at = half + z * depth
        plans += [(right_ref, at, z, 1, 0, depth), (left_ref, at, z, RING - 1, 0, depth), (own_ref, z * depth, z, 0, 0, depth)]
    for m in range(micro - 1):
        copies[2 + m].wait()
        for out, base, z, along, begin, end in plans:
            begin_m, end_m = max(begin, m * rows), min(end, (m + 1) * rows)
            if begin_m >= end_m:
                continue
            for b in range(RING):
                source = stash_in[m, begin_m - m * rows:end_m - m * rows, pl.ds(block_start(z, along, b), LANES)]
                out[base + begin_m - begin:base + end_m - begin, b * LANES:(b + 1) * LANES] = source


def first_kernel(grad_ref, weight_ref, out_ref, small_ref):
    step = 256
    for i in range(0, weight_ref.shape[0], step):
        out = lax.dot_general(grad_ref[...], weight_ref[i:i + step, :], CONTRACT_LAST, preferred_element_type=F32)
        out_ref[:, i:i + step] = out
        small_ref[:, i:i + step] = jnp.where(on_last(), out, 0.0).astype(BF16)


def second_kernel(rel_ref, first_ref, weight_ref, out_ref):
    step, share = 256, rel_ref.shape[2]
    tensor = lax.axis_index("z_lo")
    for i in range(0, weight_ref.shape[0], step):
        total = jnp.zeros((rel_ref.shape[1], step), F32)
        for k in range(RING):
            owner = lax.rem(tensor - k + RING, RING)
            cols = weight_ref[i:i + step, pl.ds(pl.multiple_of(owner * share, share), share)]
            total = total + lax.dot_general(rel_ref[k], cols, CONTRACT_LAST, preferred_element_type=F32)
        out_ref[:, i:i + step] = jnp.where(on_last(), first_ref[:, i:i + step], total)


def pack_last_kernel(head_ref, rel_ref, right_ref, left_ref, own_ref, two_ref):
    tensor = lax.axis_index("z_lo")
    rows, share = rel_ref.shape[1], rel_ref.shape[2]
    for z in range(2):
        for b in range(RING):
            for out, along in ((right_ref, 1), (left_ref, RING - 1), (own_ref, 0), (two_ref, 2)):
                at = block_start(z, along, b)
                inner = pl.multiple_of(lax.rem(at, share), LANES)
                chained = rel_ref[lax.rem(tensor - lax.div(at, share) + RING, RING), :, pl.ds(inner, LANES)]
                last = jnp.where(on_last(), head_ref[:, pl.ds(at, LANES)], chained)
                out[z * rows:(z + 1) * rows, b * LANES:(b + 1) * LANES] = last


def early_kernel(mine_on, mine_ref, own_ref, left_on, left_ref, right_on, right_ref, acc_ref):
    width, depth = acc_ref.shape[0], own_ref.shape[0] // 2
    half, lanes = width // 2, acc_ref.shape[1] // 2
    sides = [(mine_on, mine_ref), (left_on, left_ref), (right_ref, right_on)]
    for r in range(2):
        lhs = jnp.concatenate([side[r][:half, :depth] for side in sides], axis=1)
        for z in range(2):
            at = half + z * depth
            rhs = [own_ref[z * depth:(z + 1) * depth, :], left_ref[at:at + depth, :], right_ref[at:at + depth, :]]
            rhs = jnp.concatenate(rhs, axis=0)
            acc_ref[r * half:(r + 1) * half, z * lanes:(z + 1) * lanes] = jnp.dot(lhs, rhs, preferred_element_type=F32)


def late_kernel(z, acc_ref, mine_on, mine_ref, left_on, left_ref, right_on, right_ref, upper_ref, lower_ref,
                two_last, left_last, right_last, own_last, keep_ref, *rest):
    sends, sum_ref = rest[:-1], rest[-1]
    width, rows = acc_ref.shape[0], own_last.shape[0] // 2
    half, lanes = width // 2, acc_ref.shape[1] // 2
    depth = mine_ref.shape[1] - rows
    mine, left, right, far = (mine_on, mine_ref), (left_on, left_ref), (right_ref, right_on), (upper_ref, lower_ref)
    rhs = [ref[z * rows:(z + 1) * rows, :] for ref in (own_last, left_last, right_last, two_last)]
    at = half + z * depth // 2
    rhs += [ref[at:at + depth // 2, :] for ref in far]
    rhs = jnp.concatenate(rhs, axis=0)
    largest = jnp.full((1, lanes), TINY, F32)
    for r in range(2):
        lhs = [side[r][:half, depth:] for side in (mine, left, right, far)] + [far[r][:half, :depth]]
        total = jnp.dot(jnp.concatenate(lhs, axis=1), rhs, preferred_element_type=F32)
        total = total + acc_ref[r * half:(r + 1) * half, z * lanes:(z + 1) * lanes]
        largest = jnp.maximum(largest, jnp.max(jnp.abs(total), axis=0, keepdims=True))
        sum_ref[r * half:(r + 1) * half, :] = total
    power = jnp.ceil(jnp.log2(jnp.max(largest, axis=1, keepdims=True))) - TOP
    power = jnp.broadcast_to(power, (1, LANES))
    factor = jnp.exp2(-power)
    keep_ref[...] = sum_ref[:, :LANES]
    for b, out in enumerate(sends, 1):
        out[:width, :] = sum_ref[:, b * LANES:(b + 1) * LANES] * factor
        out[width:, :] = jnp.broadcast_to(power, (TAIL, LANES))


def summed(keep_ref, refs):
    rows = keep_ref.shape[0]
    total = keep_ref[...]
    for ref in refs:
        total = total + ref[:rows, :] * jnp.exp2(ref[rows:rows + 1, :])
    return total


def far_kernel(keep_ref, one_ref, two_ref, three_ref, out_ref):
    rows = keep_ref.shape[0]
    total = summed(keep_ref, (one_ref, two_ref, three_ref))
    largest = jnp.maximum(jnp.max(jnp.abs(total), axis=0, keepdims=True), TINY)
    power = jnp.ceil(jnp.log2(jnp.max(largest, axis=1, keepdims=True))) - TOP
    power = jnp.broadcast_to(power, (1, LANES))
    out_ref[:rows, :] = total * jnp.exp2(-power)
    out_ref[rows:, :] = jnp.broadcast_to(power, (TAIL, LANES))


def near_kernel(keep_ref, *rest):
    rest[-1][...] = summed(keep_ref, rest[:-1])


def on_line(value, pairs):
    pairs = [(s * RING + i, t * RING + j % RING) for (s, i), (t, j) in pairs]
    return lax.ppermute(value, ("section", "z_lo"), pairs)


def local(weights, stash_in, stash_grad, head_grad, pending):
    inputs, grads = stash_in[0], stash_grad[0]
    micro, rows, width = inputs.shape
    depth, half, lanes = (micro - 1) * rows, width // 2, RING * LANES
    columns = head_grad.shape[1]
    matmul = dict(flops=2 * rows * width * columns, moved=2 * 2**20)

    going, staying = ((half + depth, lanes), BF16), ((half + 2 * depth, lanes), BF16)
    right_on, left_on, right, left, own = call(
        entry_kernel, [going, going, staying, staying, ((2 * depth, lanes), BF16)],
        [in_hbm(v) for v in (pending, inputs, grads)], [pl.BlockSpec(memory_space=pltpu.HBM)] * 3,
        scratch=[pltpu.VMEM(inputs.shape, BF16), pltpu.VMEM(grads.shape, BF16), pltpu.SMEM(pending.shape, pending.dtype),
                 pltpu.SemaphoreType.DMA((micro + 6,))],
        flops=ENTRY_FLOPS, moved=12 * 2**20, limit=ENTRY_LIMIT,
    )
    from_left_on, from_right_on = shifted(right_on, True, 1), shifted(left_on, True, -1)

    first, small = call(first_kernel, [((rows, width), F32), ((rows, width), BF16)], (head_grad, weights[0]), whole(2), **matmul)
    shard = lax.ppermute(small, "section", [(1, 0)])
    staying_right, staying_left, shard = lax.optimization_barrier((right, left, shard))
    from_left, from_right = shifted(staying_right, True, 1), shifted(staying_left, True, -1)
    places = range(RING)
    both = small + shard
    passed = on_line(both, [((0, i), (0, i - 1)) for i in places] + [((1, i), (1, i + 1)) for i in places])
    passed, from_left_on, from_right_on = lax.optimization_barrier((passed, from_left_on, from_right_on))
    upper = shifted(from_left_on, True, 1)
    behind_two = on_line(passed, [((1, i), (0, i + 1)) for i in places])
    passed, behind_two = lax.optimization_barrier((passed, behind_two))
    behind = on_line(passed, [((1, i), (0, i)) for i in places])
    lower = shifted(from_right_on, True, -1)
    rel = [shard, behind, behind_two, passed]
    rel = jnp.stack(rel, 0)

    edge = ((2 * rows, lanes), BF16)
    last_right, last_left, last_own, last_two = call(
        pack_last_kernel, [edge] * 4, (head_grad, rel), whole(2), moved=4 * 2**20
    )
    last = [shifted(last_two, True, 2), shifted(last_right, True, 1), shifted(last_left, True, -1), last_own]
    (acc,) = call(
        early_kernel, [((width, 2 * lanes), F32)], (right_on, right, own, from_left_on, from_left, from_right_on, from_right), whole(7),
        flops=2 * width * 2 * lanes * 3 * depth, moved=12 * 2**20,
    )
    acc, upper, lower, *last = lax.optimization_barrier((acc, upper, lower, *last))
    send = ((width + TAIL, LANES), F32)

    def late(z):
        return call(
            functools.partial(late_kernel, z), [((width, LANES), F32)] + [send] * 3,
            (acc, right_on, right, from_left_on, from_left, from_right_on, from_right, upper, lower, *last), whole(13),
            scratch=[pltpu.VMEM((width, lanes), F32)],
            flops=2 * width * lanes * (3 * rows + micro * rows), moved=8 * 2**20,
        )

    keep_far, *far_sends = late(1)
    keep_near, *near_sends = late(0)
    got = [shifted(far_sends[b - 1].astype(F16), False, b) for b in (2, 1, 3)]
    rel, *got = lax.optimization_barrier((rel, *got))
    (far,) = call(far_kernel, [send], (keep_far, *[v.astype(F32) for v in got]), whole(4), moved=4 * 2**20)
    far, *near_sends = lax.optimization_barrier((far.astype(F16), *[v.astype(F16) for v in near_sends]))
    other = lax.ppermute(far, "z_hi", [(0, 1), (1, 0)])
    (second,) = call(second_kernel, [((rows, width), F32)], (rel, first, weights[0]), whole(3), **matmul)
    got = [shifted(near_sends[b - 1], False, b).astype(F32) for b in (2, 1, 3)]
    (block,) = call(near_kernel, [((width, LANES), F32)], (keep_near, other.astype(F32), *got), whole(5), moved=4 * 2**20)
    return (second[None], block[None])


def solution(mesh):
    fine = Mesh(mesh.devices.reshape(2, 4, 2, 4, 4), ("section", "z_lo", "z_hi", "y", "x"))
    dp = ("z_hi", "y", "x")
    return jax.shard_map(
        local,
        mesh=fine,
        in_specs=(
            P("section", "z_lo", None),
            P("section", None, dp, "z_lo"),
            P("section", None, dp, None),
            P(dp, None),
            P(),
        ),
        out_specs=(P("section", dp, "z_lo"), P("section", "z_lo", dp)),
        check_vma=False,
    )
```

```python
import functools

import jax
import jax.numpy as jnp
from jax import lax
from jax.experimental import pallas as pl
from jax.experimental.pallas import tpu as pltpu
from jax.sharding import Mesh
from jax.sharding import PartitionSpec as P

F32 = jnp.float32
F16 = jnp.float16
BF16 = jnp.bfloat16
RING = 4
LANES = 128
TAIL = 16
TOP = 15
TINY = 1e-30
ENTRY_LIMIT = 26
ENTRY_FLOPS = 10**10


def section():
    return lax.axis_index("section")


def on_last():
    return section() == lax.axis_size("section") - 1


def block_start(z_off, along, across):
    first = section() == 0
    y_off, x_off = jnp.where(first, across, along), jnp.where(first, along, across)
    z = lax.rem(lax.axis_index("z_hi") + z_off, 2)
    y = lax.rem(lax.axis_index("y") + y_off, RING)
    x = lax.rem(lax.axis_index("x") + x_off, RING)
    return pl.multiple_of((z * (RING * RING) + y * RING + x) * LANES, LANES)


def pairs_over(along, by):
    size, pairs = RING * RING, []
    for s in range(2):
        for y in range(RING):
            for x in range(RING):
                on_x = (s == 0) == along
                there = (y, (x + by) % RING) if on_x else ((y + by) % RING, x)
                pairs.append((s * size + y * RING + x, s * size + there[0] * RING + there[1]))
    return pairs


def shifted(value, along, by):
    return lax.ppermute(value, ("section", "y", "x"), pairs_over(along, by))


def whole(n=1):
    return [pl.BlockSpec(memory_space=pltpu.VMEM)] * n


def in_hbm(value):
    return pltpu.with_memory_space_constraint(value, pltpu.HBM)


def call(kernel, out_shapes, operands, specs, scratch=(), flops=0, moved=0, limit=20):
    return pl.pallas_call(
        kernel,
        out_shape=[jax.ShapeDtypeStruct(s, t) for s, t in out_shapes],
        in_specs=specs,
        out_specs=whole(len(out_shapes)),
        scratch_shapes=list(scratch),
        compiler_params=pltpu.CompilerParams(vmem_limit_bytes=limit * 2**20),
        cost_estimate=pl.CostEstimate(flops=flops, bytes_accessed=moved, transcendentals=0),
    )(*operands)


CONTRACT_LAST = (((1,), (1,)), ((), ()))


def entry_kernel(pending_ref, x_ref, stash_ref, right_on, left_on, right_ref, left_ref, right_near, left_near, own_ref,
                 x_in, stash_in, count_in, sems):
    micro, rows, width = x_ref.shape
    half, depth = width // 2, (micro - 1) * rows
    pieces = [(pending_ref, count_in), (x_ref, x_in)]
    pieces += [(stash_ref.at[m], stash_in.at[m]) for m in range(micro - 1)]
    copies = [pltpu.make_async_copy(a, b, sems.at[i]) for i, (a, b) in enumerate(pieces)]
    for copy in copies:
        copy.start()
    copies[0].wait()
    copies[1].wait()
    count = count_in[section()]
    for m in range(micro):
        turned = jnp.where(m >= micro - count, x_in[m].astype(F32), 0.0).T.astype(BF16)
        lanes = slice(m * rows, (m + 1) * rows)
        for out, top in ((right_on, 0), (right_ref, half), (left_on, half), (left_ref, 0)):
            out[:half, lanes] = turned[top:top + half]
    share = depth // 2
    plans = []
    for z in range(2):
        at = half + z * share
        plans += [(right_on, at, z, 2, 0, share), (left_on, at, z, 2, share, depth)]
        beside, at = ((right_near, left_near), 0) if z == 0 else ((right_ref, left_ref), half)
        plans += [(out, at, z, along, 0, depth) for out, along in zip(beside, (1, RING - 1))]
        plans += [(own_ref, z * depth, z, 0, 0, depth)]
    for m in range(micro - 1):
        copies[2 + m].wait()
        for out, base, z, along, begin, end in plans:
            begin_m, end_m = max(begin, m * rows), min(end, (m + 1) * rows)
            if begin_m >= end_m:
                continue
            for b in range(RING):
                source = stash_in[m, begin_m - m * rows:end_m - m * rows, pl.ds(block_start(z, along, b), LANES)]
                out[base + begin_m - begin:base + end_m - begin, b * LANES:(b + 1) * LANES] = source


def first_kernel(grad_ref, weight_ref, out_ref, small_ref):
    step = 256
    for i in range(0, weight_ref.shape[0], step):
        out = lax.dot_general(grad_ref[...], weight_ref[i:i + step, :], CONTRACT_LAST, preferred_element_type=F32)
        out_ref[:, i:i + step] = out
        small_ref[:, i:i + step] = jnp.where(on_last(), out, 0.0).astype(BF16)


def second_kernel(rel_ref, first_ref, weight_ref, out_ref):
    step, share = 256, rel_ref.shape[2]
    tensor = lax.axis_index("z_lo")
    for i in range(0, weight_ref.shape[0], step):
        total = jnp.zeros((rel_ref.shape[1], step), F32)
        for k in range(RING):
            owner = lax.rem(tensor - k + RING, RING)
            cols = weight_ref[i:i + step, pl.ds(pl.multiple_of(owner * share, share), share)]
            total = total + lax.dot_general(rel_ref[k], cols, CONTRACT_LAST, preferred_element_type=F32)
        out_ref[:, i:i + step] = jnp.where(on_last(), first_ref[:, i:i + step], total)


def pack_last_kernel(head_ref, rel_ref, right_in, left_in, right_ref, left_ref, own_ref, two_ref, right_near, left_near):
    tensor = lax.axis_index("z_lo")
    rows, share, depth = rel_ref.shape[1], rel_ref.shape[2], right_in.shape[0]
    right_near[:depth, :] = right_in[...]
    left_near[:depth, :] = left_in[...]
    for z in range(2):
        (right, left), base = ((right_near, left_near), depth) if z == 0 else ((right_ref, left_ref), 0)
        for b in range(RING):
            for out, top, along in ((right, base, 1), (left, base, RING - 1), (own_ref, z * rows, 0), (two_ref, z * rows, 2)):
                at = block_start(z, along, b)
                inner = pl.multiple_of(lax.rem(at, share), LANES)
                chained = rel_ref[lax.rem(tensor - lax.div(at, share) + RING, RING), :, pl.ds(inner, LANES)]
                last = jnp.where(on_last(), head_ref[:, pl.ds(at, LANES)], chained)
                out[top:top + rows, b * LANES:(b + 1) * LANES] = last


def early_kernel(z, mine_on, mine_ref, own_ref, left_on, left_ref, right_on, right_ref, left_cols, right_cols, acc_ref):
    width, depth = acc_ref.shape[0], own_ref.shape[0] // 2
    half = width // 2
    sides = [(mine_on, mine_ref), (left_on, left_ref), (right_ref, right_on)]
    at = half if z else 0
    rhs = [own_ref[z * depth:(z + 1) * depth, :], left_cols[at:at + depth, :], right_cols[at:at + depth, :]]
    rhs = jnp.concatenate(rhs, axis=0)
    for r in range(2):
        lhs = jnp.concatenate([side[r][:half, :depth] for side in sides], axis=1)
        acc_ref[r * half:(r + 1) * half, :] = jnp.dot(lhs, rhs, preferred_element_type=F32)


def late_kernel(z, acc_ref, mine_on, mine_ref, left_on, left_ref, right_on, right_ref, upper_ref, lower_ref,
                two_last, own_last, left_last, right_last, keep_ref, *rest):
    sends, sum_ref = rest[:-1], rest[-1]
    width, rows = acc_ref.shape[0], own_last.shape[0] // 2
    half, lanes = width // 2, acc_ref.shape[1]
    depth = mine_ref.shape[1] - rows
    mine, left, right, far = (mine_on, mine_ref), (left_on, left_ref), (right_ref, right_on), (upper_ref, lower_ref)
    rhs = [own_last[z * rows:(z + 1) * rows, :]]
    rhs += [ref[ref.shape[0] - rows:, :] for ref in (left_last, right_last)]
    rhs += [two_last[z * rows:(z + 1) * rows, :]]
    at = half + z * depth // 2
    rhs += [ref[at:at + depth // 2, :] for ref in far]
    rhs = jnp.concatenate(rhs, axis=0)
    largest = jnp.full((1, lanes), TINY, F32)
    for r in range(2):
        lhs = [side[r][:half, depth:] for side in (mine, left, right, far)] + [far[r][:half, :depth]]
        total = jnp.dot(jnp.concatenate(lhs, axis=1), rhs, preferred_element_type=F32)
        total = total + acc_ref[r * half:(r + 1) * half, :]
        largest = jnp.maximum(largest, jnp.max(jnp.abs(total), axis=0, keepdims=True))
        sum_ref[r * half:(r + 1) * half, :] = total
    power = jnp.ceil(jnp.log2(jnp.max(largest, axis=1, keepdims=True))) - TOP
    power = jnp.broadcast_to(power, (1, LANES))
    factor = jnp.exp2(-power)
    keep_ref[...] = sum_ref[:, :LANES]
    for b, out in enumerate(sends, 1):
        out[:width, :] = sum_ref[:, b * LANES:(b + 1) * LANES] * factor
        out[width:, :] = jnp.broadcast_to(power, (TAIL, LANES))


def summed(keep_ref, refs):
    rows = keep_ref.shape[0]
    total = keep_ref[...]
    for ref in refs:
        total = total + ref[:rows, :] * jnp.exp2(ref[rows:rows + 1, :])
    return total


def far_kernel(keep_ref, one_ref, two_ref, three_ref, out_ref):
    rows = keep_ref.shape[0]
    total = summed(keep_ref, (one_ref, two_ref, three_ref))
    largest = jnp.maximum(jnp.max(jnp.abs(total), axis=0, keepdims=True), TINY)
    power = jnp.ceil(jnp.log2(jnp.max(largest, axis=1, keepdims=True))) - TOP
    power = jnp.broadcast_to(power, (1, LANES))
    out_ref[:rows, :] = total * jnp.exp2(-power)
    out_ref[rows:, :] = jnp.broadcast_to(power, (TAIL, LANES))


def near_kernel(keep_ref, *rest):
    rest[-1][...] = summed(keep_ref, rest[:-1])


def on_line(value, pairs):
    pairs = [(s * RING + i, t * RING + j % RING) for (s, i), (t, j) in pairs]
    return lax.ppermute(value, ("section", "z_lo"), pairs)


def local(weights, stash_in, stash_grad, head_grad, pending):
    inputs, grads = stash_in[0], stash_grad[0]
    micro, rows, width = inputs.shape
    depth, half, lanes = (micro - 1) * rows, width // 2, RING * LANES
    columns = head_grad.shape[1]
    matmul = dict(flops=2 * rows * width * columns, moved=2 * 2**20)

    going, cols = ((half + depth, lanes), BF16), ((depth, lanes), BF16)
    right_on, left_on, right, left, near_right, near_left, own = call(
        entry_kernel, [going] * 4 + [cols] * 2 + [((2 * depth, lanes), BF16)],
        [in_hbm(v) for v in (pending, inputs, grads)], [pl.BlockSpec(memory_space=pltpu.HBM)] * 3,
        scratch=[pltpu.VMEM(inputs.shape, BF16), pltpu.VMEM(grads.shape, BF16), pltpu.SMEM(pending.shape, pending.dtype),
                 pltpu.SemaphoreType.DMA((micro + 6,))],
        flops=ENTRY_FLOPS, moved=12 * 2**20, limit=ENTRY_LIMIT,
    )
    from_left_on, from_right_on = shifted(right_on, True, 1), shifted(left_on, True, -1)

    first, small = call(first_kernel, [((rows, width), F32), ((rows, width), BF16)], (head_grad, weights[0]), whole(2), **matmul)
    shard = lax.ppermute(small, "section", [(1, 0)])
    staying_right, staying_left, shard = lax.optimization_barrier((right, left, shard))
    from_left, from_right = shifted(staying_right, True, 1), shifted(staying_left, True, -1)
    places = range(RING)
    both = small + shard
    passed = on_line(both, [((0, i), (0, i - 1)) for i in places] + [((1, i), (1, i + 1)) for i in places])
    passed, from_left_on, from_right_on = lax.optimization_barrier((passed, from_left_on, from_right_on))
    upper = shifted(from_left_on, True, 1)
    behind_two = on_line(passed, [((1, i), (0, i + 1)) for i in places])
    passed, behind_two = lax.optimization_barrier((passed, behind_two))
    behind = on_line(passed, [((1, i), (0, i)) for i in places])
    lower = shifted(from_right_on, True, -1)
    rel = [shard, behind, behind_two, passed]
    rel = jnp.stack(rel, 0)

    edge, both_halves, behind_cols = [((n, lanes), BF16) for n in (rows, 2 * rows, micro * rows)]
    last_right, last_left, last_own, last_two, near_right, near_left = call(
        pack_last_kernel, [edge] * 2 + [both_halves] * 2 + [behind_cols] * 2, (head_grad, rel, near_right, near_left), whole(4),
        moved=6 * 2**20,
    )
    last = [shifted(last_two, True, 2), shifted(last_right, True, 1), shifted(last_left, True, -1)]
    held = (right_on, right, own, from_left_on, from_left, from_right_on, from_right)

    def early(z, *columns):
        return call(
            functools.partial(early_kernel, z), [((width, lanes), F32)], (*held, *columns), whole(9),
            flops=2 * width * lanes * 3 * depth, moved=8 * 2**20,
        )[0]

    acc = early(1, from_left, from_right)
    acc, upper, lower, near_right, near_left, *last = lax.optimization_barrier(
        (acc, upper, lower, near_right, near_left, *last)
    )
    two, last_from_left, last_from_right = last
    near_from_left, near_from_right = shifted(near_right, True, 1), shifted(near_left, True, -1)
    send = ((width + TAIL, LANES), F32)

    def late(z, acc, *columns):
        return call(
            functools.partial(late_kernel, z), [((width, LANES), F32)] + [send] * 3,
            (acc, right_on, right, *held[3:], upper, lower, two, last_own, *columns), whole(13),
            scratch=[pltpu.VMEM((width, lanes), F32)],
            flops=2 * width * lanes * (3 * rows + micro * rows), moved=8 * 2**20,
        )

    keep_far, *far_sends = late(1, acc, last_from_left, last_from_right)
    keep_near, *near_sends = late(0, early(0, near_from_left, near_from_right), near_from_left, near_from_right)
    got = [shifted(far_sends[b - 1].astype(F16), False, b) for b in (2, 1, 3)]
    rel, *got = lax.optimization_barrier((rel, *got))
    (far,) = call(far_kernel, [send], (keep_far, *[v.astype(F32) for v in got]), whole(4), moved=4 * 2**20)
    far = far.astype(F16)
    _, *near_sends = lax.optimization_barrier((far, *[v.astype(F16) for v in near_sends]))
    other = lax.ppermute(far, "z_hi", [(0, 1), (1, 0)])
    (second,) = call(second_kernel, [((rows, width), F32)], (rel, first, weights[0]), whole(3), **matmul)
    got = [shifted(near_sends[b - 1], False, b).astype(F32) for b in (2, 1, 3)]
    (block,) = call(near_kernel, [((width, LANES), F32)], (keep_near, other.astype(F32), *got), whole(5), moved=4 * 2**20)
    return (second[None], block[None])


def solution(mesh):
    fine = Mesh(mesh.devices.reshape(2, 4, 2, 4, 4), ("section", "z_lo", "z_hi", "y", "x"))
    dp = ("z_hi", "y", "x")
    return jax.shard_map(
        local,
        mesh=fine,
        in_specs=(
            P("section", "z_lo", None),
            P("section", None, dp, "z_lo"),
            P("section", None, dp, None),
            P(dp, None),
            P(),
        ),
        out_specs=(P("section", dp, "z_lo"), P("section", "z_lo", dp)),
        check_vma=False,
    )
```

```python
import functools

import jax
import jax.numpy as jnp
from jax import lax
from jax.experimental import pallas as pl
from jax.experimental.pallas import tpu as pltpu
from jax.sharding import Mesh
from jax.sharding import PartitionSpec as P

F32 = jnp.float32
F16 = jnp.float16
BF16 = jnp.bfloat16
RING = 4
LANES = 128
TAIL = 16
TOP = 15
TINY = 1e-30
ENTRY_LIMIT = 26
ENTRY_FLOPS = 10**10


def section():
    return lax.axis_index("section")


def on_last():
    return section() == lax.axis_size("section") - 1


def block_start(z_off, along, across):
    first = section() == 0
    y_off, x_off = jnp.where(first, across, along), jnp.where(first, along, across)
    z = lax.rem(lax.axis_index("z_hi") + z_off, 2)
    y = lax.rem(lax.axis_index("y") + y_off, RING)
    x = lax.rem(lax.axis_index("x") + x_off, RING)
    return pl.multiple_of((z * (RING * RING) + y * RING + x) * LANES, LANES)


def pairs_over(along, by):
    size, pairs = RING * RING, []
    for s in range(2):
        for y in range(RING):
            for x in range(RING):
                on_x = (s == 0) == along
                there = (y, (x + by) % RING) if on_x else ((y + by) % RING, x)
                pairs.append((s * size + y * RING + x, s * size + there[0] * RING + there[1]))
    return pairs


def shifted(value, along, by):
    return lax.ppermute(value, ("section", "y", "x"), pairs_over(along, by))


def whole(n=1):
    return [pl.BlockSpec(memory_space=pltpu.VMEM)] * n


def in_hbm(value):
    return pltpu.with_memory_space_constraint(value, pltpu.HBM)


def call(kernel, out_shapes, operands, specs, scratch=(), flops=0, moved=0, limit=20):
    return pl.pallas_call(
        kernel,
        out_shape=[jax.ShapeDtypeStruct(s, t) for s, t in out_shapes],
        in_specs=specs,
        out_specs=whole(len(out_shapes)),
        scratch_shapes=list(scratch),
        compiler_params=pltpu.CompilerParams(vmem_limit_bytes=limit * 2**20),
        cost_estimate=pl.CostEstimate(flops=flops, bytes_accessed=moved, transcendentals=0),
    )(*operands)


CONTRACT_LAST = (((1,), (1,)), ((), ()))


def entry_kernel(pending_ref, x_ref, stash_ref, right_on, left_on, right_ref, left_ref, own_ref, x_in, stash_in, count_in, sems):
    micro, rows, width = x_ref.shape
    half, depth = width // 2, (micro - 1) * rows
    pieces = [(pending_ref, count_in), (x_ref, x_in)]
    pieces += [(stash_ref.at[m], stash_in.at[m]) for m in range(micro - 1)]
    copies = [pltpu.make_async_copy(a, b, sems.at[i]) for i, (a, b) in enumerate(pieces)]
    for copy in copies:
        copy.start()
    copies[0].wait()
    copies[1].wait()
    count = count_in[section()]
    for m in range(micro):
        turned = jnp.where(m >= micro - count, x_in[m].astype(F32), 0.0).T.astype(BF16)
        lanes = slice(m * rows, (m + 1) * rows)
        for out, top in ((right_on, 0), (right_ref, half), (left_on, half), (left_ref, 0)):
            out[:half, lanes] = turned[top:top + half]
    share = depth // 2
    plans = []
    for z in range(2):
        at = half + z * share
        plans += [(right_on, at, z, 2, 0, share), (left_on, at, z, 2, share, depth)]
        at = half + z * depth
        plans += [(right_ref, at, z, 1, 0, depth), (left_ref, at, z, RING - 1, 0, depth), (own_ref, z * depth, z, 0, 0, depth)]
    for m in range(micro - 1):
        copies[2 + m].wait()
        for out, base, z, along, begin, end in plans:
            begin_m, end_m = max(begin, m * rows), min(end, (m + 1) * rows)
            if begin_m >= end_m:
                continue
            for b in range(RING):
                source = stash_in[m, begin_m - m * rows:end_m - m * rows, pl.ds(block_start(z, along, b), LANES)]
                out[base + begin_m - begin:base + end_m - begin, b * LANES:(b + 1) * LANES] = source


def first_kernel(grad_ref, weight_ref, out_ref, small_ref):
    step = 256
    for i in range(0, weight_ref.shape[0], step):
        out = lax.dot_general(grad_ref[...], weight_ref[i:i + step, :], CONTRACT_LAST, preferred_element_type=F32)
        out_ref[:, i:i + step] = out
        small_ref[:, i:i + step] = jnp.where(on_last(), out, 0.0).astype(BF16)


def second_kernel(rel_ref, first_ref, weight_ref, out_ref):
    step, share = 256, rel_ref.shape[2]
    tensor = lax.axis_index("z_lo")
    for i in range(0, weight_ref.shape[0], step):
        total = jnp.zeros((rel_ref.shape[1], step), F32)
        for k in range(RING):
            owner = lax.rem(tensor - k + RING, RING)
            cols = weight_ref[i:i + step, pl.ds(pl.multiple_of(owner * share, share), share)]
            total = total + lax.dot_general(rel_ref[k], cols, CONTRACT_LAST, preferred_element_type=F32)
        out_ref[:, i:i + step] = jnp.where(on_last(), first_ref[:, i:i + step], total)


def pack_last_kernel(head_ref, rel_ref, right_ref, left_ref, own_ref, two_ref):
    tensor = lax.axis_index("z_lo")
    rows, share = rel_ref.shape[1], rel_ref.shape[2]
    for z in range(2):
        for b in range(RING):
            for out, along in ((right_ref, 1), (left_ref, RING - 1), (own_ref, 0), (two_ref, 2)):
                at = block_start(z, along, b)
                inner = pl.multiple_of(lax.rem(at, share), LANES)
                chained = rel_ref[lax.rem(tensor - lax.div(at, share) + RING, RING), :, pl.ds(inner, LANES)]
                last = jnp.where(on_last(), head_ref[:, pl.ds(at, LANES)], chained)
                out[z * rows:(z + 1) * rows, b * LANES:(b + 1) * LANES] = last


def early_kernel(mine_on, mine_ref, own_ref, left_on, left_ref, right_on, right_ref, acc_ref):
    width, depth = acc_ref.shape[0], own_ref.shape[0] // 2
    half, lanes = width // 2, acc_ref.shape[1] // 2
    sides = [(mine_on, mine_ref), (left_on, left_ref), (right_ref, right_on)]
    for r in range(2):
        lhs = jnp.concatenate([side[r][:half, :depth] for side in sides], axis=1)
        for z in range(2):
            at = half + z * depth
            rhs = [own_ref[z * depth:(z + 1) * depth, :], left_ref[at:at + depth, :], right_ref[at:at + depth, :]]
            rhs = jnp.concatenate(rhs, axis=0)
            acc_ref[r * half:(r + 1) * half, z * lanes:(z + 1) * lanes] = jnp.dot(lhs, rhs, preferred_element_type=F32)


def late_kernel(z, blocks, acc_ref, mine_on, mine_ref, left_on, left_ref, right_on, right_ref, upper_ref, lower_ref,
                two_last, left_last, right_last, own_last, *rest):
    outs, sum_ref = rest[:-1], rest[-1]
    width, rows = acc_ref.shape[0], own_last.shape[0] // 2
    half, lanes = width // 2, acc_ref.shape[1] // 2
    depth = mine_ref.shape[1] - rows
    mine, left, right, far = (mine_on, mine_ref), (left_on, left_ref), (right_ref, right_on), (upper_ref, lower_ref)
    rhs = [ref[z * rows:(z + 1) * rows, :] for ref in (own_last, left_last, right_last, two_last)]
    at = half + z * depth // 2
    rhs += [ref[at:at + depth // 2, :] for ref in far]
    rhs = jnp.concatenate(rhs, axis=0)
    rhs = jnp.concatenate([rhs[:, b * LANES:(b + 1) * LANES] for b in blocks], axis=1)
    largest = jnp.full((1, len(blocks) * LANES), TINY, F32)
    for r in range(2):
        lhs = [side[r][:half, depth:] for side in (mine, left, right, far)] + [far[r][:half, :depth]]
        total = jnp.dot(jnp.concatenate(lhs, axis=1), rhs, preferred_element_type=F32)
        earlier = [acc_ref[r * half:(r + 1) * half, z * lanes + b * LANES:z * lanes + (b + 1) * LANES] for b in blocks]
        total = total + jnp.concatenate(earlier, axis=1)
        largest = jnp.maximum(largest, jnp.max(jnp.abs(total), axis=0, keepdims=True))
        sum_ref[r * half:(r + 1) * half, :] = total
    power = jnp.ceil(jnp.log2(jnp.max(largest, axis=1, keepdims=True))) - TOP
    power = jnp.broadcast_to(power, (1, LANES))
    factor = jnp.exp2(-power)
    for i, (b, out) in enumerate(zip(blocks, outs)):
        tile = sum_ref[:, i * LANES:(i + 1) * LANES]
        if b:
            out[:width, :] = tile * factor
            out[width:, :] = jnp.broadcast_to(power, (TAIL, LANES))
        else:
            out[...] = tile


def summed(keep_ref, refs):
    rows = keep_ref.shape[0]
    total = keep_ref[...]
    for ref in refs:
        total = total + ref[:rows, :] * jnp.exp2(ref[rows:rows + 1, :])
    return total


def far_kernel(keep_ref, one_ref, two_ref, three_ref, out_ref):
    rows = keep_ref.shape[0]
    total = summed(keep_ref, (one_ref, two_ref, three_ref))
    largest = jnp.maximum(jnp.max(jnp.abs(total), axis=0, keepdims=True), TINY)
    power = jnp.ceil(jnp.log2(jnp.max(largest, axis=1, keepdims=True))) - TOP
    power = jnp.broadcast_to(power, (1, LANES))
    out_ref[:rows, :] = total * jnp.exp2(-power)
    out_ref[rows:, :] = jnp.broadcast_to(power, (TAIL, LANES))


def near_kernel(keep_ref, *rest):
    rest[-1][...] = summed(keep_ref, rest[:-1])


def on_line(value, pairs):
    pairs = [(s * RING + i, t * RING + j % RING) for (s, i), (t, j) in pairs]
    return lax.ppermute(value, ("section", "z_lo"), pairs)


def local(weights, stash_in, stash_grad, head_grad, pending):
    inputs, grads = stash_in[0], stash_grad[0]
    micro, rows, width = inputs.shape
    depth, half, lanes = (micro - 1) * rows, width // 2, RING * LANES
    columns = head_grad.shape[1]
    matmul = dict(flops=2 * rows * width * columns, moved=2 * 2**20)

    going, staying = ((half + depth, lanes), BF16), ((half + 2 * depth, lanes), BF16)
    right_on, left_on, right, left, own = call(
        entry_kernel, [going, going, staying, staying, ((2 * depth, lanes), BF16)],
        [in_hbm(v) for v in (pending, inputs, grads)], [pl.BlockSpec(memory_space=pltpu.HBM)] * 3,
        scratch=[pltpu.VMEM(inputs.shape, BF16), pltpu.VMEM(grads.shape, BF16), pltpu.SMEM(pending.shape, pending.dtype),
                 pltpu.SemaphoreType.DMA((micro + 6,))],
        flops=ENTRY_FLOPS, moved=12 * 2**20, limit=ENTRY_LIMIT,
    )
    from_left_on, from_right_on = shifted(right_on, True, 1), shifted(left_on, True, -1)

    first, small = call(first_kernel, [((rows, width), F32), ((rows, width), BF16)], (head_grad, weights[0]), whole(2), **matmul)
    shard = lax.ppermute(small, "section", [(1, 0)])
    staying_right, staying_left, shard = lax.optimization_barrier((right, left, shard))
    from_left, from_right = shifted(staying_right, True, 1), shifted(staying_left, True, -1)
    places = range(RING)
    both = small + shard
    passed = on_line(both, [((0, i), (0, i - 1)) for i in places] + [((1, i), (1, i + 1)) for i in places])
    passed, from_left_on, from_right_on = lax.optimization_barrier((passed, from_left_on, from_right_on))
    upper = shifted(from_left_on, True, 1)
    behind_two = on_line(passed, [((1, i), (0, i + 1)) for i in places])
    passed, behind_two = lax.optimization_barrier((passed, behind_two))
    behind = on_line(passed, [((1, i), (0, i)) for i in places])
    lower = shifted(from_right_on, True, -1)
    rel = [shard, behind, behind_two, passed]
    rel = jnp.stack(rel, 0)

    edge = ((2 * rows, lanes), BF16)
    last_right, last_left, last_own, last_two = call(
        pack_last_kernel, [edge] * 4, (head_grad, rel), whole(2), moved=4 * 2**20
    )
    last = [shifted(last_two, True, 2), shifted(last_right, True, 1), shifted(last_left, True, -1), last_own]
    (acc,) = call(
        early_kernel, [((width, 2 * lanes), F32)], (right_on, right, own, from_left_on, from_left, from_right_on, from_right), whole(7),
        flops=2 * width * 2 * lanes * 3 * depth, moved=12 * 2**20,
    )
    acc, upper, lower, *last = lax.optimization_barrier((acc, upper, lower, *last))
    send = ((width + TAIL, LANES), F32)

    def late(z, blocks):
        return call(
            functools.partial(late_kernel, z, blocks), [send if b else ((width, LANES), F32) for b in blocks],
            (acc, right_on, right, from_left_on, from_left, from_right_on, from_right, upper, lower, *last), whole(13),
            scratch=[pltpu.VMEM((width, len(blocks) * LANES), F32)],
            flops=2 * width * len(blocks) * LANES * (3 * rows + micro * rows), moved=8 * 2**20,
        )

    far_two, far_one = late(1, (2, 1))
    far_three, keep_far = late(1, (3, 0))
    keep_near, *near_sends = late(0, (0, 1, 2, 3))
    sends = [far_one, far_two, far_three] + near_sends
    got = [shifted(sends[i].astype(F16), False, 1 + i % 3) for i in (1, 0, 2, 4, 3, 5)]
    rel, *got[:3] = lax.optimization_barrier((rel, *got[:3]))
    got = [v.astype(F32) for v in got]
    (second,) = call(second_kernel, [((rows, width), F32)], (rel, first, weights[0]), whole(3), **matmul)
    (far,) = call(far_kernel, [send], (keep_far, *got[:3]), whole(4), moved=4 * 2**20)
    other = lax.ppermute(far.astype(F16), "z_hi", [(0, 1), (1, 0)]).astype(F32)
    (near,) = call(near_kernel, [((width, LANES), F32)], (keep_near, *got[3:]), whole(4), moved=4 * 2**20)
    (block,) = call(near_kernel, [((width, LANES), F32)], (near, other), whole(2), moved=2 * 2**20)
    return (second[None], block[None])


def solution(mesh):
    fine = Mesh(mesh.devices.reshape(2, 4, 2, 4, 4), ("section", "z_lo", "z_hi", "y", "x"))
    dp = ("z_hi", "y", "x")
    return jax.shard_map(
        local,
        mesh=fine,
        in_specs=(
            P("section", "z_lo", None),
            P("section", None, dp, "z_lo"),
            P("section", None, dp, None),
            P(dp, None),
            P(),
        ),
        out_specs=(P("section", dp, "z_lo"), P("section", "z_lo", dp)),
        check_vma=False,
    )
```

```python
import functools

import jax
import jax.numpy as jnp
from jax import lax
from jax.experimental import pallas as pl
from jax.experimental.pallas import tpu as pltpu
from jax.sharding import Mesh
from jax.sharding import PartitionSpec as P

F32 = jnp.float32
F16 = jnp.float16
BF16 = jnp.bfloat16
RING = 4
LANES = 128
TAIL = 16
TOP = 15
TINY = 1e-30
ENTRY_LIMIT = 26
ENTRY_FLOPS = 10**10


def section():
    return lax.axis_index("section")


def on_last():
    return section() == lax.axis_size("section") - 1


def block_start(z_off, along, across):
    first = section() == 0
    y_off, x_off = jnp.where(first, across, along), jnp.where(first, along, across)
    z = lax.rem(lax.axis_index("z_hi") + z_off, 2)
    y = lax.rem(lax.axis_index("y") + y_off, RING)
    x = lax.rem(lax.axis_index("x") + x_off, RING)
    return pl.multiple_of((z * (RING * RING) + y * RING + x) * LANES, LANES)


def pairs_over(along, by):
    size, pairs = RING * RING, []
    for s in range(2):
        for y in range(RING):
            for x in range(RING):
                on_x = (s == 0) == along
                there = (y, (x + by) % RING) if on_x else ((y + by) % RING, x)
                pairs.append((s * size + y * RING + x, s * size + there[0] * RING + there[1]))
    return pairs


def shifted(value, along, by):
    return lax.ppermute(value, ("section", "y", "x"), pairs_over(along, by))


def whole(n=1):
    return [pl.BlockSpec(memory_space=pltpu.VMEM)] * n


def in_hbm(value):
    return pltpu.with_memory_space_constraint(value, pltpu.HBM)


def call(kernel, out_shapes, operands, specs, scratch=(), flops=0, moved=0, limit=20):
    return pl.pallas_call(
        kernel,
        out_shape=[jax.ShapeDtypeStruct(s, t) for s, t in out_shapes],
        in_specs=specs,
        out_specs=whole(len(out_shapes)),
        scratch_shapes=list(scratch),
        compiler_params=pltpu.CompilerParams(vmem_limit_bytes=limit * 2**20),
        cost_estimate=pl.CostEstimate(flops=flops, bytes_accessed=moved, transcendentals=0),
    )(*operands)


CONTRACT_LAST = (((1,), (1,)), ((), ()))


def entry_kernel(pending_ref, x_ref, stash_ref, right_on, left_on, right_ref, left_ref, own_ref, x_in, stash_in, count_in, sems):
    micro, rows, width = x_ref.shape
    half, depth = width // 2, (micro - 1) * rows
    pieces = [(pending_ref, count_in), (x_ref, x_in)]
    pieces += [(stash_ref.at[m], stash_in.at[m]) for m in range(micro - 1)]
    copies = [pltpu.make_async_copy(a, b, sems.at[i]) for i, (a, b) in enumerate(pieces)]
    for copy in copies:
        copy.start()
    copies[0].wait()
    copies[1].wait()
    count = count_in[section()]
    for m in range(micro):
        turned = jnp.where(m >= micro - count, x_in[m].astype(F32), 0.0).T.astype(BF16)
        lanes = slice(m * rows, (m + 1) * rows)
        for out, top in ((right_on, 0), (right_ref, half), (left_on, half), (left_ref, 0)):
            out[:half, lanes] = turned[top:top + half]
    share = depth // 2
    plans = []
    for z in range(2):
        at = half + z * share
        plans += [(right_on, at, z, 2, 0, share), (left_on, at, z, 2, share, depth)]
        at = half + z * depth
        plans += [(right_ref, at, z, 1, 0, depth), (left_ref, at, z, RING - 1, 0, depth), (own_ref, z * depth, z, 0, 0, depth)]
    for m in range(micro - 1):
        copies[2 + m].wait()
        for out, base, z, along, begin, end in plans:
            begin_m, end_m = max(begin, m * rows), min(end, (m + 1) * rows)
            if begin_m >= end_m:
                continue
            for b in range(RING):
                source = stash_in[m, begin_m - m * rows:end_m - m * rows, pl.ds(block_start(z, along, b), LANES)]
                out[base + begin_m - begin:base + end_m - begin, b * LANES:(b + 1) * LANES] = source


def first_kernel(grad_ref, weight_ref, out_ref, small_ref):
    step = 256
    for i in range(0, weight_ref.shape[0], step):
        out = lax.dot_general(grad_ref[...], weight_ref[i:i + step, :], CONTRACT_LAST, preferred_element_type=F32)
        out_ref[:, i:i + step] = out
        small_ref[:, i:i + step] = jnp.where(on_last(), out, 0.0).astype(BF16)


def second_kernel(rel_ref, first_ref, weight_ref, out_ref):
    step, share = 256, rel_ref.shape[2]
    tensor = lax.axis_index("z_lo")
    for i in range(0, weight_ref.shape[0], step):
        total = jnp.zeros((rel_ref.shape[1], step), F32)
        for k in range(RING):
            owner = lax.rem(tensor - k + RING, RING)
            cols = weight_ref[i:i + step, pl.ds(pl.multiple_of(owner * share, share), share)]
            total = total + lax.dot_general(rel_ref[k], cols, CONTRACT_LAST, preferred_element_type=F32)
        out_ref[:, i:i + step] = jnp.where(on_last(), first_ref[:, i:i + step], total)


def pack_last_kernel(head_ref, rel_ref, right_ref, left_ref, own_ref, two_ref):
    tensor = lax.axis_index("z_lo")
    rows, share = rel_ref.shape[1], rel_ref.shape[2]
    for z in range(2):
        for b in range(RING):
            for out, along in ((right_ref, 1), (left_ref, RING - 1), (own_ref, 0), (two_ref, 2)):
                at = block_start(z, along, b)
                inner = pl.multiple_of(lax.rem(at, share), LANES)
                chained = rel_ref[lax.rem(tensor - lax.div(at, share) + RING, RING), :, pl.ds(inner, LANES)]
                last = jnp.where(on_last(), head_ref[:, pl.ds(at, LANES)], chained)
                out[z * rows:(z + 1) * rows, b * LANES:(b + 1) * LANES] = last


def early_kernel(mine_on, mine_ref, own_ref, left_on, left_ref, right_on, right_ref, acc_ref):
    width, depth = acc_ref.shape[0], own_ref.shape[0] // 2
    half, lanes = width // 2, acc_ref.shape[1] // 2
    sides = [(mine_on, mine_ref), (left_on, left_ref), (right_ref, right_on)]
    for r in range(2):
        lhs = jnp.concatenate([side[r][:half, :depth] for side in sides], axis=1)
        for z in range(2):
            at = half + z * depth
            rhs = [own_ref[z * depth:(z + 1) * depth, :], left_ref[at:at + depth, :], right_ref[at:at + depth, :]]
            rhs = jnp.concatenate(rhs, axis=0)
            acc_ref[r * half:(r + 1) * half, z * lanes:(z + 1) * lanes] = jnp.dot(lhs, rhs, preferred_element_type=F32)


def late_kernel(z, acc_ref, mine_on, mine_ref, left_on, left_ref, right_on, right_ref, upper_ref, lower_ref,
                two_last, left_last, right_last, own_last, keep_ref, *rest):
    sends, sum_ref = rest[:-1], rest[-1]
    width, rows = acc_ref.shape[0], own_last.shape[0] // 2
    half, lanes = width // 2, acc_ref.shape[1] // 2
    depth = mine_ref.shape[1] - rows
    mine, left, right, far = (mine_on, mine_ref), (left_on, left_ref), (right_ref, right_on), (upper_ref, lower_ref)
    rhs = [ref[z * rows:(z + 1) * rows, :] for ref in (own_last, left_last, right_last, two_last)]
    at = half + z * depth // 2
    rhs += [ref[at:at + depth // 2, :] for ref in far]
    rhs = jnp.concatenate(rhs, axis=0)
    largest = jnp.full((1, lanes), TINY, F32)
    for r in range(2):
        lhs = [side[r][:half, depth:] for side in (mine, left, right, far)] + [far[r][:half, :depth]]
        total = jnp.dot(jnp.concatenate(lhs, axis=1), rhs, preferred_element_type=F32)
        total = total + acc_ref[r * half:(r + 1) * half, z * lanes:(z + 1) * lanes]
        largest = jnp.maximum(largest, jnp.max(jnp.abs(total), axis=0, keepdims=True))
        sum_ref[r * half:(r + 1) * half, :] = total
    power = jnp.ceil(jnp.log2(jnp.max(largest, axis=1, keepdims=True))) - TOP
    power = jnp.broadcast_to(power, (1, LANES))
    factor = jnp.exp2(-power)
    keep_ref[...] = sum_ref[:, :LANES]
    for b, out in enumerate(sends, 1):
        out[:width, :] = sum_ref[:, b * LANES:(b + 1) * LANES] * factor
        out[width:, :] = jnp.broadcast_to(power, (TAIL, LANES))


def summed(keep_ref, refs):
    rows = keep_ref.shape[0]
    total = keep_ref[...]
    for ref in refs:
        total = total + ref[:rows, :] * jnp.exp2(ref[rows:rows + 1, :])
    return total


def far_kernel(keep_ref, one_ref, two_ref, three_ref, out_ref):
    rows = keep_ref.shape[0]
    total = summed(keep_ref, (one_ref, two_ref, three_ref))
    largest = jnp.maximum(jnp.max(jnp.abs(total), axis=0, keepdims=True), TINY)
    power = jnp.ceil(jnp.log2(jnp.max(largest, axis=1, keepdims=True))) - TOP
    power = jnp.broadcast_to(power, (1, LANES))
    out_ref[:rows, :] = total * jnp.exp2(-power)
    out_ref[rows:, :] = jnp.broadcast_to(power, (TAIL, LANES))


def near_kernel(keep_ref, one_ref, two_ref, three_ref, other_ref, out_ref):
    out_ref[...] = summed(keep_ref, (one_ref, two_ref, three_ref, other_ref))


def on_line(value, pairs):
    pairs = [(s * RING + i, t * RING + j % RING) for (s, i), (t, j) in pairs]
    return lax.ppermute(value, ("section", "z_lo"), pairs)


def local(weights, stash_in, stash_grad, head_grad, pending):
    inputs, grads = stash_in[0], stash_grad[0]
    micro, rows, width = inputs.shape
    depth, half, lanes = (micro - 1) * rows, width // 2, RING * LANES
    columns = head_grad.shape[1]
    matmul = dict(flops=2 * rows * width * columns, moved=2 * 2**20)

    going, staying = ((half + depth, lanes), BF16), ((half + 2 * depth, lanes), BF16)
    right_on, left_on, right, left, own = call(
        entry_kernel, [going, going, staying, staying, ((2 * depth, lanes), BF16)],
        [in_hbm(v) for v in (pending, inputs, grads)], [pl.BlockSpec(memory_space=pltpu.HBM)] * 3,
        scratch=[pltpu.VMEM(inputs.shape, BF16), pltpu.VMEM(grads.shape, BF16), pltpu.SMEM(pending.shape, pending.dtype),
                 pltpu.SemaphoreType.DMA((micro + 6,))],
        flops=ENTRY_FLOPS, moved=12 * 2**20, limit=ENTRY_LIMIT,
    )
    from_left_on, from_right_on = shifted(right_on, True, 1), shifted(left_on, True, -1)

    first, small = call(first_kernel, [((rows, width), F32), ((rows, width), BF16)], (head_grad, weights[0]), whole(2), **matmul)
    shard = lax.ppermute(small, "section", [(1, 0)])
    from_left, from_right = shifted(right, True, 1), shifted(left, True, -1)
    places = range(RING)
    both = small + shard
    passed = on_line(both, [((0, i), (0, i - 1)) for i in places] + [((1, i), (1, i + 1)) for i in places])
    passed, from_left_on, from_right_on = lax.optimization_barrier((passed, from_left_on, from_right_on))
    upper = shifted(from_left_on, True, 1)
    behind_two = on_line(passed, [((1, i), (0, i + 1)) for i in places])
    passed, behind_two = lax.optimization_barrier((passed, behind_two))
    behind = on_line(passed, [((1, i), (0, i)) for i in places])
    lower = shifted(from_right_on, True, -1)
    rel = [shard, behind, behind_two, passed]
    rel = jnp.stack(rel, 0)

    edge = ((2 * rows, lanes), BF16)
    last_right, last_left, last_own, last_two = call(
        pack_last_kernel, [edge] * 4, (head_grad, rel), whole(2), moved=4 * 2**20
    )
    last = [shifted(last_two, True, 2), shifted(last_right, True, 1), shifted(last_left, True, -1), last_own]
    (acc,) = call(
        early_kernel, [((width, 2 * lanes), F32)], (right_on, right, own, from_left_on, from_left, from_right_on, from_right), whole(7),
        flops=2 * width * 2 * lanes * 3 * depth, moved=12 * 2**20,
    )
    acc, upper, lower, *last = lax.optimization_barrier((acc, upper, lower, *last))
    send = ((width + TAIL, LANES), F32)

    def late(z):
        return call(
            functools.partial(late_kernel, z), [((width, LANES), F32)] + [send] * 3,
            (acc, right_on, right, from_left_on, from_left, from_right_on, from_right, upper, lower, *last), whole(13),
            scratch=[pltpu.VMEM((width, lanes), F32)],
            flops=2 * width * lanes * (3 * rows + micro * rows), moved=8 * 2**20,
        )

    keep_far, *far_sends = late(1)
    keep_near, *near_sends = late(0)
    sends = far_sends + near_sends
    got = [shifted(sends[i].astype(F16), False, 1 + i % 3) for i in (1, 0, 2, 4, 3, 5)]
    rel, *got[:3] = lax.optimization_barrier((rel, *got[:3]))
    got = [v.astype(F32) for v in got]
    (second,) = call(second_kernel, [((rows, width), F32)], (rel, first, weights[0]), whole(3), **matmul)
    (far,) = call(far_kernel, [send], (keep_far, *got[:3]), whole(4), moved=4 * 2**20)
    other = lax.ppermute(far.astype(F16), "z_hi", [(0, 1), (1, 0)]).astype(F32)
    (block,) = call(near_kernel, [((width, LANES), F32)], (keep_near, *got[3:], other), whole(5), moved=4 * 2**20)
    return (second[None], block[None])


def solution(mesh):
    fine = Mesh(mesh.devices.reshape(2, 4, 2, 4, 4), ("section", "z_lo", "z_hi", "y", "x"))
    dp = ("z_hi", "y", "x")
    return jax.shard_map(
        local,
        mesh=fine,
        in_specs=(
            P("section", "z_lo", None),
            P("section", None, dp, "z_lo"),
            P("section", None, dp, None),
            P(dp, None),
            P(),
        ),
        out_specs=(P("section", dp, "z_lo"), P("section", "z_lo", dp)),
        check_vma=False,
    )
```

```python
import functools

import jax
import jax.numpy as jnp
from jax import lax
from jax.experimental import pallas as pl
from jax.experimental.pallas import tpu as pltpu
from jax.sharding import Mesh
from jax.sharding import PartitionSpec as P

F32 = jnp.float32
F16 = jnp.float16
BF16 = jnp.bfloat16
RING = 4
LANES = 128
TAIL = 16
TOP = 15
TINY = 1e-30
ENTRY_LIMIT = 26
ENTRY_FLOPS = 10**10


def section():
    return lax.axis_index("section")


def on_last():
    return section() == lax.axis_size("section") - 1


def block_start(z_off, along, across):
    first = section() == 0
    y_off, x_off = jnp.where(first, across, along), jnp.where(first, along, across)
    z = lax.rem(lax.axis_index("z_hi") + z_off, 2)
    y = lax.rem(lax.axis_index("y") + y_off, RING)
    x = lax.rem(lax.axis_index("x") + x_off, RING)
    return pl.multiple_of((z * (RING * RING) + y * RING + x) * LANES, LANES)


def pairs_over(along, by):
    size, pairs = RING * RING, []
    for s in range(2):
        for y in range(RING):
            for x in range(RING):
                on_x = (s == 0) == along
                there = (y, (x + by) % RING) if on_x else ((y + by) % RING, x)
                pairs.append((s * size + y * RING + x, s * size + there[0] * RING + there[1]))
    return pairs


def shifted(value, along, by):
    return lax.ppermute(value, ("section", "y", "x"), pairs_over(along, by))


def whole(n=1):
    return [pl.BlockSpec(memory_space=pltpu.VMEM)] * n


def in_hbm(value):
    return pltpu.with_memory_space_constraint(value, pltpu.HBM)


def call(kernel, out_shapes, operands, specs, scratch=(), flops=0, moved=0, limit=20):
    return pl.pallas_call(
        kernel,
        out_shape=[jax.ShapeDtypeStruct(s, t) for s, t in out_shapes],
        in_specs=specs,
        out_specs=whole(len(out_shapes)),
        scratch_shapes=list(scratch),
        compiler_params=pltpu.CompilerParams(vmem_limit_bytes=limit * 2**20),
        cost_estimate=pl.CostEstimate(flops=flops, bytes_accessed=moved, transcendentals=0),
    )(*operands)


CONTRACT_LAST = (((1,), (1,)), ((), ()))


def entry_kernel(pending_ref, x_ref, stash_ref, right_on, left_on, right_ref, left_ref, own_ref, x_in, stash_in, count_in, sems):
    micro, rows, width = x_ref.shape
    half, depth = width // 2, (micro - 1) * rows
    pieces = [(pending_ref, count_in), (x_ref, x_in)]
    pieces += [(stash_ref.at[m], stash_in.at[m]) for m in range(micro - 1)]
    copies = [pltpu.make_async_copy(a, b, sems.at[i]) for i, (a, b) in enumerate(pieces)]
    for copy in copies:
        copy.start()
    copies[0].wait()
    copies[1].wait()
    count = count_in[section()]
    for m in range(micro):
        turned = jnp.where(m >= micro - count, x_in[m].astype(F32), 0.0).T.astype(BF16)
        lanes = slice(m * rows, (m + 1) * rows)
        for out, top in ((right_on, 0), (right_ref, half), (left_on, half), (left_ref, 0)):
            out[:half, lanes] = turned[top:top + half]
    share = depth // 2
    plans = []
    for z in range(2):
        at = half + z * share
        plans += [(right_on, at, z, 2, 0, share), (left_on, at, z, 2, share, depth)]
        at = half + z * depth
        plans += [(right_ref, at, z, 1, 0, depth), (left_ref, at, z, RING - 1, 0, depth), (own_ref, z * depth, z, 0, 0, depth)]
    for m in range(micro - 1):
        copies[2 + m].wait()
        for out, base, z, along, begin, end in plans:
            begin_m, end_m = max(begin, m * rows), min(end, (m + 1) * rows)
            if begin_m >= end_m:
                continue
            for b in range(RING):
                source = stash_in[m, begin_m - m * rows:end_m - m * rows, pl.ds(block_start(z, along, b), LANES)]
                out[base + begin_m - begin:base + end_m - begin, b * LANES:(b + 1) * LANES] = source


def first_kernel(grad_ref, weight_ref, out_ref, small_ref):
    step = 256
    for i in range(0, weight_ref.shape[0], step):
        out = lax.dot_general(grad_ref[...], weight_ref[i:i + step, :], CONTRACT_LAST, preferred_element_type=F32)
        out_ref[:, i:i + step] = out
        small_ref[:, i:i + step] = jnp.where(on_last(), out, 0.0).astype(BF16)


def second_kernel(rel_ref, first_ref, weight_ref, out_ref):
    step, share = 256, rel_ref.shape[2]
    tensor = lax.axis_index("z_lo")
    for i in range(0, weight_ref.shape[0], step):
        total = jnp.zeros((rel_ref.shape[1], step), F32)
        for k in range(RING):
            owner = lax.rem(tensor - k + RING, RING)
            cols = weight_ref[i:i + step, pl.ds(pl.multiple_of(owner * share, share), share)]
            total = total + lax.dot_general(rel_ref[k], cols, CONTRACT_LAST, preferred_element_type=F32)
        out_ref[:, i:i + step] = jnp.where(on_last(), first_ref[:, i:i + step], total)


def pack_last_kernel(head_ref, rel_ref, right_ref, left_ref, own_ref, two_ref):
    tensor = lax.axis_index("z_lo")
    rows, share = rel_ref.shape[1], rel_ref.shape[2]
    for z in range(2):
        for b in range(RING):
            for out, along in ((right_ref, 1), (left_ref, RING - 1), (own_ref, 0), (two_ref, 2)):
                at = block_start(z, along, b)
                inner = pl.multiple_of(lax.rem(at, share), LANES)
                chained = rel_ref[lax.rem(tensor - lax.div(at, share) + RING, RING), :, pl.ds(inner, LANES)]
                last = jnp.where(on_last(), head_ref[:, pl.ds(at, LANES)], chained)
                out[z * rows:(z + 1) * rows, b * LANES:(b + 1) * LANES] = last


def early_kernel(mine_on, mine_ref, own_ref, left_on, left_ref, right_on, right_ref, acc_ref):
    width, depth = acc_ref.shape[0], own_ref.shape[0] // 2
    half, lanes = width // 2, acc_ref.shape[1] // 2
    sides = [(mine_on, mine_ref), (left_on, left_ref), (right_ref, right_on)]
    for r in range(2):
        lhs = jnp.concatenate([side[r][:half, :depth] for side in sides], axis=1)
        for z in range(2):
            at = half + z * depth
            rhs = [own_ref[z * depth:(z + 1) * depth, :], left_ref[at:at + depth, :], right_ref[at:at + depth, :]]
            rhs = jnp.concatenate(rhs, axis=0)
            acc_ref[r * half:(r + 1) * half, z * lanes:(z + 1) * lanes] = jnp.dot(lhs, rhs, preferred_element_type=F32)


def late_kernel(z, acc_ref, mine_on, mine_ref, left_on, left_ref, right_on, right_ref, upper_ref, lower_ref,
                two_last, left_last, right_last, own_last, keep_ref, *rest):
    sends, sum_ref = rest[:-1], rest[-1]
    width, rows = acc_ref.shape[0], own_last.shape[0] // 2
    half, lanes = width // 2, acc_ref.shape[1] // 2
    depth = mine_ref.shape[1] - rows
    mine, left, right, far = (mine_on, mine_ref), (left_on, left_ref), (right_ref, right_on), (upper_ref, lower_ref)
    rhs = [ref[z * rows:(z + 1) * rows, :] for ref in (own_last, left_last, right_last, two_last)]
    at = half + z * depth // 2
    rhs += [ref[at:at + depth // 2, :] for ref in far]
    rhs = jnp.concatenate(rhs, axis=0)
    largest = jnp.full((1, lanes), TINY, F32)
    for r in range(2):
        lhs = [side[r][:half, depth:] for side in (mine, left, right, far)] + [far[r][:half, :depth]]
        total = jnp.dot(jnp.concatenate(lhs, axis=1), rhs, preferred_element_type=F32)
        total = total + acc_ref[r * half:(r + 1) * half, z * lanes:(z + 1) * lanes]
        largest = jnp.maximum(largest, jnp.max(jnp.abs(total), axis=0, keepdims=True))
        sum_ref[r * half:(r + 1) * half, :] = total
    power = jnp.ceil(jnp.log2(jnp.max(largest, axis=1, keepdims=True))) - TOP
    power = jnp.broadcast_to(power, (1, LANES))
    factor = jnp.exp2(-power)
    keep_ref[...] = sum_ref[:, :LANES]
    for b, out in enumerate(sends, 1):
        out[:width, :] = sum_ref[:, b * LANES:(b + 1) * LANES] * factor
        out[width:, :] = jnp.broadcast_to(power, (TAIL, LANES))


def summed(keep_ref, refs):
    rows = keep_ref.shape[0]
    total = keep_ref[...]
    for ref in refs:
        total = total + ref[:rows, :] * jnp.exp2(ref[rows:rows + 1, :])
    return total


def far_kernel(keep_ref, one_ref, two_ref, three_ref, out_ref):
    rows = keep_ref.shape[0]
    total = summed(keep_ref, (one_ref, two_ref, three_ref))
    largest = jnp.maximum(jnp.max(jnp.abs(total), axis=0, keepdims=True), TINY)
    power = jnp.ceil(jnp.log2(jnp.max(largest, axis=1, keepdims=True))) - TOP
    power = jnp.broadcast_to(power, (1, LANES))
    out_ref[:rows, :] = total * jnp.exp2(-power)
    out_ref[rows:, :] = jnp.broadcast_to(power, (TAIL, LANES))


def near_kernel(keep_ref, one_ref, two_ref, three_ref, other_ref, out_ref):
    out_ref[...] = summed(keep_ref, (one_ref, two_ref, three_ref, other_ref))


def on_line(value, pairs):
    pairs = [(s * RING + i, t * RING + j % RING) for (s, i), (t, j) in pairs]
    return lax.ppermute(value, ("section", "z_lo"), pairs)


def local(weights, stash_in, stash_grad, head_grad, pending):
    inputs, grads = stash_in[0], stash_grad[0]
    micro, rows, width = inputs.shape
    depth, half, lanes = (micro - 1) * rows, width // 2, RING * LANES
    columns = head_grad.shape[1]
    matmul = dict(flops=2 * rows * width * columns, moved=2 * 2**20)

    going, staying = ((half + depth, lanes), BF16), ((half + 2 * depth, lanes), BF16)
    right_on, left_on, right, left, own = call(
        entry_kernel, [going, going, staying, staying, ((2 * depth, lanes), BF16)],
        [in_hbm(v) for v in (pending, inputs, grads)], [pl.BlockSpec(memory_space=pltpu.HBM)] * 3,
        scratch=[pltpu.VMEM(inputs.shape, BF16), pltpu.VMEM(grads.shape, BF16), pltpu.SMEM(pending.shape, pending.dtype),
                 pltpu.SemaphoreType.DMA((micro + 6,))],
        flops=ENTRY_FLOPS, moved=12 * 2**20, limit=ENTRY_LIMIT,
    )
    from_left_on, from_right_on = shifted(right_on, True, 1), shifted(left_on, True, -1)

    first, small = call(first_kernel, [((rows, width), F32), ((rows, width), BF16)], (head_grad, weights[0]), whole(2), **matmul)
    shard = lax.ppermute(small, "section", [(1, 0)])
    from_left, from_right = shifted(right, True, 1), shifted(left, True, -1)
    places = range(RING)
    both = small + shard
    passed = on_line(both, [((0, i), (0, i - 1)) for i in places] + [((1, i), (1, i + 1)) for i in places])
    passed, from_left_on, from_right_on = lax.optimization_barrier((passed, from_left_on, from_right_on))
    upper = shifted(from_left_on, True, 1)
    behind_two = on_line(passed, [((1, i), (0, i + 1)) for i in places])
    passed, behind_two = lax.optimization_barrier((passed, behind_two))
    behind = on_line(passed, [((1, i), (0, i)) for i in places])
    lower = shifted(from_right_on, True, -1)
    rel = [shard, behind, behind_two, passed]
    rel = jnp.stack(rel, 0)

    edge = ((2 * rows, lanes), BF16)
    last_right, last_left, last_own, last_two = call(
        pack_last_kernel, [edge] * 4, (head_grad, rel), whole(2), moved=4 * 2**20
    )
    last = [shifted(last_two, True, 2), shifted(last_right, True, 1), shifted(last_left, True, -1), last_own]
    (acc,) = call(
        early_kernel, [((width, 2 * lanes), F32)], (right_on, right, own, from_left_on, from_left, from_right_on, from_right), whole(7),
        flops=2 * width * 2 * lanes * 3 * depth, moved=12 * 2**20,
    )
    acc, upper, lower, *last = lax.optimization_barrier((acc, upper, lower, *last))
    send = ((width + TAIL, LANES), F32)

    def late(z):
        return call(
            functools.partial(late_kernel, z), [((width, LANES), F32)] + [send] * 3,
            (acc, right_on, right, from_left_on, from_left, from_right_on, from_right, upper, lower, *last), whole(13),
            scratch=[pltpu.VMEM((width, lanes), F32)],
            flops=2 * width * lanes * (3 * rows + micro * rows), moved=8 * 2**20,
        )

    keep_far, *far_sends = late(1)
    keep_near, *near_sends = late(0)
    sends = far_sends + near_sends
    got = [shifted(sends[i].astype(F16), False, 1 + i % 3) for i in (0, 2, 1, 3, 5, 4)]
    rel, *got[:3] = lax.optimization_barrier((rel, *got[:3]))
    got = [v.astype(F32) for v in got]
    (second,) = call(second_kernel, [((rows, width), F32)], (rel, first, weights[0]), whole(3), **matmul)
    (far,) = call(far_kernel, [send], (keep_far, *got[:3]), whole(4), moved=4 * 2**20)
    other = lax.ppermute(far.astype(F16), "z_hi", [(0, 1), (1, 0)]).astype(F32)
    (block,) = call(near_kernel, [((width, LANES), F32)], (keep_near, *got[3:], other), whole(5), moved=4 * 2**20)
    return (second[None], block[None])


def solution(mesh):
    fine = Mesh(mesh.devices.reshape(2, 4, 2, 4, 4), ("section", "z_lo", "z_hi", "y", "x"))
    dp = ("z_hi", "y", "x")
    return jax.shard_map(
        local,
        mesh=fine,
        in_specs=(
            P("section", "z_lo", None),
            P("section", None, dp, "z_lo"),
            P("section", None, dp, None),
            P(dp, None),
            P(),
        ),
        out_specs=(P("section", dp, "z_lo"), P("section", "z_lo", dp)),
        check_vma=False,
    )
```
